256 devices in a mesh: gx: 4 (over x), gy: 4 (over z_lo), gz: 16 (over z_hi, y, core).
Axes of the slice: x: 4, y: 4, z: 8 (z_hi: 2, z_lo: 4; z = z_hi * 4 + z_lo), core: 2. Of those that a mesh axis runs over, the one named last changes fastest.
Arguments:
- fields: float32 [4, 64, 64, 2048], P(None, 'gx', 'gy', 'gz'), may hold values from -6 to 6
- tone_freq: float32 [48], replicated, may hold values from 0.02 to 2.5
- mode_freq: float32 [2000], replicated, may hold values from 0.05 to 2.5
- mode_amp: float32 [2000], replicated, may hold values from -3 to 3
- mode_map: int32 [2000], replicated, may hold values from 0 to 47
- src_pos: int32 [3, 4096], replicated, may hold values from 16 to 1535, as said below
- src_id: int32 [4096], replicated, may hold values from 0 to 47
- src_gain: float32 [4096], replicated, may hold values from -6 to 6
- sample_cell: int32 [4, 4, 16, 16, 128], P('gx', 'gy', 'gz'), may hold values from 0 to 32767
- sample_count: int32 [4, 4, 16, 16], P('gx', 'gy', None, 'gz'), may hold values from 0 to 128, as said below
- history: float32 [124, 4, 4, 16, 16, 128], P(None, 'gx', 'gy', 'gz'), may hold values from -6 to 6
Outputs:
- fields_out: float32 [4, 64, 64, 2048], P(None, 'gx', 'gy', 'gz')
- coefficients: float32 [96, 4, 4, 16, 16, 128], P(None, 'gx', 'gy', 'gz')
The draws below stay inside these ranges and needn't reach their ends.
Inputs may be any that keep to these rules, and one draw needn't show every extreme that they name: `src_pos`: row 0 is below 64, row 1 below 64, row 2 below 2048; the cells lie on the surface of a box inside the grid. `sample_count`: in every draw some owner receives 128 live slots from every tile of its column. `sample_cell`: slots at or past the count also hold cells of the tile.
All inputs are finite; a program needn't handle non-finite values.
Results may differ from the reference program's by a relative error of at most 0.00017.
Values sent between devices are 32-bit elements; how exact they have to be, the bound alone decides.
A program may use at most 128 MiB of HBM per device.

```python
import math
import jax
import jax.numpy as jnp
from jax import lax

CX = 16
CY = 16
CZ = 128
STEPS = 4
HIST = 124
TONES = 48
MODES = 2000
SOURCES = 48
SRC_CELLS = 4096
CAP = 128
NX = 64
NY = 64
NZ = 2048
N_GX = 4
N_GY = 4
N_GZ = 16


def draw_src_pos(key, part):
    key = jax.random.fold_in(key, 11)
    face_key, coord_key = jax.random.split(key)
    face_pick = jax.random.randint(face_key, (SRC_CELLS,), 0, 6)
    lower_corner = jnp.array([NX // 4, NY // 4, NZ // 4], jnp.int32)
    upper_corner = jnp.array([3 * NX // 4 - 1, 3 * NY // 4 - 1, 3 * NZ // 4 - 1], jnp.int32)
    random_bits = jax.random.randint(coord_key, (3, SRC_CELLS), 0, 2 ** 30)
    interior = lower_corner[:, None] + random_bits % (upper_corner - lower_corner + 1)[:, None]
    coordinate = jnp.arange(3)[:, None]
    planar = jnp.where(face_pick[None, :] % 2 == 1, upper_corner[:, None], lower_corner[:, None])
    return jnp.where(coordinate == (face_pick // 2)[None, :], planar, interior).astype(jnp.int32)


def draw_sample_count(key, part):
    key = jax.random.fold_in(key, 23)
    count_key, owner_key = jax.random.split(key)
    counts = jax.random.randint(count_key, (N_GX, N_GY, N_GZ, N_GZ), 0, CAP + 1)
    chosen = jax.random.randint(owner_key, (), 0, N_GZ)
    full_owner = jnp.arange(N_GZ)[None, None, None, :] == chosen
    return jnp.where(full_owner, CAP, counts).astype(jnp.int32)


def touch_ends(values, key, smallest, top_value):
    place = [jax.random.randint(jax.random.fold_in(key, axis), (), 0, length) for axis, length in enumerate(values.shape)]
    widest = values.shape.index(max(values.shape))
    beside = place[:widest] + [(place[widest] + 1) % values.shape[widest]] + place[widest + 1:]
    return values.at[tuple(place)].set(smallest).at[tuple(beside)].set(top_value)


def steps_of(own_key, shape, cuts, low, high):
    def one(axis_at, parts):
        heights = jax.random.uniform(jax.random.fold_in(jax.random.fold_in(own_key, 6), axis_at), (parts,), jnp.float32, low / len(cuts), high / len(cuts))
        return jnp.repeat(jnp.exp(heights), shape[axis_at] // parts).reshape((-1,) + (1,) * (len(shape) - axis_at - 1))

    gain = one(*cuts[0])
    for cut in cuts[1:]:
        gain = gain * one(*cut)
    return gain


def centred(key, dims, deviation, bound, cuts=(), dtype=jnp.bfloat16):
    values = deviation * jax.random.normal(key, dims, jnp.float32)
    if cuts:
        values = values * steps_of(key, dims, cuts, -0.22, 0.18)
    return jnp.clip(values, -bound, bound).astype(dtype)


def setup_inputs(seed: int = 0) -> dict:
    key_of = jax.random.split(jax.random.key(seed), 12)
    return {
        "fields": centred(key_of[0], (4, NX, NY, NZ), 1.0, 6.0, ((1, 4), (2, 4), (3, 16)), jnp.float32),
        "tone_freq": jnp.clip(jnp.exp(jax.random.uniform(key_of[1], (TONES,), jnp.float32, math.log(0.02), math.log(2.5))), 0.02, 2.5),
        "mode_freq": jnp.clip(jnp.exp(jax.random.uniform(key_of[2], (MODES,), jnp.float32, math.log(0.05), math.log(2.5))), 0.05, 2.5),
        "mode_amp": centred(key_of[3], (MODES,), 0.2, 3.0, (), jnp.float32),
        "mode_map": touch_ends(jax.random.randint(key_of[4], (MODES,), 0, SOURCES), jax.random.fold_in(key_of[4], 1), 0, SOURCES - 1).astype(jnp.int32),
        "src_pos": draw_src_pos(jax.random.fold_in(key_of[11], 71), 0),
        "src_id": touch_ends(jax.random.randint(key_of[6], (SRC_CELLS,), 0, SOURCES), jax.random.fold_in(key_of[6], 1), 0, SOURCES - 1).astype(jnp.int32),
        "src_gain": centred(key_of[7], (SRC_CELLS,), 1.0, 6.0, (), jnp.float32),
        "sample_cell": touch_ends(jax.random.randint(key_of[8], (N_GX, N_GY, N_GZ, N_GZ, CAP), 0, CX * CY * CZ), jax.random.fold_in(key_of[8], 1), 0, (CX * CY * CZ) - 1).astype(jnp.int32),
        "sample_count": draw_sample_count(jax.random.fold_in(key_of[11], 71), 0),
        "history": centred(key_of[10], (HIST, N_GX, N_GY, N_GZ, N_GZ, CAP), 1.0, 6.0, ((1, 4), (2, 4), (3, 16)), jnp.float32),
    }


COURANT = 0.5

def ahead_difference(values, direction):
    size_along = values.shape[direction]
    following = jnp.concatenate([lax.slice_in_dim(values, 1, size_along, axis=direction), jnp.zeros_like(lax.slice_in_dim(values, 0, 1, axis=direction))], axis=direction)
    return following - values

def behind_difference(values, direction):
    size_along = values.shape[direction]
    previous = jnp.concatenate([jnp.zeros_like(lax.slice_in_dim(values, 0, 1, axis=direction)), lax.slice_in_dim(values, 0, size_along - 1, axis=direction)], axis=direction)
    return values - previous

def source_drive(mode_freq, mode_amp, mode_map):
    moments = (HIST + jnp.arange(STEPS)).astype(jnp.float32)
    selector = (mode_map[None, :] == jnp.arange(SOURCES)[:, None]).astype(jnp.float32)
    waves = mode_amp[:, None] * jnp.sin(mode_freq[:, None] * moments[None, :])
    return jnp.dot(selector, waves, precision=lax.Precision.HIGHEST)

def sine_basis(tone_freq):
    moments = jnp.arange(HIST + STEPS).astype(jnp.float32)
    angles = moments[:, None] * tone_freq[None, :]
    return jnp.concatenate([jnp.cos(angles), jnp.sin(angles)], axis=1)

def reference(fields, tone_freq, mode_freq, mode_amp, mode_map, src_pos, src_id, src_gain, sample_cell, sample_count, history):
    source_wave = source_drive(mode_freq, mode_amp, mode_map)
    pressure, along_x, along_y, along_z = (fields[0], fields[1], fields[2], fields[3])
    tile_x = jnp.arange(N_GX).reshape(N_GX, 1, 1, 1, 1)
    tile_y = jnp.arange(N_GY).reshape(1, N_GY, 1, 1, 1)
    tile_z = jnp.arange(N_GZ).reshape(1, 1, N_GZ, 1, 1)
    cell_x = tile_x * CX + sample_cell // (CY * CZ)
    cell_y = tile_y * CY + sample_cell // CZ % CY
    cell_z = tile_z * CZ + sample_cell % CZ
    heard_list = []
    for moment in range(STEPS):
        along_x = along_x - COURANT * ahead_difference(pressure, 0)
        along_y = along_y - COURANT * ahead_difference(pressure, 1)
        along_z = along_z - COURANT * ahead_difference(pressure, 2)
        pressure = pressure - COURANT * (behind_difference(along_x, 0) + behind_difference(along_y, 1) + behind_difference(along_z, 2))
        pressure = pressure.at[src_pos[0], src_pos[1], src_pos[2]].add(src_gain * source_wave[src_id, moment])
        heard_list.append(pressure[cell_x, cell_y, cell_z])
    recorded = jnp.transpose(jnp.stack(heard_list), (0, 1, 2, 4, 3, 5))
    timeline = jnp.concatenate([history, recorded], axis=0)
    basis = sine_basis(tone_freq)
    coefficients = jnp.einsum('tj,tabcde->jabcde', basis, timeline, precision=lax.Precision.HIGHEST) * math.sqrt(2.0 / (HIST + STEPS))
    occupied = (jnp.arange(CAP).reshape(1, 1, 1, 1, CAP) < jnp.transpose(sample_count, (0, 1, 3, 2))[..., None]).astype(jnp.float32)
    coefficients = coefficients * occupied[None]
    return (jnp.stack([pressure, along_x, along_y, along_z]), coefficients)
```

```python
import jax
import jax.numpy as jnp
from jax import lax
from jax.experimental import pallas as pl
from jax.experimental.pallas import tpu as pltpu
from jax.sharding import PartitionSpec as P

STEPS = 4
HIST = 124
SOURCES = 48
TONES = 48
MODES = 2000
SRC = 4096
TX, TY, TZ = 16, 16, 128
ROWS = TX * TY
OWN = 16
CAP = 128
SLOTS = OWN * CAP
NB = 2 * TONES
KC = 1024
F32 = jnp.float32
BF = jnp.bfloat16
MESH = pl.DeviceIdType.MESH


def split(values):
    high = values.astype(BF)
    return high, (values - high.astype(F32)).astype(BF)


def dot_nn(a, b):
    return lax.dot_general(a, b, (((1,), (0,)), ((), ())), preferred_element_type=F32)


def dot_nt(a, b):
    return lax.dot_general(a, b, (((1,), (1,)), ((), ())), preferred_element_type=F32)


def half_wave(x, half):
    k = jnp.floor(x * 0.3183098861837907 + (0.5 - half))
    h = k + half
    r = x - h * 3.140625
    r = r - h * 0.0009670257568359375
    r = r - h * 6.2771141529083251953e-07
    q = r * r
    s = -2.505210838544172e-08
    for c in (2.7557319223985893e-06, -1.984126984126984e-04, 8.333333333333333e-03, -0.16666666666666666):
        s = s * q + c
    s = r + r * q * s
    sign = 1.0 - 2.0 * (k - 2.0 * jnp.floor(k * 0.5))
    return jnp.where(half > 0.25, -sign, sign) * s


def iota(shape, dim):
    return lax.broadcasted_iota(jnp.int32, shape, dim)


def kernel(
    fields_h, tone_r, mfreq_r, mamp_r, mmap_r, spos_r, sid_r, sgain_r, cell_r, count_r, hist_h,
    fout_h, cout_h,
    fv, hv, pst, uv, psum, ms, wv, srow, scol, acc, cone, rsel, ov, bt, sb, rb,
    ys, zs, gxm, gxp, gym, gyp, gzm, gzp, gvx, gvy, svy,
    fsem, hsem, osem, ss, rs, vss, vrs, ass, ars,
):
    ix = lax.axis_index("gx")
    iy = lax.axis_index("gy")
    iz = lax.axis_index("gz")
    low_x, high_x = ix == 0, ix == 3
    low_y, high_y = iy == 0, iy == 3
    low_z, high_z = iz == 0, iz == OWN - 1

    loads = [pltpu.make_async_copy(fields_h.at[k], fv.at[k], fsem.at[k]) for k in range(4)]
    for k in (0, 3, 1, 2):
        loads[k].start()
    hist_load = pltpu.make_async_copy(hist_h, hv.at[pl.ds(0, HIST * OWN)], hsem)
    hist_load.start()

    barrier = pltpu.get_barrier_semaphore()
    for k in range(1, OWN):
        pl.semaphore_signal(barrier, inc=1, device_id={"gz": lax.rem(iz + k, OWN)}, device_id_type=MESH)

    sides = (
        (jnp.logical_not(low_x), {"gx": ix - 1}),
        (jnp.logical_not(high_x), {"gx": ix + 1}),
        (jnp.logical_not(low_y), {"gy": iy - 1}),
        (jnp.logical_not(high_y), {"gy": iy + 1}),
        (jnp.logical_not(low_z), {"gz": iz - 1}),
        (jnp.logical_not(high_z), {"gz": iz + 1}),
    )
    for has, target in sides[:4]:
        @pl.when(has)
        def _(target=target):
            pl.semaphore_signal(barrier, inc=1, device_id=target, device_id_type=MESH)

    row8 = iota((8, 1), 0)
    ms[...] = jnp.zeros_like(ms)
    ms[0:1, 0:MODES] = mfreq_r[...]
    ms[1:2, 0:MODES] = mamp_r[...]
    ms[2:3, 0:MODES] = mmap_r[...].astype(F32)
    moment = (HIST + row8 % STEPS).astype(F32)
    waves = ms[1:2, :] * half_wave(ms[0:1, :] * moment, jnp.zeros((8, 1), F32))
    high = waves.astype(BF).astype(F32)
    waves = jnp.where(row8 < STEPS, high, waves - high).astype(BF)
    pick = jnp.where(iota((SOURCES, 1), 0).astype(F32) == ms[2:3, :], 1.0, 0.0).astype(BF)
    drive = dot_nt(waves, pick)
    drive = drive + pltpu.roll(drive, 4, 0)
    high = drive.astype(BF).astype(F32)
    drive = jnp.where(row8 < STEPS, high, drive - high).astype(BF)
    pick = jnp.where(iota((SOURCES, 1), 0) == sid_r[...], 1.0, 0.0).astype(BF)
    weight = dot_nn(drive, pick)
    weight = (weight + pltpu.roll(weight, 4, 0)) * sgain_r[...]
    high = weight.astype(BF).astype(F32)
    wv[...] = jnp.where(row8 < STEPS, high, weight - high)
    lx = spos_r[0:1, :] - ix * TX
    ly = spos_r[1:2, :] - iy * TY
    lz = spos_r[2:3, :] - iz * TZ
    inside = (lx >= 0) & (lx < TX) & (ly >= 0) & (ly < TY) & (lz >= 0) & (lz < TZ)
    srow[...] = jnp.where(inside, lx * TY + ly, -1).astype(F32)
    scol[...] = lz.astype(F32)

    lane = iota((1, TZ), 1)
    even = lane % 2 == 0

    def z_pack(slabs, base, packed):
        for i, piece in slabs:
            turned = pltpu.roll(piece, (base + 2 * i) % TZ, 1) if (base + 2 * i) % TZ else piece
            here = ((lane + 1 - base + TZ) % TZ) // 2 == i
            packed = jnp.where(here, turned, packed)
        return packed

    def pieces(ref, n):
        return [(i, ref[n, i * 8:(i + 1) * 8, :]) for i in range(ROWS // 8)]

    def face_copies(n):
        src = pst.at[n]
        ends = (
            (src.at[pl.ds(0, TY)], gxp.at[n]),
            (src.at[pl.ds(ROWS - TY, TY)], gxm.at[n]),
            (ys.at[n, 0], gyp.at[n]),
            (ys.at[n, 1], gym.at[n]),
            (zs.at[n], gzp.at[n]),
            (zs.at[n], gzm.at[n]),
        )
        return [
            (has, pltpu.make_async_remote_copy(
                src_ref=a, dst_ref=b, send_sem=ss.at[n, i], recv_sem=rs.at[n, i],
                device_id=target, device_id_type=MESH))
            for i, ((has, target), (a, b)) in enumerate(zip(sides, ends))
        ]

    def send_faces(n):
        for has, copy in face_copies(n):
            @pl.when(has)
            def _(copy=copy):
                copy.start()

    def recv_faces(n):
        copies = face_copies(n)
        for i in range(6):
            has = sides[i ^ 1][0]
            copy = copies[i][1]
            @pl.when(has)
            def _(copy=copy):
                copy.wait_recv()

    def y_faces(n):
        ys[n, 0] = pst[n, pl.ds(0, TX, stride=TY), :]
        ys[n, 1] = pst[n, pl.ds(TY - 1, TX, stride=TY), :]

    for k in (0, 3, 1, 2):
        loads[k].wait()
    pst[0] = fv[0]
    y_faces(0)
    svy[...] = fv[2, pl.ds(TY - 1, TX, stride=TY), :]
    packed = z_pack(pieces(fv, 0), 0, jnp.zeros((8, TZ), F32))
    zs[0] = z_pack(pieces(fv, 3), 64, packed)

    expected = (
        OWN - 1
        + jnp.where(low_x, 0, 1) + jnp.where(high_x, 0, 1)
        + jnp.where(low_y, 0, 1) + jnp.where(high_y, 0, 1)
    )
    pl.semaphore_wait(barrier, expected)
    send_faces(0)
    vx_copy = pltpu.make_async_remote_copy(
        src_ref=fv.at[1, pl.ds(ROWS - TY, TY)], dst_ref=gvx, send_sem=vss.at[0], recv_sem=vrs.at[0],
        device_id=sides[1][1], device_id_type=MESH)
    vy_copy = pltpu.make_async_remote_copy(
        src_ref=svy, dst_ref=gvy, send_sem=vss.at[1], recv_sem=vrs.at[1],
        device_id=sides[3][1], device_id_type=MESH)

    @pl.when(sides[1][0])
    def _():
        vx_copy.start()

    @pl.when(sides[3][0])
    def _():
        vy_copy.start()

    acc[...] = jnp.zeros_like(acc)

    @pl.loop(0, SRC // KC)
    def _(chunk):
        span = pl.ds(pl.multiple_of(chunk * KC, KC), KC)
        a = jnp.where(iota((ROWS, 1), 0).astype(F32) == srow[:, span], 1.0, 0.0).astype(BF)
        m = iota((TZ, 1), 0).astype(F32) == scol[:, span]
        b = jnp.concatenate([jnp.where(m, wv[q:q + 1, span], 0.0).astype(BF) for q in range(2 * STEPS)], axis=0)
        acc[...] += dot_nt(a, b)

    eye = iota((TONES, TONES), 0) == iota((TONES, TONES), 1)
    freq = jnp.sum(jnp.where(eye, tone_r[...], 0.0), axis=1, keepdims=True)
    freq = jnp.concatenate([freq, freq], axis=0)
    angle = freq * lane.astype(F32)
    basis = half_wave(angle, jnp.where(iota((NB, 1), 0) < TONES, 0.5, 0.0).astype(F32)) * 0.125
    for n in range(STEPS):
        bt[n * NB:(n + 1) * NB, :] = jnp.broadcast_to(basis[:, HIST + n:HIST + n + 1], (NB, CAP))

    live = jnp.where(lane < count_r[...], 1.0, 0.0).astype(F32)
    hist_load.wait()
    hv[HIST * OWN:, :] = jnp.zeros((STEPS * OWN, CAP), F32)
    bh, bl = split(basis)
    lhs = jnp.concatenate([bh, bl, bh], axis=1)
    for e in range(0, OWN, 2):
        hh, hl = split(jnp.concatenate(
            [hv[pl.ds(e, HIST + STEPS, stride=OWN), :], hv[pl.ds(e + 1, HIST + STEPS, stride=OWN), :]], axis=1))
        part = dot_nn(lhs, jnp.concatenate([hh, hh, hl], axis=0))
        ov[pl.ds(e, NB, stride=OWN), :] = part[:, :CAP] * live[e:e + 1]
        ov[pl.ds(e + 1, NB, stride=OWN), :] = part[:, CAP:] * live[e + 1:e + 2]

    for d in range(OWN):
        cells = cell_r[d:d + 1, :]
        span = slice(d * CAP, (d + 1) * CAP)
        one = jnp.where(iota((TZ, 1), 0) == cells % TZ, 1.0, 0.0).astype(BF)
        cone[0:TZ, span] = one
        cone[TZ:2 * TZ, span] = one
        rsel[:, span] = cells // TZ
    sb[...] = jnp.zeros_like(sb)

    def listen(n):
        lhs = jnp.concatenate(split(pst[n + 1]), axis=1)
        for d in range(0, OWN, 2):
            span = slice(d * CAP, (d + 2) * CAP)
            seen = dot_nn(lhs, cone[:, span])
            got = jnp.sum(jnp.where(iota((ROWS, 1), 0) == rsel[:, span], seen, 0.0), axis=0, keepdims=True)
            sb[d * 8 + n:d * 8 + n + 1, :] = got[:, :CAP]
            sb[(d + 1) * 8 + n:(d + 1) * 8 + n + 1, :] = got[:, CAP:]

    sub = iota((TY, 1), 0)

    def behind(get, x, gx, gy, merged):
        own = get(x)
        xm = get(x - 1) if x else gx
        ym = jnp.where(sub == 0, gy[x:x + 1, :], pltpu.roll(own, 1, 0))
        ring = jnp.concatenate([roll_lanes(merged, -4 * x), roll_lanes(merged, -4 * x - 2)], axis=0)
        zm = pltpu.roll(jnp.where(lane == TZ - 1, ring, own), 1, 1)
        return xm, ym, zm

    def ahead(get, x, gx, gy, merged):
        own = get(x)
        xp = get(x + 1) if x < TX - 1 else gx
        yp = jnp.where(sub == TY - 1, gy[x:x + 1, :], pltpu.roll(own, TY - 1, 0))
        ring = jnp.concatenate([roll_lanes(merged, -4 * x), roll_lanes(merged, -4 * x - 2)], axis=0)
        zp = pltpu.roll(jnp.where(lane == 0, ring, own), TZ - 1, 1)
        return xp, yp, zp

    def roll_lanes(v, by):
        return pltpu.roll(v, by % TZ, 1) if by % TZ else v

    def slab(ref, x):
        return ref[x * TY:(x + 1) * TY, :]

    @pl.when(jnp.logical_not(low_x))
    def _():
        vx_copy.wait_recv()

    @pl.when(jnp.logical_not(low_y))
    def _():
        vy_copy.wait_recv()

    recv_faces(0)
    from_low = jnp.where(low_z, 0.0, gzm[0])
    vzg = roll_lanes(from_low, -64)
    vxg = jnp.where(low_x, 0.0, gvx[...])
    vyg = jnp.where(low_y, 0.0, gvy[...])
    for x in range(TX):
        own = [slab(fv.at[k], x) for k in (1, 2, 3)]
        xm = slab(fv.at[1], x - 1) if x else vxg
        ym = jnp.where(sub == 0, vyg[x:x + 1, :], pltpu.roll(own[1], 1, 0))
        ring = jnp.concatenate([roll_lanes(vzg, -4 * x), roll_lanes(vzg, -4 * x - 2)], axis=0)
        zm = pltpu.roll(jnp.where(lane == TZ - 1, ring, own[2]), 1, 1)
        uv[x * TY:(x + 1) * TY, :] = 0.5 * ((own[0] - xm) + (own[1] - ym) + (own[2] - zm))

    gx_sum = jnp.zeros((TY, TZ), F32)
    gy_sum = jnp.zeros((TX, TZ), F32)
    gz_sum = jnp.zeros((8, TZ), F32)
    for n in range(STEPS):
        if n:
            recv_faces(n)
        get = lambda x, n=n: pst[n, x * TY:(x + 1) * TY, :]
        xg = jnp.where(high_x, 0.0, gxp[n])
        yg = jnp.where(high_y, 0.0, gyp[n])
        zg = jnp.where(high_z, 0.0, gzp[n])
        gx_sum, gy_sum, gz_sum = gx_sum + xg, gy_sum + yg, gz_sum + zg
        xl = jnp.where(low_x, get(0), gxm[n])
        yl = jnp.where(low_y, ys[n, 0], gym[n])
        zl = jnp.where(low_z, roll_lanes(zs[n], -1), gzm[n])
        merged = jnp.where(even, zg, zl)
        for x in range(TX):
            at = slice(x * TY, (x + 1) * TY)
            own = get(x)
            xm, ym, zm = behind(get, x, xl, yl, merged)
            xp, yp, zp = ahead(get, x, xg, yg, merged)
            lap = (xm + xp) + (ym + yp) + (zm + zp) - 6.0 * own
            u = uv[at, :] - 0.25 * lap
            uv[at, :] = u
            new = own - u + (acc[at, n * TZ:(n + 1) * TZ] + acc[at, (STEPS + n) * TZ:(STEPS + n + 1) * TZ])
            pst[n + 1, at, :] = new
            psum[at, :] = own if n == 0 else psum[at, :] + own
        if n < STEPS - 1:
            y_faces(n + 1)
            zs[n + 1] = z_pack(pieces(pst, n + 1), 0, jnp.zeros((8, TZ), F32))
            send_faces(n + 1)
        listen(n)

    def block_copy(k):
        target = lax.rem(iz + k, OWN)
        return pltpu.make_async_remote_copy(
            src_ref=sb.at[pl.ds(pl.multiple_of(target * 8, 8), 8)],
            dst_ref=rb.at[pl.ds(pl.multiple_of(iz * 8, 8), 8)],
            send_sem=ass.at[k], recv_sem=ars.at[k], device_id={"gz": target}, device_id_type=MESH)

    sends = [block_copy(k) for k in range(1, OWN)]
    for copy in sends:
        copy.start()
    mine = pl.ds(pl.multiple_of(iz * 8, 8), 8)
    rb[mine, :] = sb[mine, :]

    for n in range(STEPS):
        for has, copy in face_copies(n):
            @pl.when(has)
            def _(copy=copy):
                copy.wait_send()

    @pl.when(sides[1][0])
    def _():
        vx_copy.wait_send()

    @pl.when(sides[3][0])
    def _():
        vy_copy.wait_send()

    outs = [pltpu.make_async_copy(pst.at[STEPS], fout_h.at[0], osem.at[0])]
    outs[0].start()
    total = lambda x: slab(psum, x)
    for x in range(TX):
        at = slice(x * TY, (x + 1) * TY)
        own = total(x)
        xp, yp, zp = ahead(total, x, gx_sum, gy_sum, gz_sum)
        fv[1, at, :] = fv[1, at, :] - 0.5 * (xp - own)
        fv[2, at, :] = fv[2, at, :] - 0.5 * (yp - own)
        fv[3, at, :] = fv[3, at, :] - 0.5 * (zp - own)
    outs.append(pltpu.make_async_copy(fv.at[pl.ds(1, 3)], fout_h.at[pl.ds(1, 3)], osem.at[1]))
    outs[1].start()

    for copy in sends:
        copy.wait_recv()
    heard = [rb[pl.ds(n, OWN, stride=8), :] * live for n in range(STEPS)]
    parts = 4
    per = NB // parts
    for part in range(parts):
        for j in range(part * per, (part + 1) * per):
            at = slice(j * OWN, (j + 1) * OWN)
            term = ov[at, :]
            for n in range(STEPS):
                term = term + bt[n * NB + j:n * NB + j + 1, :] * heard[n]
            ov[at, :] = term
        rows = pl.ds(part * per * OWN, per * OWN)
        outs.append(pltpu.make_async_copy(ov.at[rows], cout_h.at[rows], osem.at[2 + part]))
        outs[-1].start()
    for copy in sends:
        copy.wait_send()
    for copy in outs:
        copy.wait()


def body(
    fields, tone_freq, mode_freq, mode_amp, mode_map, src_pos, src_id, src_gain, sample_cell, sample_count, history
):
    vmem = pl.BlockSpec(memory_space=pltpu.VMEM)
    hbm = pl.BlockSpec(memory_space=pl.ANY)
    face = (STEPS, TY, TZ)
    fields_out, coefficients = pl.pallas_call(
        kernel,
        out_shape=(
            jax.ShapeDtypeStruct((4, ROWS, TZ), F32),
            jax.ShapeDtypeStruct((NB * OWN, CAP), F32),
        ),
        in_specs=[hbm] + [vmem] * 9 + [hbm],
        out_specs=(hbm, hbm),
        scratch_shapes=[
            pltpu.VMEM((4, ROWS, TZ), F32),
            pltpu.VMEM(((HIST + STEPS) * OWN, CAP), F32),
            pltpu.VMEM((STEPS + 1, ROWS, TZ), F32),
            pltpu.VMEM((ROWS, TZ), F32),
            pltpu.VMEM((ROWS, TZ), F32),
            pltpu.VMEM((8, 2048), F32),
            pltpu.VMEM((8, SRC), F32),
            pltpu.VMEM((1, SRC), F32),
            pltpu.VMEM((1, SRC), F32),
            pltpu.VMEM((ROWS, 2 * STEPS * TZ), F32),
            pltpu.VMEM((2 * TZ, SLOTS), BF),
            pltpu.VMEM((1, SLOTS), jnp.int32),
            pltpu.VMEM((NB * OWN, CAP), F32),
            pltpu.VMEM((STEPS * NB, CAP), F32),
            pltpu.VMEM((OWN * 8, CAP), F32),
            pltpu.VMEM((OWN * 8, CAP), F32),
            pltpu.VMEM((STEPS, 2, TX, TZ), F32),
            pltpu.VMEM((STEPS, 8, TZ), F32),
            pltpu.VMEM(face, F32),
            pltpu.VMEM(face, F32),
            pltpu.VMEM(face, F32),
            pltpu.VMEM(face, F32),
            pltpu.VMEM((STEPS, 8, TZ), F32),
            pltpu.VMEM((STEPS, 8, TZ), F32),
            pltpu.VMEM((TY, TZ), F32),
            pltpu.VMEM((TX, TZ), F32),
            pltpu.VMEM((TX, TZ), F32),
            pltpu.SemaphoreType.DMA((4,)),
            pltpu.SemaphoreType.DMA,
            pltpu.SemaphoreType.DMA((6,)),
            pltpu.SemaphoreType.DMA((STEPS, 6)),
            pltpu.SemaphoreType.DMA((STEPS, 6)),
            pltpu.SemaphoreType.DMA((2,)),
            pltpu.SemaphoreType.DMA((2,)),
            pltpu.SemaphoreType.DMA((OWN,)),
            pltpu.SemaphoreType.DMA((OWN,)),
        ],
        compiler_params=pltpu.CompilerParams(
            collective_id=0, has_side_effects=True, vmem_limit_bytes=40 * 1024 * 1024
        ),
    )(
        fields.reshape(4, ROWS, TZ),
        tone_freq.reshape(1, TONES),
        mode_freq.reshape(1, MODES),
        mode_amp.reshape(1, MODES),
        mode_map.reshape(1, MODES),
        src_pos,
        src_id.reshape(1, SRC),
        src_gain.reshape(1, SRC),
        sample_cell.reshape(OWN, CAP),
        sample_count.reshape(OWN, 1),
        history.reshape(HIST * OWN, CAP),
    )
    return fields_out.reshape(fields.shape), coefficients.reshape(NB, 1, 1, 1, OWN, CAP)


def solution(mesh):
    in_specs = (
        P(None, "gx", "gy", "gz"),
        P(),
        P(),
        P(),
        P(),
        P(),
        P(),
        P(),
        P("gx", "gy", "gz", None, None),
        P("gx", "gy", None, "gz"),
        P(None, "gx", "gy", "gz", None, None),
    )
    out_specs = (P(None, "gx", "gy", "gz"), P(None, "gx", "gy", "gz", None, None))
    return jax.shard_map(body, mesh=mesh, in_specs=in_specs, out_specs=out_specs, check_vma=False)
```

```python
import jax
import jax.numpy as jnp
from jax import lax
from jax.experimental import pallas as pl
from jax.experimental.pallas import tpu as pltpu
from jax.sharding import PartitionSpec as P

STEPS = 4
HIST = 124
SOURCES = 48
TONES = 48
MODES = 2000
SRC = 4096
TX, TY, TZ = 16, 16, 128
ROWS = TX * TY
OWN = 16
CAP = 128
SLOTS = OWN * CAP
NB = 2 * TONES
KC = 1024
F32 = jnp.float32
BF = jnp.bfloat16
MESH = pl.DeviceIdType.MESH


def split(values):
    high = values.astype(BF)
    return high, (values - high.astype(F32)).astype(BF)


def dot_nn(a, b):
    return lax.dot_general(a, b, (((1,), (0,)), ((), ())), preferred_element_type=F32)


def dot_nt(a, b):
    return lax.dot_general(a, b, (((1,), (1,)), ((), ())), preferred_element_type=F32)


def half_wave(x, half):
    k = jnp.floor(x * 0.3183098861837907 + (0.5 - half))
    h = k + half
    r = x - h * 3.140625
    r = r - h * 0.0009670257568359375
    r = r - h * 6.2771141529083251953e-07
    q = r * r
    s = -2.505210838544172e-08
    for c in (2.7557319223985893e-06, -1.984126984126984e-04, 8.333333333333333e-03, -0.16666666666666666):
        s = s * q + c
    s = r + r * q * s
    sign = 1.0 - 2.0 * (k - 2.0 * jnp.floor(k * 0.5))
    return jnp.where(half > 0.25, -sign, sign) * s


def iota(shape, dim):
    return lax.broadcasted_iota(jnp.int32, shape, dim)


def kernel(
    fields_h, tone_r, mfreq_r, mamp_r, mmap_r, spos_r, sid_r, sgain_r, cell_r, count_r, hist_h,
    fout_h, cout_h,
    fv, hv, pst, uv, psum, ms, wv, srow, scol, acc, cone, rsel, ov, bt, sb, rb,
    ys, zs, gxm, gxp, gym, gyp, gzm, gzp, gvx, gvy, svy,
    fsem, hsem, osem, ss, rs, vss, vrs, ass, ars,
):
    ix = lax.axis_index("gx")
    iy = lax.axis_index("gy")
    iz = lax.axis_index("gz")
    low_x, high_x = ix == 0, ix == 3
    low_y, high_y = iy == 0, iy == 3
    low_z, high_z = iz == 0, iz == OWN - 1

    loads = [pltpu.make_async_copy(fields_h.at[k], fv.at[k], fsem.at[k]) for k in range(4)]
    for k in (0, 3, 1, 2):
        loads[k].start()
    hist_load = pltpu.make_async_copy(hist_h, hv.at[pl.ds(0, HIST * OWN)], hsem)
    hist_load.start()

    barrier = pltpu.get_barrier_semaphore()
    for k in range(1, OWN):
        pl.semaphore_signal(barrier, inc=1, device_id={"gz": lax.rem(iz + k, OWN)}, device_id_type=MESH)

    sides = (
        (jnp.logical_not(low_x), {"gx": ix - 1}),
        (jnp.logical_not(high_x), {"gx": ix + 1}),
        (jnp.logical_not(low_y), {"gy": iy - 1}),
        (jnp.logical_not(high_y), {"gy": iy + 1}),
        (jnp.logical_not(low_z), {"gz": iz - 1}),
        (jnp.logical_not(high_z), {"gz": iz + 1}),
    )
    for has, target in sides[:4]:
        @pl.when(has)
        def _(target=target):
            pl.semaphore_signal(barrier, inc=1, device_id=target, device_id_type=MESH)

    row8 = iota((8, 1), 0)
    ms[...] = jnp.zeros_like(ms)
    ms[0:1, 0:MODES] = mfreq_r[...]
    ms[1:2, 0:MODES] = mamp_r[...]
    ms[2:3, 0:MODES] = mmap_r[...].astype(F32)
    moment = (HIST + row8 % STEPS).astype(F32)
    waves = ms[1:2, :] * half_wave(ms[0:1, :] * moment, jnp.zeros((8, 1), F32))
    high = waves.astype(BF).astype(F32)
    waves = jnp.where(row8 < STEPS, high, waves - high).astype(BF)
    pick = jnp.where(iota((SOURCES, 1), 0).astype(F32) == ms[2:3, :], 1.0, 0.0).astype(BF)
    drive = dot_nt(waves, pick)
    drive = drive + pltpu.roll(drive, 4, 0)
    high = drive.astype(BF).astype(F32)
    drive = jnp.where(row8 < STEPS, high, drive - high).astype(BF)
    pick = jnp.where(iota((SOURCES, 1), 0) == sid_r[...], 1.0, 0.0).astype(BF)
    weight = dot_nn(drive, pick)
    weight = (weight + pltpu.roll(weight, 4, 0)) * sgain_r[...]
    high = weight.astype(BF).astype(F32)
    wv[...] = jnp.where(row8 < STEPS, high, weight - high)
    lx = spos_r[0:1, :] - ix * TX
    ly = spos_r[1:2, :] - iy * TY
    lz = spos_r[2:3, :] - iz * TZ
    inside = (lx >= 0) & (lx < TX) & (ly >= 0) & (ly < TY) & (lz >= 0) & (lz < TZ)
    srow[...] = jnp.where(inside, lx * TY + ly, -1).astype(F32)
    scol[...] = lz.astype(F32)

    lane = iota((1, TZ), 1)
    even = lane % 2 == 0

    def z_pack(slabs, base, packed):
        for i, piece in slabs:
            turned = pltpu.roll(piece, (base + 2 * i) % TZ, 1) if (base + 2 * i) % TZ else piece
            here = ((lane + 1 - base + TZ) % TZ) // 2 == i
            packed = jnp.where(here, turned, packed)
        return packed

    def pieces(ref, n):
        return [(i, ref[n, i * 8:(i + 1) * 8, :]) for i in range(ROWS // 8)]

    def face_copies(n):
        src = pst.at[n]
        ends = (
            (src.at[pl.ds(0, TY)], gxp.at[n]),
            (src.at[pl.ds(ROWS - TY, TY)], gxm.at[n]),
            (ys.at[n, 0], gyp.at[n]),
            (ys.at[n, 1], gym.at[n]),
            (zs.at[n], gzp.at[n]),
            (zs.at[n], gzm.at[n]),
        )
        return [
            (has, pltpu.make_async_remote_copy(
                src_ref=a, dst_ref=b, send_sem=ss.at[n, i], recv_sem=rs.at[n, i],
                device_id=target, device_id_type=MESH))
            for i, ((has, target), (a, b)) in enumerate(zip(sides, ends))
        ]

    def send_faces(n):
        for has, copy in face_copies(n):
            @pl.when(has)
            def _(copy=copy):
                copy.start()

    def recv_faces(n):
        copies = face_copies(n)
        for i in range(6):
            has = sides[i ^ 1][0]
            copy = copies[i][1]
            @pl.when(has)
            def _(copy=copy):
                copy.wait_recv()

    def y_faces(n):
        ys[n, 0] = pst[n, pl.ds(0, TX, stride=TY), :]
        ys[n, 1] = pst[n, pl.ds(TY - 1, TX, stride=TY), :]

    for k in (0, 3, 1, 2):
        loads[k].wait()
    pst[0] = fv[0]
    y_faces(0)
    svy[...] = fv[2, pl.ds(TY - 1, TX, stride=TY), :]
    packed = z_pack(pieces(fv, 0), 0, jnp.zeros((8, TZ), F32))
    zs[0] = z_pack(pieces(fv, 3), 64, packed)

    expected = (
        OWN - 1
        + jnp.where(low_x, 0, 1) + jnp.where(high_x, 0, 1)
        + jnp.where(low_y, 0, 1) + jnp.where(high_y, 0, 1)
    )
    pl.semaphore_wait(barrier, expected)
    send_faces(0)
    vx_copy = pltpu.make_async_remote_copy(
        src_ref=fv.at[1, pl.ds(ROWS - TY, TY)], dst_ref=gvx, send_sem=vss.at[0], recv_sem=vrs.at[0],
        device_id=sides[1][1], device_id_type=MESH)
    vy_copy = pltpu.make_async_remote_copy(
        src_ref=svy, dst_ref=gvy, send_sem=vss.at[1], recv_sem=vrs.at[1],
        device_id=sides[3][1], device_id_type=MESH)

    @pl.when(sides[1][0])
    def _():
        vx_copy.start()

    @pl.when(sides[3][0])
    def _():
        vy_copy.start()

    acc[...] = jnp.zeros_like(acc)

    @pl.loop(0, SRC // KC)
    def _(chunk):
        span = pl.ds(pl.multiple_of(chunk * KC, KC), KC)
        a = jnp.where(iota((ROWS, 1), 0).astype(F32) == srow[:, span], 1.0, 0.0).astype(BF)
        m = iota((TZ, 1), 0).astype(F32) == scol[:, span]
        b = jnp.concatenate([jnp.where(m, wv[q:q + 1, span], 0.0).astype(BF) for q in range(2 * STEPS)], axis=0)
        acc[...] += dot_nt(a, b)

    eye = iota((TONES, TONES), 0) == iota((TONES, TONES), 1)
    freq = jnp.sum(jnp.where(eye, tone_r[...], 0.0), axis=1, keepdims=True)
    freq = jnp.concatenate([freq, freq], axis=0)
    angle = freq * lane.astype(F32)
    basis = half_wave(angle, jnp.where(iota((NB, 1), 0) < TONES, 0.5, 0.0).astype(F32)) * 0.125
    for n in range(STEPS):
        bt[n * NB:(n + 1) * NB, :] = jnp.broadcast_to(basis[:, HIST + n:HIST + n + 1], (NB, CAP))

    held = iota((OWN, OWN), 0) == iota((OWN, OWN), 1)
    counts = jnp.sum(jnp.where(held, count_r[...].astype(F32), 0.0), axis=1, keepdims=True)
    live = jnp.where(lane.astype(F32) < counts, 1.0, 0.0).astype(F32)
    hist_load.wait()
    hv[HIST * OWN:, :] = jnp.zeros((STEPS * OWN, CAP), F32)
    bh, bl = split(basis)
    lhs = jnp.concatenate([bh, bl, bh], axis=1)
    for e in range(0, OWN, 2):
        hh, hl = split(jnp.concatenate(
            [hv[pl.ds(e, HIST + STEPS, stride=OWN), :], hv[pl.ds(e + 1, HIST + STEPS, stride=OWN), :]], axis=1))
        part = dot_nn(lhs, jnp.concatenate([hh, hh, hl], axis=0))
        ov[pl.ds(e, NB, stride=OWN), :] = part[:, :CAP] * live[e:e + 1]
        ov[pl.ds(e + 1, NB, stride=OWN), :] = part[:, CAP:] * live[e + 1:e + 2]

    for d in range(OWN):
        cells = cell_r[d:d + 1, :]
        span = slice(d * CAP, (d + 1) * CAP)
        one = jnp.where(iota((TZ, 1), 0) == cells % TZ, 1.0, 0.0).astype(BF)
        cone[0:TZ, span] = one
        cone[TZ:2 * TZ, span] = one
        rsel[:, span] = cells // TZ
    sb[...] = jnp.zeros_like(sb)

    def listen(n):
        lhs = jnp.concatenate(split(pst[n + 1]), axis=1)
        for d in range(0, OWN, 2):
            span = slice(d * CAP, (d + 2) * CAP)
            seen = dot_nn(lhs, cone[:, span])
            got = jnp.sum(jnp.where(iota((ROWS, 1), 0) == rsel[:, span], seen, 0.0), axis=0, keepdims=True)
            sb[d * 8 + n:d * 8 + n + 1, :] = got[:, :CAP]
            sb[(d + 1) * 8 + n:(d + 1) * 8 + n + 1, :] = got[:, CAP:]

    sub = iota((TY, 1), 0)

    def behind(get, x, gx, gy, merged):
        own = get(x)
        xm = get(x - 1) if x else gx
        ym = jnp.where(sub == 0, gy[x:x + 1, :], pltpu.roll(own, 1, 0))
        ring = jnp.concatenate([roll_lanes(merged, -4 * x), roll_lanes(merged, -4 * x - 2)], axis=0)
        zm = pltpu.roll(jnp.where(lane == TZ - 1, ring, own), 1, 1)
        return xm, ym, zm

    def ahead(get, x, gx, gy, merged):
        own = get(x)
        xp = get(x + 1) if x < TX - 1 else gx
        yp = jnp.where(sub == TY - 1, gy[x:x + 1, :], pltpu.roll(own, TY - 1, 0))
        ring = jnp.concatenate([roll_lanes(merged, -4 * x), roll_lanes(merged, -4 * x - 2)], axis=0)
        zp = pltpu.roll(jnp.where(lane == 0, ring, own), TZ - 1, 1)
        return xp, yp, zp

    def roll_lanes(v, by):
        return pltpu.roll(v, by % TZ, 1) if by % TZ else v

    def slab(ref, x):
        return ref[x * TY:(x + 1) * TY, :]

    @pl.when(jnp.logical_not(low_x))
    def _():
        vx_copy.wait_recv()

    @pl.when(jnp.logical_not(low_y))
    def _():
        vy_copy.wait_recv()

    recv_faces(0)
    from_low = jnp.where(low_z, 0.0, gzm[0])
    vzg = roll_lanes(from_low, -64)
    vxg = jnp.where(low_x, 0.0, gvx[...])
    vyg = jnp.where(low_y, 0.0, gvy[...])
    for x in range(TX):
        own = [slab(fv.at[k], x) for k in (1, 2, 3)]
        xm = slab(fv.at[1], x - 1) if x else vxg
        ym = jnp.where(sub == 0, vyg[x:x + 1, :], pltpu.roll(own[1], 1, 0))
        ring = jnp.concatenate([roll_lanes(vzg, -4 * x), roll_lanes(vzg, -4 * x - 2)], axis=0)
        zm = pltpu.roll(jnp.where(lane == TZ - 1, ring, own[2]), 1, 1)
        uv[x * TY:(x + 1) * TY, :] = 0.5 * ((own[0] - xm) + (own[1] - ym) + (own[2] - zm))

    gx_sum = jnp.zeros((TY, TZ), F32)
    gy_sum = jnp.zeros((TX, TZ), F32)
    gz_sum = jnp.zeros((8, TZ), F32)
    for n in range(STEPS):
        if n:
            recv_faces(n)
        get = lambda x, n=n: pst[n, x * TY:(x + 1) * TY, :]
        xg = jnp.where(high_x, 0.0, gxp[n])
        yg = jnp.where(high_y, 0.0, gyp[n])
        zg = jnp.where(high_z, 0.0, gzp[n])
        gx_sum, gy_sum, gz_sum = gx_sum + xg, gy_sum + yg, gz_sum + zg
        xl = jnp.where(low_x, get(0), gxm[n])
        yl = jnp.where(low_y, ys[n, 0], gym[n])
        zl = jnp.where(low_z, roll_lanes(zs[n], -1), gzm[n])
        merged = jnp.where(even, zg, zl)
        for x in range(TX):
            at = slice(x * TY, (x + 1) * TY)
            own = get(x)
            xm, ym, zm = behind(get, x, xl, yl, merged)
            xp, yp, zp = ahead(get, x, xg, yg, merged)
            lap = (xm + xp) + (ym + yp) + (zm + zp) - 6.0 * own
            u = uv[at, :] - 0.25 * lap
            uv[at, :] = u
            new = own - u + (acc[at, n * TZ:(n + 1) * TZ] + acc[at, (STEPS + n) * TZ:(STEPS + n + 1) * TZ])
            pst[n + 1, at, :] = new
            psum[at, :] = own if n == 0 else psum[at, :] + own
        if n < STEPS - 1:
            y_faces(n + 1)
            zs[n + 1] = z_pack(pieces(pst, n + 1), 0, jnp.zeros((8, TZ), F32))
            send_faces(n + 1)
        listen(n)

    def block_copy(k):
        target = lax.rem(iz + k, OWN)
        return pltpu.make_async_remote_copy(
            src_ref=sb.at[pl.ds(pl.multiple_of(target * 8, 8), 8)],
            dst_ref=rb.at[pl.ds(pl.multiple_of(iz * 8, 8), 8)],
            send_sem=ass.at[k], recv_sem=ars.at[k], device_id={"gz": target}, device_id_type=MESH)

    sends = [block_copy(k) for k in range(1, OWN)]
    for copy in sends:
        copy.start()
    mine = pl.ds(pl.multiple_of(iz * 8, 8), 8)
    rb[mine, :] = sb[mine, :]

    for n in range(STEPS):
        for has, copy in face_copies(n):
            @pl.when(has)
            def _(copy=copy):
                copy.wait_send()

    @pl.when(sides[1][0])
    def _():
        vx_copy.wait_send()

    @pl.when(sides[3][0])
    def _():
        vy_copy.wait_send()

    outs = [pltpu.make_async_copy(pst.at[STEPS], fout_h.at[0], osem.at[0])]
    outs[0].start()
    total = lambda x: slab(psum, x)
    for x in range(TX):
        at = slice(x * TY, (x + 1) * TY)
        own = total(x)
        xp, yp, zp = ahead(total, x, gx_sum, gy_sum, gz_sum)
        fv[1, at, :] = fv[1, at, :] - 0.5 * (xp - own)
        fv[2, at, :] = fv[2, at, :] - 0.5 * (yp - own)
        fv[3, at, :] = fv[3, at, :] - 0.5 * (zp - own)
    outs.append(pltpu.make_async_copy(fv.at[pl.ds(1, 3)], fout_h.at[pl.ds(1, 3)], osem.at[1]))
    outs[1].start()

    for copy in sends:
        copy.wait_recv()
    heard = [rb[pl.ds(n, OWN, stride=8), :] * live for n in range(STEPS)]
    parts = 4
    per = NB // parts
    for part in range(parts):
        for j in range(part * per, (part + 1) * per):
            at = slice(j * OWN, (j + 1) * OWN)
            term = ov[at, :]
            for n in range(STEPS):
                term = term + bt[n * NB + j:n * NB + j + 1, :] * heard[n]
            ov[at, :] = term
        rows = pl.ds(part * per * OWN, per * OWN)
        outs.append(pltpu.make_async_copy(ov.at[rows], cout_h.at[rows], osem.at[2 + part]))
        outs[-1].start()
    for copy in sends:
        copy.wait_send()
    for copy in outs:
        copy.wait()


def body(
    fields, tone_freq, mode_freq, mode_amp, mode_map, src_pos, src_id, src_gain, sample_cell, sample_count, history
):
    vmem = pl.BlockSpec(memory_space=pltpu.VMEM)
    hbm = pl.BlockSpec(memory_space=pl.ANY)
    face = (STEPS, TY, TZ)
    fields_out, coefficients = pl.pallas_call(
        kernel,
        out_shape=(
            jax.ShapeDtypeStruct((4, ROWS, TZ), F32),
            jax.ShapeDtypeStruct((NB * OWN, CAP), F32),
        ),
        in_specs=[hbm] + [vmem] * 9 + [hbm],
        out_specs=(hbm, hbm),
        scratch_shapes=[
            pltpu.VMEM((4, ROWS, TZ), F32),
            pltpu.VMEM(((HIST + STEPS) * OWN, CAP), F32),
            pltpu.VMEM((STEPS + 1, ROWS, TZ), F32),
            pltpu.VMEM((ROWS, TZ), F32),
            pltpu.VMEM((ROWS, TZ), F32),
            pltpu.VMEM((8, 2048), F32),
            pltpu.VMEM((8, SRC), F32),
            pltpu.VMEM((1, SRC), F32),
            pltpu.VMEM((1, SRC), F32),
            pltpu.VMEM((ROWS, 2 * STEPS * TZ), F32),
            pltpu.VMEM((2 * TZ, SLOTS), BF),
            pltpu.VMEM((1, SLOTS), jnp.int32),
            pltpu.VMEM((NB * OWN, CAP), F32),
            pltpu.VMEM((STEPS * NB, CAP), F32),
            pltpu.VMEM((OWN * 8, CAP), F32),
            pltpu.VMEM((OWN * 8, CAP), F32),
            pltpu.VMEM((STEPS, 2, TX, TZ), F32),
            pltpu.VMEM((STEPS, 8, TZ), F32),
            pltpu.VMEM(face, F32),
            pltpu.VMEM(face, F32),
            pltpu.VMEM(face, F32),
            pltpu.VMEM(face, F32),
            pltpu.VMEM((STEPS, 8, TZ), F32),
            pltpu.VMEM((STEPS, 8, TZ), F32),
            pltpu.VMEM((TY, TZ), F32),
            pltpu.VMEM((TX, TZ), F32),
            pltpu.VMEM((TX, TZ), F32),
            pltpu.SemaphoreType.DMA((4,)),
            pltpu.SemaphoreType.DMA,
            pltpu.SemaphoreType.DMA((6,)),
            pltpu.SemaphoreType.DMA((STEPS, 6)),
            pltpu.SemaphoreType.DMA((STEPS, 6)),
            pltpu.SemaphoreType.DMA((2,)),
            pltpu.SemaphoreType.DMA((2,)),
            pltpu.SemaphoreType.DMA((OWN,)),
            pltpu.SemaphoreType.DMA((OWN,)),
        ],
        compiler_params=pltpu.CompilerParams(
            collective_id=0, has_side_effects=True, vmem_limit_bytes=63 * 1024 * 1024
        ),
    )(
        fields.reshape(4, ROWS, TZ),
        tone_freq.reshape(1, TONES),
        mode_freq.reshape(1, MODES),
        mode_amp.reshape(1, MODES),
        mode_map.reshape(1, MODES),
        src_pos,
        src_id.reshape(1, SRC),
        src_gain.reshape(1, SRC),
        sample_cell.reshape(OWN, CAP),
        sample_count.reshape(1, OWN),
        history.reshape(HIST * OWN, CAP),
    )
    return fields_out.reshape(fields.shape), coefficients.reshape(NB, 1, 1, 1, OWN, CAP)


def solution(mesh):
    in_specs = (
        P(None, "gx", "gy", "gz"),
        P(),
        P(),
        P(),
        P(),
        P(),
        P(),
        P(),
        P("gx", "gy", "gz", None, None),
        P("gx", "gy", None, "gz"),
        P(None, "gx", "gy", "gz", None, None),
    )
    out_specs = (P(None, "gx", "gy", "gz"), P(None, "gx", "gy", "gz", None, None))
    return jax.shard_map(body, mesh=mesh, in_specs=in_specs, out_specs=out_specs, check_vma=False)
```

```python
import jax
import jax.numpy as jnp
from jax import lax
from jax.experimental import pallas as pl
from jax.experimental.pallas import tpu as pltpu
from jax.sharding import PartitionSpec as P

STEPS = 4
HIST = 124
SOURCES = 48
TONES = 48
MODES = 2000
SRC = 4096
TX, TY, TZ = 16, 16, 128
ROWS = TX * TY
OWN = 16
CAP = 128
SLOTS = OWN * CAP
NB = 2 * TONES
KC = 1024
F32 = jnp.float32
BF = jnp.bfloat16
MESH = pl.DeviceIdType.MESH


def split(values):
    high = values.astype(BF)
    return high, (values - high.astype(F32)).astype(BF)


def dot_nn(a, b):
    return lax.dot_general(a, b, (((1,), (0,)), ((), ())), preferred_element_type=F32)


def dot_nt(a, b):
    return lax.dot_general(a, b, (((1,), (1,)), ((), ())), preferred_element_type=F32)


def half_wave(x, half):
    k = jnp.floor(x * 0.3183098861837907 + (0.5 - half))
    h = k + half
    r = x - h * 3.140625
    r = r - h * 0.0009670257568359375
    r = r - h * 6.2771141529083251953e-07
    q = r * r
    s = -2.505210838544172e-08
    for c in (2.7557319223985893e-06, -1.984126984126984e-04, 8.333333333333333e-03, -0.16666666666666666):
        s = s * q + c
    s = r + r * q * s
    sign = 1.0 - 2.0 * (k - 2.0 * jnp.floor(k * 0.5))
    return jnp.where(half > 0.25, -sign, sign) * s


def iota(shape, dim):
    return lax.broadcasted_iota(jnp.int32, shape, dim)


GROUP = 8
WIDE = 24
EXT = 584
WIDTHS = (("p", 4), ("c", 3), ("v", 3), ("d2", 2), ("d3", 1))
PLANES = [(f, k) for f, width in WIDTHS for k in range(width)]
DIAGS = ((-1, -1), (-1, 1), (1, -1), (1, 1))
SIDES = ((-1, 0), (1, 0), (0, -1), (0, 1)) + DIAGS
CORNER = [("p", i, j) for i in range(3) for j in range(3 - i)] + [
    (f, i, j) for f in ("c", "v") for i in range(2) for j in range(2 - i)] + [("d2", 0, 0)]
ZPACK = (("p", 4, 65), ("c", 4, 65), ("d2", 10, 53), ("d3", 13, 47))


def row_of(x, y):
    return 8 + WIDE * (x + 4) + y


def zpack_slots():
    start, at = {}, 0
    for f, first, count in ZPACK:
        start[f] = at
        at += -(-count // 16)
    return start, at


ZSTART, ZCOUNT = zpack_slots()


def roll_lanes(v, by):
    return pltpu.roll(v, by % TZ, 1) if by % TZ else v


def kernel(
    fields_h, tone_r, mfreq_r, mamp_r, mmap_r, spos_r, sid_r, sgain_r, cell_r, count_r, hist_h,
    fout_h, cout_h,
    fv, hv, pm, pq, cm, cq, d2m, d2q, d3m, d3q, d4, vzm, vxs, vys, plast, sm, sq,
    ms, wv, srow, scol, acc, cone, rsel, ov, bt, sb, rb,
    xs, xr, ys, yr, ds, dr, zs, zr,
    fsem, hsem, osem, ss, rs, zss, zrs, ass, ars,
):
    ix = lax.axis_index("gx")
    iy = lax.axis_index("gy")
    iz = lax.axis_index("gz")
    low_x, high_x = ix == 0, ix == 3
    low_y, high_y = iy == 0, iy == 3
    low_z, high_z = iz == 0, iz == OWN - 1

    loads = [pltpu.make_async_copy(fields_h.at[k], fv.at[k], fsem.at[k]) for k in range(4)]
    for copy in loads:
        copy.start()
    hist_load = pltpu.make_async_copy(hist_h, hv.at[pl.ds(0, HIST * OWN)], hsem)
    hist_load.start()

    def has(sx, sy):
        ok = None
        for s, low, high in ((sx, low_x, high_x), (sy, low_y, high_y)):
            if s:
                here = jnp.logical_not(low if s < 0 else high)
                ok = here if ok is None else ok & here
        return ok

    def at_side(sx, sy):
        where = {}
        if sx:
            where["gx"] = ix + sx
        if sy:
            where["gy"] = iy + sy
        return where

    barrier = pltpu.get_barrier_semaphore()
    for k in range(1, OWN):
        pl.semaphore_signal(barrier, inc=1, device_id={"gz": lax.rem(iz + k, OWN)}, device_id_type=MESH)
    expected = OWN - 1
    for side in SIDES:
        expected = expected + jnp.where(has(*side), 1, 0)

        @pl.when(has(*side))
        def _(side=side):
            pl.semaphore_signal(barrier, inc=1, device_id=at_side(*side), device_id_type=MESH)

    lane = iota((1, TZ), 1)
    sub = iota((TY, 1), 0)
    row8 = iota((8, 1), 0)
    ext = {"p": pm.at[0], "c": cm, "v": vzm, "d2": d2m, "d3": d3m}
    ring = {"p": pq.at[0], "c": cq, "d2": d2q, "d3": d3q}
    for ref in (cm, cq, d2m, d2q, d3m, d3q, vzm, vxs, vys, sm, sq, pm, pq):
        ref[...] = jnp.zeros_like(ref)

    ms[...] = jnp.zeros_like(ms)
    ms[0:1, 0:MODES] = mfreq_r[...]
    ms[1:2, 0:MODES] = mamp_r[...]
    ms[2:3, 0:MODES] = mmap_r[...].astype(F32)
    moment = (HIST + row8 % STEPS).astype(F32)
    waves = ms[1:2, :] * half_wave(ms[0:1, :] * moment, jnp.zeros((8, 1), F32))
    high = waves.astype(BF).astype(F32)
    waves = jnp.where(row8 < STEPS, high, waves - high).astype(BF)
    pick = jnp.where(iota((SOURCES, 1), 0).astype(F32) == ms[2:3, :], 1.0, 0.0).astype(BF)
    drive = dot_nt(waves, pick)
    drive = drive + pltpu.roll(drive, 4, 0)
    high = drive.astype(BF).astype(F32)
    drive = jnp.where(row8 < STEPS, high, drive - high).astype(BF)
    pick = jnp.where(iota((SOURCES, 1), 0) == sid_r[...], 1.0, 0.0).astype(BF)
    weight = dot_nn(drive, pick)
    weight = (weight + pltpu.roll(weight, 4, 0)) * sgain_r[...]
    high = weight.astype(BF).astype(F32)
    wv[...] = jnp.where(row8 < STEPS, high, weight - high)
    lx = spos_r[0:1, :] - ix * TX
    ly = spos_r[1:2, :] - iy * TY
    lz = spos_r[2:3, :] - iz * TZ
    inside = (lx >= 0) & (lx < TX) & (ly >= 0) & (ly < TY) & (lz >= 0) & (lz < TZ)
    srow[...] = jnp.where(inside, lx * TY + ly, -1).astype(F32)
    scol[...] = lz.astype(F32)

    acc[...] = jnp.zeros_like(acc)

    @pl.loop(0, SRC // KC)
    def _(chunk):
        span = pl.ds(pl.multiple_of(chunk * KC, KC), KC)
        a = jnp.where(iota((ROWS, 1), 0).astype(F32) == srow[:, span], 1.0, 0.0).astype(BF)
        m = iota((TZ, 1), 0).astype(F32) == scol[:, span]
        b = jnp.concatenate([jnp.where(m, wv[q:q + 1, span], 0.0).astype(BF) for q in range(2 * STEPS)], axis=0)
        acc[...] += dot_nt(a, b)

    for copy in loads:
        copy.wait()
    for x in range(TX):
        at = slice(x * TY, (x + 1) * TY)
        to = slice(row_of(x, 0), row_of(x, 0) + TY)
        added = [acc[at, n * TZ:(n + 1) * TZ] + acc[at, (STEPS + n) * TZ:(STEPS + n + 1) * TZ] for n in range(STEPS)]
        p = fv[0, at, :]
        vx, vy, vz = (fv[k, at, :] for k in (1, 2, 3))
        gone = vx + (vy - jnp.where(sub == 0, 0.0, pltpu.roll(vy, 1, 0)))
        gone = gone + (vz - jnp.where(lane == 0, 0.0, pltpu.roll(vz, 1, 1)))
        if x:
            gone = gone - fv[1, (x - 1) * TY:x * TY, :]
        pm[0, to, :] = p
        cm[to, :] = added[0] - 0.5 * (gone + p)
        d2m[to, :] = added[1] - added[0]
        d3m[to, :] = added[2] - added[1]
        d4[at, :] = added[3] - added[2]
        vzm[to, :] = 0.5 * vz
    vxs[1, 4:20, :] = 0.5 * fv[1, ROWS - TY:ROWS, :]
    vys[1, 4:20, :] = 0.5 * fv[2, pl.ds(TY - 1, TX, stride=TY), :]

    for s in (0, 1):
        cell = (lambda k: k) if s == 0 else (lambda k: TX - 1 - k)
        for i, (f, k) in enumerate(PLANES):
            xs[s, i * 16:(i + 1) * 16, :] = ext[f][row_of(cell(k), 0):row_of(cell(k), 0) + TY, :]
            ys[s, i * 16:(i + 1) * 16, :] = ext[f][pl.ds(row_of(0, cell(k)), TX, stride=WIDE), :]
        for k in range(3):
            xs[s, 208 + k:209 + k, :] = vys[1, 4 + cell(k):5 + cell(k), :]
            ys[s, 208 + k:209 + k, :] = vxs[1, 4 + cell(k):5 + cell(k), :]
    xs[1, 224:240, :] = vxs[1, 4:20, :]
    ys[1, 224:240, :] = vys[1, 4:20, :]
    for s, (sx, sy) in enumerate(DIAGS):
        cx = (lambda k: k) if sx < 0 else (lambda k: TX - 1 - k)
        cy = (lambda k: k) if sy < 0 else (lambda k: TY - 1 - k)
        for i, (f, a, b) in enumerate(CORNER):
            r = row_of(cx(a), cy(b))
            ds[s, i:i + 1, :] = ext[f][r:r + 1, :]
        for k in range(3):
            ds[s, 13 + k:14 + k, :] = vxs[1, 4 + cy(k):5 + cy(k), :]
            ds[s, 16 + k:17 + k, :] = vys[1, 4 + cx(k):5 + cx(k), :]

    eye = iota((TONES, TONES), 0) == iota((TONES, TONES), 1)
    freq = jnp.sum(jnp.where(eye, tone_r[...], 0.0), axis=1, keepdims=True)
    freq = jnp.concatenate([freq, freq], axis=0)
    angle = freq * lane.astype(F32)
    basis = half_wave(angle, jnp.where(iota((NB, 1), 0) < TONES, 0.5, 0.0).astype(F32)) * 0.125
    for n in range(STEPS):
        bt[n * NB:(n + 1) * NB, :] = jnp.broadcast_to(basis[:, HIST + n:HIST + n + 1], (NB, CAP))
    held = iota((OWN, OWN), 0) == iota((OWN, OWN), 1)
    counts = jnp.sum(jnp.where(held, count_r[...].astype(F32), 0.0), axis=1, keepdims=True)
    live = jnp.where(lane.astype(F32) < counts, 1.0, 0.0).astype(F32)
    hist_load.wait()
    hv[HIST * OWN:, :] = jnp.zeros((STEPS * OWN, CAP), F32)
    bh, bl = split(basis)
    lhs = jnp.concatenate([bh, bl, bh], axis=1)
    for e in range(0, OWN, 2):
        hh, hl = split(jnp.concatenate(
            [hv[pl.ds(e, HIST + STEPS, stride=OWN), :], hv[pl.ds(e + 1, HIST + STEPS, stride=OWN), :]], axis=1))
        part = dot_nn(lhs, jnp.concatenate([hh, hh, hl], axis=0))
        ov[pl.ds(e, NB, stride=OWN), :] = part[:, :CAP] * live[e:e + 1]
        ov[pl.ds(e + 1, NB, stride=OWN), :] = part[:, CAP:] * live[e + 1:e + 2]

    for d in range(OWN):
        cells = cell_r[d:d + 1, :]
        span = slice(d * CAP, (d + 1) * CAP)
        one = jnp.where(iota((TZ, 1), 0) == cells % TZ, 1.0, 0.0).astype(BF)
        cone[0:TZ, span] = one
        cone[TZ:2 * TZ, span] = one
        rsel[:, span] = cells // TZ
    sb[...] = jnp.zeros_like(sb)

    def first_copies():
        made = []
        for i, side in enumerate(SIDES):
            if i < 2:
                src, dst, rows = xs.at[i], xr.at[i], 224 + 16 * i
            elif i < 4:
                src, dst, rows = ys.at[i - 2], yr.at[i - 2], 224 + 16 * (i - 2)
            else:
                src, dst, rows = ds.at[i - 4], dr.at[i - 4], 24
            made.append(pltpu.make_async_remote_copy(
                src_ref=src.at[pl.ds(0, rows)], dst_ref=dst.at[pl.ds(0, rows)], send_sem=ss.at[i], recv_sem=rs.at[i],
                device_id=at_side(*side), device_id_type=MESH))
        return made

    firsts = first_copies()
    pl.semaphore_wait(barrier, expected)
    for side, copy in zip(SIDES, firsts):
        @pl.when(has(*side))
        def _(copy=copy):
            copy.start()

    for i in range(4):
        sx, sy = SIDES[i]
        s = i % 2
        out = (lambda k: TX + k) if s == 0 else (lambda k: -1 - k)

        @pl.when(has(-sx, -sy))
        def _(i=i, s=s, out=out):
            firsts[i].wait_recv()
            for j, (f, k) in enumerate(PLANES):
                if i < 2:
                    ext[f][row_of(out(k), 0):row_of(out(k), 0) + TY, :] = xr[s, j * 16:(j + 1) * 16, :]
                else:
                    ext[f][pl.ds(row_of(0, out(k)), TX, stride=WIDE), :] = yr[s, j * 16:(j + 1) * 16, :]
            got = xr if i < 2 else yr
            side_v, low_v = (vys, vxs) if i < 2 else (vxs, vys)
            for k in range(3):
                side_v[1, 4 + out(k):5 + out(k), :] = got[s, 208 + k:209 + k, :]
            if s == 1:
                low_v[0, 4:20, :] = got[s, 224:240, :]

    for i in range(4, 8):
        sx, sy = SIDES[i]
        ox = (lambda k: TX + k) if sx < 0 else (lambda k: -1 - k)
        oy = (lambda k: TY + k) if sy < 0 else (lambda k: -1 - k)

        @pl.when(has(-sx, -sy))
        def _(i=i, sx=sx, sy=sy, ox=ox, oy=oy):
            firsts[i].wait_recv()
            for j, (f, a, b) in enumerate(CORNER):
                r = row_of(ox(a), oy(b))
                ext[f][r:r + 1, :] = dr[i - 4, j:j + 1, :]
            for k in range(3):
                if sx > 0:
                    vxs[0, 4 + oy(k):5 + oy(k), :] = dr[i - 4, 13 + k:14 + k, :]
                if sy > 0:
                    vys[0, 4 + ox(k):5 + ox(k), :] = dr[i - 4, 16 + k:17 + k, :]

    for k, x in ((0, 0), (1, TX)):
        r = row_of(x, -4)
        cm[r:r + WIDE, :] = cm[r:r + WIDE, :] + vxs[k]
    for k, y in ((0, 0), (1, TY)):
        r = pl.ds(row_of(-4, y), WIDE, stride=WIDE)
        cm[r, :] = cm[r, :] + vys[k]

    for flag, low, along_x in ((low_x, True, True), (high_x, False, True), (low_y, True, False), (high_y, False, False)):
        @pl.when(flag)
        def _(low=low, along_x=along_x):
            def rows(q):
                return pl.ds(row_of(q, -4), WIDE) if along_x else pl.ds(row_of(-4, q), WIDE, stride=WIDE)

            for f, width in WIDTHS:
                for k in range(width):
                    if low:
                        ext[f][rows(-1 - k), :] = ext[f][rows(k), :]
                    elif k == 0:
                        ext[f][rows(TX), :] = jnp.zeros((WIDE, TZ), F32)
                    else:
                        ext[f][rows(TX + k), :] = -ext[f][rows(TX - k), :]

    for f, first, count in ZPACK:
        for t in range(0, count, 16):
            packed = jnp.zeros((GROUP, TZ), F32)
            for u in range(min(16, count - t)):
                g = first + t + u
                value = ext[f][g * 8:g * 8 + 8, :]
                if f == "c":
                    value = jnp.where(lane == TZ - 4, roll_lanes(vzm[g * 8:g * 8 + 8, :], -3), value)
                here = ((lane + 4) % TZ) // 8 == u
                packed = jnp.where(here, roll_lanes(value, 8 * u), packed)
            zs[ZSTART[f] + t // 16] = packed

    to_z = [
        pltpu.make_async_remote_copy(
            src_ref=zs, dst_ref=zr.at[s], send_sem=zss.at[s], recv_sem=zrs.at[s],
            device_id={"gz": iz + (2 * s - 1)}, device_id_type=MESH)
        for s in (0, 1)
    ]
    from_z = (jnp.logical_not(high_z), jnp.logical_not(low_z))
    for s in (0, 1):
        @pl.when(from_z[1 - s])
        def _(s=s):
            to_z[s].start()
    for s in (0, 1):
        @pl.when(from_z[s])
        def _(s=s):
            to_z[s].wait_recv()

    place = (lane + 4) % 8
    for f, first, count in ZPACK:
        for t in range(0, count, 16):
            slot = ZSTART[f] + t // 16
            own = zs[slot]
            below = jnp.zeros((GROUP, TZ), F32)
            above = jnp.zeros((GROUP, TZ), F32)
            for k in range(4):
                if not (f == "c" and k == 3):
                    below = jnp.where(place == 3 - k, roll_lanes(own, -(2 * k + 1)), below)
                if k:
                    above = jnp.where(place == 4 + k, -roll_lanes(own, 2 * k), above)
            merged = jnp.where(
                place < 4, jnp.where(low_z, below, zr[1, slot]), jnp.where(high_z, above, zr[0, slot]))
            for u in range(min(16, count - t)):
                g = first + t + u
                at = slice(g * 8, g * 8 + 8)
                value = roll_lanes(merged, -8 * u)
                if f == "c":
                    flow = roll_lanes(jnp.where(lane == TZ - 4, value, 0.0), 4)
                    cm[at, :] = cm[at, :] + flow
                    flow = roll_lanes(jnp.where(lane == TZ - 1, vzm[at, :], 0.0), 1)
                    value = value + jnp.where(high_z, 0.0, flow)
                ring[f][at, :] = value

    def listen(n, get):
        lhs = jnp.concatenate(split(get), axis=1)
        for d in range(0, OWN, 2):
            span = slice(d * CAP, (d + 2) * CAP)
            seen = dot_nn(lhs, cone[:, span])
            got = jnp.sum(jnp.where(iota((ROWS, 1), 0) == rsel[:, span], seen, 0.0), axis=0, keepdims=True)
            sb[d * 8 + n:d * 8 + n + 1, :] = got[:, :CAP]
            sb[(d + 1) * 8 + n:(d + 1) * 8 + n + 1, :] = got[:, CAP:]

    for n in range(STEPS):
        d_main = (cm, d2m, d3m, d4)[n]
        d_ring = (cq, d2q, d3q, None)[n]
        main_span = (range(4, 69), range(7, 66), range(10, 63), [g for g in range(13, 60) if g % 3])[n]
        ring_span = (range(7, 66), range(10, 63), range(13, 60), ())[n]
        for g in main_span:
            at = slice(g * 8, g * 8 + 8)
            here, ghost = pm[n, at, :], pq[n, at, :]

            def stepped(ref, d, here, other):
                sums = (ref[n, g * 8 - WIDE:g * 8 - WIDE + 8, :] + ref[n, g * 8 + WIDE:g * 8 + WIDE + 8, :]) + (
                    ref[n, g * 8 - 1:g * 8 + 7, :] + ref[n, g * 8 + 1:g * 8 + 9, :])
                back = pltpu.roll(jnp.where(lane == TZ - 1, other, here), 1, 1)
                fore = pltpu.roll(jnp.where(lane == 0, other, here), TZ - 1, 1)
                new = d + 0.25 * (sums + (back + fore))
                return new if n == 0 else new + (0.5 * here - ref[n - 1, at, :])

            if n < STEPS - 1:
                pm[n + 1, at, :] = stepped(pm, d_main[at, :], here, ghost)
                if g in ring_span:
                    pq[n + 1, at, :] = stepped(pq, d_ring[at, :], ghost, here)
            else:
                x, half = divmod(g - 13, 3)
                own = slice(x * TY + half * 8, x * TY + half * 8 + 8)
                plast[own, :] = stepped(pm, d4[own, :], here, ghost)
        if n < STEPS - 1:
            listen(n, jnp.concatenate([pm[n + 1, row_of(x, 0):row_of(x, 0) + TY, :] for x in range(TX)], axis=0))
        else:
            listen(n, plast[...])

    def block_copy(k):
        target = lax.rem(iz + k, OWN)
        return pltpu.make_async_remote_copy(
            src_ref=sb.at[pl.ds(pl.multiple_of(target * 8, 8), 8)],
            dst_ref=rb.at[pl.ds(pl.multiple_of(iz * 8, 8), 8)],
            send_sem=ass.at[k], recv_sem=ars.at[k], device_id={"gz": target}, device_id_type=MESH)

    sends = [block_copy(k) for k in range(1, OWN)]
    for k in (8, 7, 9, 6, 10, 5, 11, 4, 12, 3, 13, 2, 14, 1, 15):
        sends[k - 1].start()
    mine = pl.ds(pl.multiple_of(iz * 8, 8), 8)
    rb[mine, :] = sb[mine, :]

    outs = [pltpu.make_async_copy(plast, fout_h.at[0], osem.at[0])]
    outs[0].start()
    for side, copy in zip(SIDES, firsts):
        @pl.when(has(*side))
        def _(copy=copy):
            copy.wait_send()
    for s in (0, 1):
        @pl.when(from_z[1 - s])
        def _(s=s):
            to_z[s].wait_send()
    for g in range(13, 64):
        at = slice(g * 8, g * 8 + 8)
        sm[at, :] = (pm[0, at, :] + pm[1, at, :]) + (pm[2, at, :] + pm[3, at, :])
        sq[at, :] = (pq[0, at, :] + pq[1, at, :]) + (pq[2, at, :] + pq[3, at, :])
    for x in range(TX):
        at = slice(x * TY, (x + 1) * TY)
        r = row_of(x, 0)
        own = sm[r:r + TY, :]
        fv[1, at, :] = fv[1, at, :] - 0.5 * (sm[r + WIDE:r + WIDE + TY, :] - own)
        fv[2, at, :] = fv[2, at, :] - 0.5 * (sm[r + 1:r + 1 + TY, :] - own)
        fore = pltpu.roll(jnp.where(lane == 0, sq[r:r + TY, :], own), TZ - 1, 1)
        fv[3, at, :] = fv[3, at, :] - 0.5 * (fore - own)
    outs.append(pltpu.make_async_copy(fv.at[pl.ds(1, 3)], fout_h.at[pl.ds(1, 3)], osem.at[1]))
    outs[1].start()

    for copy in sends:
        copy.wait_recv()
    heard = [rb[pl.ds(n, OWN, stride=8), :] * live for n in range(STEPS)]
    parts = 4
    per = NB // parts
    for part in range(parts):
        for j in range(part * per, (part + 1) * per):
            at = slice(j * OWN, (j + 1) * OWN)
            term = ov[at, :]
            for n in range(STEPS):
                term = term + bt[n * NB + j:n * NB + j + 1, :] * heard[n]
            ov[at, :] = term
        rows = pl.ds(part * per * OWN, per * OWN)
        outs.append(pltpu.make_async_copy(ov.at[rows], cout_h.at[rows], osem.at[2 + part]))
        outs[-1].start()
    for copy in sends:
        copy.wait_send()
    for copy in outs:
        copy.wait()


def body(
    fields, tone_freq, mode_freq, mode_amp, mode_map, src_pos, src_id, src_gain, sample_cell, sample_count, history
):
    vmem = pl.BlockSpec(memory_space=pltpu.VMEM)
    hbm = pl.BlockSpec(memory_space=pl.ANY)
    face = (STEPS, TY, TZ)
    fields_out, coefficients = pl.pallas_call(
        kernel,
        out_shape=(
            jax.ShapeDtypeStruct((4, ROWS, TZ), F32),
            jax.ShapeDtypeStruct((NB * OWN, CAP), F32),
        ),
        in_specs=[hbm] + [vmem] * 9 + [hbm],
        out_specs=(hbm, hbm),
        scratch_shapes=[
            pltpu.VMEM((4, ROWS, TZ), F32),
            pltpu.VMEM(((HIST + STEPS) * OWN, CAP), F32),
            pltpu.VMEM((STEPS, EXT, TZ), F32),
            pltpu.VMEM((STEPS, EXT, TZ), F32),
            pltpu.VMEM((EXT, TZ), F32),
            pltpu.VMEM((EXT, TZ), F32),
            pltpu.VMEM((EXT, TZ), F32),
            pltpu.VMEM((EXT, TZ), F32),
            pltpu.VMEM((EXT, TZ), F32),
            pltpu.VMEM((EXT, TZ), F32),
            pltpu.VMEM((ROWS, TZ), F32),
            pltpu.VMEM((EXT, TZ), F32),
            pltpu.VMEM((2, WIDE, TZ), F32),
            pltpu.VMEM((2, WIDE, TZ), F32),
            pltpu.VMEM((ROWS, TZ), F32),
            pltpu.VMEM((EXT, TZ), F32),
            pltpu.VMEM((EXT, TZ), F32),
            pltpu.VMEM((8, 2048), F32),
            pltpu.VMEM((8, SRC), F32),
            pltpu.VMEM((1, SRC), F32),
            pltpu.VMEM((1, SRC), F32),
            pltpu.VMEM((ROWS, 2 * STEPS * TZ), F32),
            pltpu.VMEM((2 * TZ, SLOTS), BF),
            pltpu.VMEM((1, SLOTS), jnp.int32),
            pltpu.VMEM((NB * OWN, CAP), F32),
            pltpu.VMEM((STEPS * NB, CAP), F32),
            pltpu.VMEM((OWN * 8, CAP), F32),
            pltpu.VMEM((OWN * 8, CAP), F32),
            pltpu.VMEM((2, 240, TZ), F32),
            pltpu.VMEM((2, 240, TZ), F32),
            pltpu.VMEM((2, 240, TZ), F32),
            pltpu.VMEM((2, 240, TZ), F32),
            pltpu.VMEM((4, 24, TZ), F32),
            pltpu.VMEM((4, 24, TZ), F32),
            pltpu.VMEM((ZCOUNT, GROUP, TZ), F32),
            pltpu.VMEM((2, ZCOUNT, GROUP, TZ), F32),
            pltpu.SemaphoreType.DMA((4,)),
            pltpu.SemaphoreType.DMA,
            pltpu.SemaphoreType.DMA((6,)),
            pltpu.SemaphoreType.DMA((8,)),
            pltpu.SemaphoreType.DMA((8,)),
            pltpu.SemaphoreType.DMA((2,)),
            pltpu.SemaphoreType.DMA((2,)),
            pltpu.SemaphoreType.DMA((OWN,)),
            pltpu.SemaphoreType.DMA((OWN,)),
        ],
        compiler_params=pltpu.CompilerParams(
            collective_id=0, has_side_effects=True, vmem_limit_bytes=63 * 1024 * 1024
        ),
    )(
        fields.reshape(4, ROWS, TZ),
        tone_freq.reshape(1, TONES),
        mode_freq.reshape(1, MODES),
        mode_amp.reshape(1, MODES),
        mode_map.reshape(1, MODES),
        src_pos,
        src_id.reshape(1, SRC),
        src_gain.reshape(1, SRC),
        sample_cell.reshape(OWN, CAP),
        sample_count.reshape(1, OWN),
        history.reshape(HIST * OWN, CAP),
    )
    return fields_out.reshape(fields.shape), coefficients.reshape(NB, 1, 1, 1, OWN, CAP)


def solution(mesh):
    in_specs = (
        P(None, "gx", "gy", "gz"),
        P(),
        P(),
        P(),
        P(),
        P(),
        P(),
        P(),
        P("gx", "gy", "gz", None, None),
        P("gx", "gy", None, "gz"),
        P(None, "gx", "gy", "gz", None, None),
    )
    out_specs = (P(None, "gx", "gy", "gz"), P(None, "gx", "gy", "gz", None, None))
    return jax.shard_map(body, mesh=mesh, in_specs=in_specs, out_specs=out_specs, check_vma=False)
```

```python
import jax
import jax.numpy as jnp
import numpy as np
from jax import lax
from jax.experimental import pallas as pl
from jax.experimental.pallas import tpu as pltpu
from jax.sharding import PartitionSpec as P

STEPS = 4
HIST = 124
SOURCES = 48
TONES = 48
MODES = 2000
SRC = 4096
TX, TY, TZ = 16, 16, 128
ROWS = TX * TY
OWN = 16
CAP = 128
SLOTS = OWN * CAP
NB = 2 * TONES
KC = 1024
F32 = jnp.float32
BF = jnp.bfloat16
MESH = pl.DeviceIdType.MESH
ONE = np.asarray(1, BF)
ZERO = np.asarray(0, BF)


def split(values):
    high = values.astype(BF)
    return high, (values - high.astype(F32)).astype(BF)


def dot_nn(a, b):
    return lax.dot_general(a, b, (((1,), (0,)), ((), ())), preferred_element_type=F32)


def dot_nt(a, b):
    return lax.dot_general(a, b, (((1,), (1,)), ((), ())), preferred_element_type=F32)


def half_wave(x, half):
    k = jnp.floor(x * 0.3183098861837907 + (0.5 - half))
    h = k + half
    r = x - h * 3.140625
    r = r - h * 0.0009670257568359375
    r = r - h * 6.2771141529083251953e-07
    q = r * r
    s = -2.505210838544172e-08
    for c in (2.7557319223985893e-06, -1.984126984126984e-04, 8.333333333333333e-03, -0.16666666666666666):
        s = s * q + c
    s = r + r * q * s
    sign = 1.0 - 2.0 * (k - 2.0 * jnp.floor(k * 0.5))
    return jnp.where(half > 0.25, -sign, sign) * s


def iota(shape, dim):
    return lax.broadcasted_iota(jnp.int32, shape, dim)


GROUP = 8
HALF = 8
BRIDGE = 3
WIDE = 24
EXT = 584
WIDTHS = (("p", 4), ("c", 3), ("d2", 2), ("d3", 1))
PLANES = [(f, k) for f, width in WIDTHS for k in range(width)]
RING_WIDTHS = (("p", 3), ("c", 2), ("d2", 1), ("v", 3))
RING_PLANES = [(f, k) for f, width in RING_WIDTHS for k in range(width)]
DIAGS = ((-1, -1), (-1, 1), (1, -1), (1, 1))
SIDES = ((-1, 0), (1, 0), (0, -1), (0, 1)) + DIAGS
CORNER = [("p", i, j) for i in range(3) for j in range(3 - i)] + [
    (f, i, j) for f in ("c", "v") for i in range(2) for j in range(2 - i)] + [("d2", 0, 0)]
RING_CORNER = [(f, i, j) for f in ("p", "v") for i in range(2) for j in range(2 - i)] + [("c", 0, 0)]
ALONG_Z = ("p", "c", "d2", "d3")
MAIN_GROUPS = [g for g in range(13, 60) if g % 3]


def row_of(x, y):
    return 8 + WIDE * (x + 4) + y


def roll_lanes(v, by):
    return pltpu.roll(v, by % TZ, 1) if by % TZ else v


def kernel(
    fields_h, tone_h, mfreq_h, mamp_h, mmap_h, spos_h, sid_h, sgain_h, cell_h, count_h, hist_h,
    fout_h, cout_h, heard_h, bt_h,
    tone_r, mfreq_r, mamp_r, mmap_r, spos_r, sid_r, sgain_r, cell_r, count_r,
    fv, hv, pm, pq, cm, cq, d2m, d2q, d3m, d3q, d4, vzm, vzq, vxs, vys, vxq, vyq, plast, sm, sq,
    ms, wv, srow, scol, acc, cone, zsel, both, ov, bt, sb, rb, hb,
    xs, xr, ys, yr, ds, dr, zs, zr, qs, qr, es, er, spare, zown,
    isem, fsem, hsem, osem, ss, rs, zss, zrs, qss, qrs, ass, ars, met, all_in,
):
    ix = lax.axis_index("gx")
    iy = lax.axis_index("gy")
    iz = lax.axis_index("gz")
    low_x, high_x = ix == 0, ix == 3
    low_y, high_y = iy == 0, iy == 3
    low_z, high_z = iz == 0, iz == OWN - 1

    def has(sx, sy):
        ok = None
        for s, low, high in ((sx, low_x, high_x), (sy, low_y, high_y)):
            if s:
                here = jnp.logical_not(low if s < 0 else high)
                ok = here if ok is None else ok & here
        return ok

    def at_side(sx, sy):
        where = {}
        if sx:
            where["gx"] = ix + sx
        if sy:
            where["gy"] = iy + sy
        return where

    barrier = pltpu.get_barrier_semaphore()
    half = (iz // HALF) * HALF
    bridge = (iz == BRIDGE) | (iz == BRIDGE + HALF)
    border = (iz == HALF - 1) | (iz == HALF)
    across = {"gz": lax.rem(iz + HALF, OWN)}
    mates = [{"gz": half + lax.rem(iz - half + k, HALF)} for k in range(1, HALF)]

    @pl.when(border)
    def _():
        pl.semaphore_signal(barrier, inc=1, device_id={"gz": OWN - 1 - iz}, device_id_type=MESH)

    @pl.when(bridge)
    def _():
        pl.semaphore_signal(barrier, inc=1, device_id=across, device_id_type=MESH)

    for mate in mates:
        pl.semaphore_signal(barrier, inc=1, device_id=mate, device_id_type=MESH)
    expected = HALF - 1 + jnp.where(border, 1, 0) + jnp.where(bridge, 1, 0)
    for side in SIDES:
        expected = expected + jnp.where(has(*side), 1, 0)

        @pl.when(has(*side))
        def _(side=side):
            pl.semaphore_signal(barrier, inc=1, device_id=at_side(*side), device_id_type=MESH)

    small = [
        pltpu.make_async_copy(src, dst, isem.at[k])
        for k, (src, dst) in enumerate((
            (mfreq_h, mfreq_r), (mamp_h, mamp_r), (mmap_h, mmap_r), (sid_h, sid_r), (sgain_h, sgain_r),
            (spos_h, spos_r), (tone_h, tone_r), (cell_h, cell_r), (count_h, count_r)))
    ]
    for copy in small:
        copy.start()
    loads = [pltpu.make_async_copy(fields_h.at[k], fv.at[k], fsem.at[k]) for k in range(4)]
    for copy in loads:
        copy.start()
    hist_load = pltpu.make_async_copy(hist_h, hv.at[pl.ds(0, HIST * OWN)], hsem)
    hist_load.start()

    lane = iota((1, TZ), 1)
    sub = iota((TY, 1), 0)
    row8 = iota((8, 1), 0)
    ext = {"p": pm.at[0], "c": cm, "v": vzm, "d2": d2m, "d3": d3m}
    ring = {"p": pq.at[0], "c": cq, "d2": d2q, "d3": d3q, "v": vzq}
    for ref in (vxs, vys, vxq, vyq, spare, sb):
        ref[...] = jnp.zeros_like(ref)

    ms[...] = jnp.zeros_like(ms)
    for copy in small:
        copy.wait()
    ms[0:1, 0:MODES] = mfreq_r[...]
    ms[1:2, 0:MODES] = mamp_r[...]
    ms[2:3, 0:MODES] = mmap_r[...].astype(F32)
    moment = (HIST + row8 % STEPS).astype(F32)
    waves = ms[1:2, :] * half_wave(ms[0:1, :] * moment, jnp.zeros((8, 1), F32))
    high = waves.astype(BF).astype(F32)
    waves = jnp.where(row8 < STEPS, high, waves - high).astype(BF)
    pick = jnp.where(iota((SOURCES, 1), 0).astype(F32) == ms[2:3, :], 1.0, 0.0).astype(BF)
    drive = dot_nt(waves, pick)
    drive = drive + pltpu.roll(drive, 4, 0)
    high = drive.astype(BF).astype(F32)
    drive = jnp.where(row8 < STEPS, high, drive - high).astype(BF)
    pick = jnp.where(iota((SOURCES, 1), 0) == sid_r[...], 1.0, 0.0).astype(BF)
    weight = dot_nn(drive, pick)
    weight = (weight + pltpu.roll(weight, 4, 0)) * sgain_r[...]
    high = weight.astype(BF).astype(F32)
    wv[...] = jnp.where(row8 < STEPS, high, weight - high)
    lx = spos_r[0:1, :] - ix * TX
    ly = spos_r[1:2, :] - iy * TY
    lz = spos_r[2:3, :] - iz * TZ
    inside = (lx >= 0) & (lx < TX) & (ly >= 0) & (ly < TY) & (lz >= 0) & (lz < TZ)
    srow[...] = jnp.where(inside, lx * TY + ly, -1).astype(F32)
    scol[...] = lz.astype(F32)

    def scattered(span):
        a = jnp.where(iota((ROWS, 1), 0).astype(F32).astype(BF) == srow[:, span].astype(BF), ONE, ZERO)
        m = iota((TZ, 1), 0).astype(F32).astype(BF) == scol[:, span].astype(BF)
        b = jnp.concatenate([jnp.where(m, wv[q:q + 1, span].astype(BF), ZERO) for q in range(2 * STEPS)], axis=0)
        return dot_nt(a, b)

    acc[...] = scattered(pl.ds(0, KC))

    @pl.loop(1, SRC // KC)
    def _(chunk):
        acc[...] += scattered(pl.ds(pl.multiple_of(chunk * KC, KC), KC))

    for copy in loads:
        copy.wait()
    for x in range(TX):
        at = slice(x * TY, (x + 1) * TY)
        to = slice(row_of(x, 0), row_of(x, 0) + TY)
        added = [acc[at, n * TZ:(n + 1) * TZ] + acc[at, (STEPS + n) * TZ:(STEPS + n + 1) * TZ] for n in range(STEPS)]
        p = fv[0, at, :]
        vx, vy, vz = (fv[k, at, :] for k in (1, 2, 3))
        gone = vx + (vy - jnp.where(sub == 0, 0.0, pltpu.roll(vy, 1, 0)))
        gone = gone + (vz - jnp.where(lane == 0, 0.0, pltpu.roll(vz, 1, 1)))
        if x:
            gone = gone - fv[1, (x - 1) * TY:x * TY, :]
        pm[0, to, :] = p
        cm[to, :] = added[0] - 0.5 * (gone + p)
        d2m[to, :] = added[1] - added[0]
        d3m[to, :] = added[2] - added[1]
        d4[at, :] = added[3] - added[2]
        vzm[to, :] = 0.5 * vz
    vxs[1, 4:20, :] = 0.5 * fv[1, ROWS - TY:ROWS, :]
    vys[1, 4:20, :] = 0.5 * fv[2, pl.ds(TY - 1, TX, stride=TY), :]

    def plane_at(along_x, q):
        return pl.ds(row_of(q, 0), TY) if along_x else pl.ds(row_of(0, q), TX, stride=WIDE)

    def inner(s):
        return (lambda k: k) if s == 0 else (lambda k: TX - 1 - k)

    def outer(s):
        return (lambda k: TX + k) if s == 0 else (lambda k: -1 - k)

    def up(step):
        return 0 if step < 0 else 1

    for face in range(4):
        along_x, s = face < 2, face % 2
        cell = inner(s)
        to = (xs if along_x else ys).at[s]
        for i, (f, k) in enumerate(PLANES):
            to[i * 16:(i + 1) * 16, :] = ext[f][plane_at(along_x, cell(k)), :]
        ends = jnp.zeros((TY, TZ), F32)
        for k in range(3):
            ends = jnp.where(lane == k, pltpu.roll(vzm[plane_at(along_x, cell(k)), :], k + 1, 1), ends)
        to[160:176, :] = ends
        beside, through = (vys, vxs) if along_x else (vxs, vys)
        for k in range(3):
            to[176 + k:177 + k, :] = beside[1, 4 + cell(k):5 + cell(k), :]
        if s == 1:
            to[192:208, :] = through[1, 4:20, :]
    for s, (sx, sy) in enumerate(DIAGS):
        cx, cy = inner(up(sx)), inner(up(sy))
        for i, (f, a, b) in enumerate(CORNER):
            r = row_of(cx(a), cy(b))
            ds[s, i:i + 1, :] = ext[f][r:r + 1, :]
        for k in range(3):
            ds[s, 13 + k:14 + k, :] = vxs[1, 4 + cy(k):5 + cy(k), :]
            ds[s, 16 + k:17 + k, :] = vys[1, 4 + cx(k):5 + cx(k), :]

    def slot(u):
        return ((lane + 4) % TZ) // 8 == u

    packs = {}
    for f in ALONG_Z:
        packs[f] = []
        for odd in (0, 1):
            packed = jnp.zeros((GROUP, TZ), F32)
            for u in range(16):
                g = MAIN_GROUPS[2 * u + odd]
                value = ext[f][g * 8:g * 8 + 8, :]
                if f == "c":
                    value = jnp.where(lane == TZ - 4, roll_lanes(vzm[g * 8:g * 8 + 8, :], -3), value)
                packed = jnp.where(slot(u), roll_lanes(value, 8 * u), packed)
            packs[f].append(packed)
    packed = jnp.zeros((GROUP, TZ), F32)
    for u in range(4):
        value = (vxs, vys)[u // 2][1, 4 + 8 * (u % 2):12 + 8 * (u % 2), :]
        packed = jnp.where(slot(u), roll_lanes(value, 8 * u), packed)
    lower = lane % 8 < 4
    for i, f in enumerate(ALONG_Z):
        one, two = packs[f]
        zs[0, i] = jnp.where(lower, one, roll_lanes(two, 4))
        zs[1, i] = jnp.where(lower, roll_lanes(one, 4), roll_lanes(two, 8))
        zown[2 * i] = one
        zown[2 * i + 1] = two
    zs[0, 4] = packed
    zs[1, 4] = packed
    zown[8] = packed

    def copies(sems, buffers):
        return [
            pltpu.make_async_remote_copy(
                src_ref=src, dst_ref=dst, send_sem=sems[0].at[i], recv_sem=sems[1].at[i],
                device_id=at_side(*side), device_id_type=MESH)
            for i, (side, (src, dst)) in enumerate(zip(SIDES, buffers))
        ]

    firsts = copies((ss, rs), [
        (a.at[s, pl.ds(0, 192 + 16 * s)], b.at[s, pl.ds(0, 192 + 16 * s)]) for a, b in ((xs, xr), (ys, yr)) for s in (0, 1)
    ] + [(ds.at[s], dr.at[s]) for s in range(4)])
    to_z = [
        pltpu.make_async_remote_copy(
            src_ref=zs.at[s], dst_ref=zr.at[s], send_sem=zss.at[s], recv_sem=zrs.at[s],
            device_id={"gz": iz + (2 * s - 1)}, device_id_type=MESH)
        for s in (0, 1)
    ]
    from_z = (jnp.logical_not(high_z), jnp.logical_not(low_z))
    pl.semaphore_wait(barrier, expected)

    @pl.when(bridge)
    def _():
        pl.semaphore_signal(met, inc=1, device_id=across, device_id_type=MESH)

    for s in (0, 1):
        @pl.when(from_z[1 - s])
        def _(s=s):
            to_z[s].start()
    for side, copy in zip(SIDES, firsts):
        @pl.when(has(*side))
        def _(copy=copy):
            copy.start()

    for d in range(OWN):
        cells = cell_r[d:d + 1, :]
        span = slice(d * CAP, (d + 1) * CAP)
        one = jnp.where(iota((ROWS, 1), 0) == cells // TZ, 1.0, 0.0).astype(BF)
        cone[0:ROWS, span] = one
        cone[ROWS:2 * ROWS, span] = one
        zsel[:, span] = jnp.where(iota((TZ, 1), 0) == cells % TZ, 1.0, 0.0).astype(F32)

    eye = iota((TONES, TONES), 0) == iota((TONES, TONES), 1)
    freq = jnp.sum(jnp.where(eye, tone_r[...], 0.0), axis=1, keepdims=True)
    freq = jnp.concatenate([freq, freq], axis=0)
    angle = freq * lane.astype(F32)
    basis = half_wave(angle, jnp.where(iota((NB, 1), 0) < TONES, 0.5, 0.0).astype(F32)) * 0.125
    for n in range(STEPS):
        bt[n * NB:(n + 1) * NB, :] = jnp.broadcast_to(basis[:, HIST + n:HIST + n + 1], (NB, CAP))
    held = iota((OWN, OWN), 0) == iota((OWN, OWN), 1)
    counts = jnp.sum(jnp.where(held, count_r[...].astype(F32), 0.0), axis=1, keepdims=True)
    live = jnp.where(lane.astype(F32) < counts, 1.0, 0.0).astype(F32)
    bt_out = pltpu.make_async_copy(bt, bt_h, osem.at[3])
    bt_out.start()

    @pl.when(bridge)
    def _():
        pl.semaphore_wait(met, 1)
        for mate in mates:
            pl.semaphore_signal(all_in, inc=1, device_id=mate, device_id_type=MESH)

    for i in range(4):
        sx, sy = SIDES[i]

        @pl.when(has(-sx, -sy))
        def _(i=i):
            along_x, s = i < 2, i % 2
            out = outer(s)
            firsts[i].wait_recv()
            got = (xr if along_x else yr).at[s]
            for j, (f, k) in enumerate(PLANES):
                ext[f][plane_at(along_x, out(k)), :] = got[j * 16:(j + 1) * 16, :]
            beside, through = (vys, vxs) if along_x else (vxs, vys)
            ends = got[160:176, :]
            for k in range(3):
                vzm[plane_at(along_x, out(k)), :] = pltpu.roll(ends, TZ - 1 - k, 1)
                beside[1, 4 + out(k):5 + out(k), :] = got[176 + k:177 + k, :]
            if s == 1:
                through[0, 4:20, :] = got[192:208, :]

    for i in range(4, 8):
        sx, sy = SIDES[i]

        @pl.when(has(-sx, -sy))
        def _(i=i, sx=sx, sy=sy):
            ox, oy = outer(up(sx)), outer(up(sy))
            firsts[i].wait_recv()
            for j, (f, a, b) in enumerate(CORNER):
                r = row_of(ox(a), oy(b))
                ext[f][r:r + 1, :] = dr[i - 4, j:j + 1, :]
            for k in range(3):
                if sx > 0:
                    vxs[0, 4 + oy(k):5 + oy(k), :] = dr[i - 4, 13 + k:14 + k, :]
                if sy > 0:
                    vys[0, 4 + ox(k):5 + ox(k), :] = dr[i - 4, 16 + k:17 + k, :]

    def borders(change, vx, vy):
        for k, x in ((0, 0), (1, TX)):
            r = row_of(x, -4)
            change[r:r + WIDE, :] = change[r:r + WIDE, :] + vx[k]
        for k, y in ((0, 0), (1, TY)):
            r = pl.ds(row_of(-4, y), WIDE, stride=WIDE)
            change[r, :] = change[r, :] + vy[k]

    def mirrors(refs, widths):
        for flag, low, along_x in (
            (low_x, True, True), (high_x, False, True), (low_y, True, False), (high_y, False, False)
        ):
            @pl.when(flag)
            def _(low=low, along_x=along_x):
                def rows(q):
                    return pl.ds(row_of(q, -4), WIDE) if along_x else pl.ds(row_of(-4, q), WIDE, stride=WIDE)

                for f, width in widths:
                    for k in range(width):
                        if low:
                            refs[f][rows(-1 - k), :] = refs[f][rows(k), :]
                        elif k == 0:
                            refs[f][rows(TX), :] = jnp.zeros((WIDE, TZ), F32)
                        else:
                            refs[f][rows(TX + k), :] = -refs[f][rows(TX - k), :]

    borders(cm, vxs, vys)
    mirrors(ext, WIDTHS + (("v", 3),))

    for s in (0, 1):
        @pl.when(from_z[s])
        def _(s=s):
            to_z[s].wait_recv()

    place = (lane + 4) % 8

    def joined(own, from_low, from_high, skip):
        below = jnp.zeros((GROUP, TZ), F32)
        above = jnp.zeros((GROUP, TZ), F32)
        for k in range(4):
            if not (skip and k == 3):
                below = jnp.where(place == 3 - k, roll_lanes(own, -(2 * k + 1)), below)
            if k:
                above = jnp.where(place == 4 + k, -roll_lanes(own, 2 * k), above)
        return jnp.where(
            place < 4, jnp.where(low_z, below, from_low), jnp.where(high_z, above, from_high))

    for i, f in enumerate(ALONG_Z):
        lows, highs = zr[1, i], zr[0, i]
        for odd in (0, 1):
            merged = joined(
                zown[2 * i + odd], roll_lanes(lows, -4 - 4 * odd), roll_lanes(highs, -4 * odd), f == "c")
            for u in range(16):
                g = MAIN_GROUPS[2 * u + odd]
                value = roll_lanes(merged, -8 * u)
                ring[f][g * 8:g * 8 + 8, :] = value
                if f == "c":
                    vzq[g * 8:g * 8 + 8, :] = roll_lanes(value, 3)
    merged = joined(zown[8], zr[1, 4], zr[0, 4], False)
    for u in range(4):
        (vxq, vyq)[u // 2][1, 4 + 8 * (u % 2):12 + 8 * (u % 2), :] = roll_lanes(merged, -8 * u)

    for face in range(4):
        along_x, s = face < 2, face % 2
        cell = inner(s)
        beside, through = (vyq, vxq) if along_x else (vxq, vyq)
        for k in range(3):
            spare[face, k:k + 1, :] = beside[1, 4 + cell(k):5 + cell(k), :]
        planes = [ring[f][plane_at(along_x, cell(k)), :] for f, k in RING_PLANES] + [spare[face]]
        if s == 1:
            planes.append(through[1, 4:20, :])
        packed = jnp.zeros((TY, TZ), F32)
        for u, value in enumerate(planes):
            packed = jnp.where(slot(u), roll_lanes(value, 8 * u), packed)
        qs[face] = packed
    for s, (sx, sy) in enumerate(DIAGS):
        cx, cy = inner(up(sx)), inner(up(sy))
        for i, (f, a, b) in enumerate(RING_CORNER):
            r = row_of(cx(a), cy(b))
            es[s, i:i + 1, :] = ring[f][r:r + 1, :]
        for k in range(2):
            es[s, 8 + k:9 + k, :] = vxq[1, 4 + cy(k):5 + cy(k), :]
            es[s, 10 + k:11 + k, :] = vyq[1, 4 + cx(k):5 + cx(k), :]
    seconds = copies((qss, qrs), [(qs.at[s], qr.at[s]) for s in range(4)] + [(es.at[s], er.at[s]) for s in range(4)])
    for side, copy in zip(SIDES, seconds):
        @pl.when(has(*side))
        def _(copy=copy):
            copy.start()

    for i in range(4):
        sx, sy = SIDES[i]

        @pl.when(has(-sx, -sy))
        def _(i=i):
            along_x, s = i < 2, i % 2
            out = outer(s)
            seconds[i].wait_recv()
            got = qr[i]
            for u, (f, k) in enumerate(RING_PLANES):
                ring[f][plane_at(along_x, out(k)), :] = roll_lanes(got, -8 * u)
            beside, through = (vyq, vxq) if along_x else (vxq, vyq)
            last = len(RING_PLANES)
            side_rows = roll_lanes(got, -8 * last)
            for k in range(3):
                beside[1, 4 + out(k):5 + out(k), :] = side_rows[k:k + 1, :]
            if s == 1:
                through[0, 4:20, :] = roll_lanes(got, -8 * (last + 1))

    for i in range(4, 8):
        sx, sy = SIDES[i]

        @pl.when(has(-sx, -sy))
        def _(i=i, sx=sx, sy=sy):
            ox, oy = outer(up(sx)), outer(up(sy))
            seconds[i].wait_recv()
            for j, (f, a, b) in enumerate(RING_CORNER):
                r = row_of(ox(a), oy(b))
                ring[f][r:r + 1, :] = er[i - 4, j:j + 1, :]
            for k in range(2):
                if sx > 0:
                    vxq[0, 4 + oy(k):5 + oy(k), :] = er[i - 4, 8 + k:9 + k, :]
                if sy > 0:
                    vyq[0, 4 + ox(k):5 + ox(k), :] = er[i - 4, 10 + k:11 + k, :]

    borders(cq, vxq, vyq)
    mirrors(ring, RING_WIDTHS)

    for g in range(4, 69):
        at = slice(g * 8, g * 8 + 8)
        cm[at, :] = cm[at, :] + roll_lanes(jnp.where(lane == TZ - 1, vzq[at, :], 0.0), 1)
        if 7 <= g < 66:
            flow = roll_lanes(jnp.where(lane == TZ - 1, vzm[at, :], 0.0), 1)
            cq[at, :] = cq[at, :] + jnp.where(high_z, 0.0, flow)

    for n in range(STEPS):
        d_main = (cm, d2m, d3m, d4)[n]
        d_ring = (cq, d2q, d3q, None)[n]
        main_span = (range(4, 69), range(7, 66), range(10, 63), [g for g in range(13, 60) if g % 3])[n]
        ring_span = (range(7, 66), range(10, 63), range(13, 60), ())[n]
        for g in main_span:
            at = slice(g * 8, g * 8 + 8)
            here, ghost = pm[n, at, :], pq[n, at, :]

            def stepped(ref, d, here, other):
                sums = (ref[n, g * 8 - WIDE:g * 8 - WIDE + 8, :] + ref[n, g * 8 + WIDE:g * 8 + WIDE + 8, :]) + (
                    ref[n, g * 8 - 1:g * 8 + 7, :] + ref[n, g * 8 + 1:g * 8 + 9, :])
                back = pltpu.roll(jnp.where(lane == TZ - 1, other, here), 1, 1)
                fore = pltpu.roll(jnp.where(lane == 0, other, here), TZ - 1, 1)
                new = d + 0.25 * (sums + (back + fore))
                return new if n == 0 else new + (0.5 * here - ref[n - 1, at, :])

            if n < STEPS - 1:
                pm[n + 1, at, :] = stepped(pm, d_main[at, :], here, ghost)
                if g in ring_span:
                    pq[n + 1, at, :] = stepped(pq, d_ring[at, :], ghost, here)
            else:
                x, half = divmod(g - 13, 3)
                own = slice(x * TY + half * 8, x * TY + half * 8 + 8)
                plast[own, :] = stepped(pm, d4[own, :], here, ghost)
        new = plast[...] if n == STEPS - 1 else jnp.concatenate(
            [pm[n + 1, row_of(x, 0):row_of(x, 0) + TY, :] for x in range(TX)], axis=0)
        both[n * TZ:(n + 1) * TZ, :] = jnp.concatenate(split(new.T), axis=1)

    for d in range(0, OWN, 2):
        span = slice(d * CAP, (d + 2) * CAP)
        seen = dot_nn(both[...], cone[:, span])
        for n in range(STEPS):
            got = jnp.sum(seen[n * TZ:(n + 1) * TZ, :] * zsel[:, span], axis=0, keepdims=True)
            sb[d * 8 + n:d * 8 + n + 1, :] = got[:, :CAP]
            sb[(d + 1) * 8 + n:(d + 1) * 8 + n + 1, :] = got[:, CAP:]

    def block_copy(k):
        target = lax.rem(iz + k, OWN)
        return pltpu.make_async_remote_copy(
            src_ref=sb.at[pl.ds(pl.multiple_of(target * 8, 8), 8)],
            dst_ref=rb.at[pl.ds(pl.multiple_of(iz * 8, 8), 8)],
            send_sem=ass.at[k], recv_sem=ars.at[k], device_id={"gz": target}, device_id_type=MESH)

    @pl.when(jnp.logical_not(bridge))
    def _():
        pl.semaphore_wait(all_in, 1)

    sends = [block_copy(k) for k in range(1, OWN)]
    for k in (8, 7, 9, 6, 10, 5, 11, 4, 12, 3, 13, 2, 14, 1, 15):
        sends[k - 1].start()
    mine = pl.ds(pl.multiple_of(iz * 8, 8), 8)
    rb[mine, :] = sb[mine, :]

    outs = [pltpu.make_async_copy(plast, fout_h.at[0], osem.at[0])]
    outs[0].start()
    for side, one, two in zip(SIDES, firsts, seconds):
        @pl.when(has(*side))
        def _(one=one, two=two):
            one.wait_send()
            two.wait_send()
    for s in (0, 1):
        @pl.when(from_z[1 - s])
        def _(s=s):
            to_z[s].wait_send()
    for g in range(13, 64):
        at = slice(g * 8, g * 8 + 8)
        sm[at, :] = (pm[0, at, :] + pm[1, at, :]) + (pm[2, at, :] + pm[3, at, :])
        sq[at, :] = (pq[0, at, :] + pq[1, at, :]) + (pq[2, at, :] + pq[3, at, :])
    for x in range(TX):
        at = slice(x * TY, (x + 1) * TY)
        r = row_of(x, 0)
        own = sm[r:r + TY, :]
        fv[1, at, :] = fv[1, at, :] - 0.5 * (sm[r + WIDE:r + WIDE + TY, :] - own)
        fv[2, at, :] = fv[2, at, :] - 0.5 * (sm[r + 1:r + 1 + TY, :] - own)
        fore = pltpu.roll(jnp.where(lane == 0, sq[r:r + TY, :], own), TZ - 1, 1)
        fv[3, at, :] = fv[3, at, :] - 0.5 * (fore - own)
    outs.append(pltpu.make_async_copy(fv.at[pl.ds(1, 3)], fout_h.at[pl.ds(1, 3)], osem.at[1]))
    outs[1].start()

    hist_load.wait()
    hv[HIST * OWN:, :] = jnp.zeros((STEPS * OWN, CAP), F32)
    bh, bl = split(basis)
    lhs = jnp.concatenate([bh, bl, bh], axis=1)
    for e in range(0, OWN, 2):
        hh, hl = split(jnp.concatenate(
            [hv[pl.ds(e, HIST + STEPS, stride=OWN), :], hv[pl.ds(e + 1, HIST + STEPS, stride=OWN), :]], axis=1))
        part = dot_nn(lhs, jnp.concatenate([hh, hh, hl], axis=0))
        ov[pl.ds(e, NB, stride=OWN), :] = part[:, :CAP] * live[e:e + 1]
        ov[pl.ds(e + 1, NB, stride=OWN), :] = part[:, CAP:] * live[e + 1:e + 2]
    ov_out = pltpu.make_async_copy(ov, cout_h, osem.at[2])
    ov_out.start()

    for copy in sends:
        copy.wait_recv()
    for n in range(STEPS):
        hb[n * OWN:(n + 1) * OWN, :] = rb[pl.ds(n, OWN, stride=8), :] * live
    outs.append(pltpu.make_async_copy(hb, heard_h, osem.at[4]))
    outs[-1].start()
    for copy in sends:
        copy.wait_send()
    for copy in outs + [bt_out, ov_out]:
        copy.wait()


PARTS = 4
PER = NB // PARTS


def finish(fields_h, part_h, heard_h, bt_h, fout_h, cout_h, fv, ov, hb, bt, sems, fsems):
    pieces = [pl.ds(k * PER * OWN, PER * OWN) for k in range(PARTS)]
    first = [pltpu.make_async_copy(heard_h, hb, sems.at[0]), pltpu.make_async_copy(bt_h, bt, sems.at[1])]
    loads = [pltpu.make_async_copy(part_h.at[r], ov.at[r], sems.at[2 + k]) for k, r in enumerate(pieces)]
    stores = [pltpu.make_async_copy(ov.at[r], cout_h.at[r], sems.at[2 + PARTS + k]) for k, r in enumerate(pieces)]
    gets = [pltpu.make_async_copy(fields_h.at[k], fv.at[k], fsems.at[k]) for k in range(4)]
    puts = [pltpu.make_async_copy(fv.at[k], fout_h.at[k], fsems.at[4 + k]) for k in range(4)]
    for copy in first + loads + gets:
        copy.start()
    for copy in first:
        copy.wait()
    heard = [hb[n * OWN:(n + 1) * OWN, :] for n in range(STEPS)]
    for k in range(PARTS):
        loads[k].wait()
        for j in range(k * PER, (k + 1) * PER):
            at = slice(j * OWN, (j + 1) * OWN)
            term = ov[at, :]
            for n in range(STEPS):
                term = term + bt[n * NB + j:n * NB + j + 1, :] * heard[n]
            ov[at, :] = term
        stores[k].start()
        gets[k].wait()
        puts[k].start()
    for copy in stores + puts:
        copy.wait()


def body(
    fields, tone_freq, mode_freq, mode_amp, mode_map, src_pos, src_id, src_gain, sample_cell, sample_count, history
):
    hbm = pl.BlockSpec(memory_space=pl.ANY)
    made = pl.pallas_call(
        kernel,
        out_shape=(
            jax.ShapeDtypeStruct((4, ROWS, TZ), F32),
            jax.ShapeDtypeStruct((NB * OWN, CAP), F32),
            jax.ShapeDtypeStruct((STEPS * OWN, CAP), F32),
            jax.ShapeDtypeStruct((STEPS * NB, CAP), F32),
        ),
        in_specs=[hbm] * 11,
        out_specs=(hbm,) * 4,
        scratch_shapes=[
            pltpu.VMEM((1, TONES), F32),
            pltpu.VMEM((1, MODES), F32),
            pltpu.VMEM((1, MODES), F32),
            pltpu.VMEM((1, MODES), jnp.int32),
            pltpu.VMEM((3, SRC), jnp.int32),
            pltpu.VMEM((1, SRC), jnp.int32),
            pltpu.VMEM((1, SRC), F32),
            pltpu.VMEM((OWN, CAP), jnp.int32),
            pltpu.VMEM((1, OWN), jnp.int32),
            pltpu.VMEM((4, ROWS, TZ), F32),
            pltpu.VMEM(((HIST + STEPS) * OWN, CAP), F32),
            pltpu.VMEM((STEPS, EXT, TZ), F32),
            pltpu.VMEM((STEPS, EXT, TZ), F32),
            pltpu.VMEM((EXT, TZ), F32),
            pltpu.VMEM((EXT, TZ), F32),
            pltpu.VMEM((EXT, TZ), F32),
            pltpu.VMEM((EXT, TZ), F32),
            pltpu.VMEM((EXT, TZ), F32),
            pltpu.VMEM((EXT, TZ), F32),
            pltpu.VMEM((ROWS, TZ), F32),
            pltpu.VMEM((EXT, TZ), F32),
            pltpu.VMEM((EXT, TZ), F32),
            pltpu.VMEM((2, WIDE, TZ), F32),
            pltpu.VMEM((2, WIDE, TZ), F32),
            pltpu.VMEM((2, WIDE, TZ), F32),
            pltpu.VMEM((2, WIDE, TZ), F32),
            pltpu.VMEM((ROWS, TZ), F32),
            pltpu.VMEM((EXT, TZ), F32),
            pltpu.VMEM((EXT, TZ), F32),
            pltpu.VMEM((8, 2048), F32),
            pltpu.VMEM((8, SRC), F32),
            pltpu.VMEM((1, SRC), F32),
            pltpu.VMEM((1, SRC), F32),
            pltpu.VMEM((ROWS, 2 * STEPS * TZ), F32),
            pltpu.VMEM((2 * ROWS, SLOTS), BF),
            pltpu.VMEM((TZ, SLOTS), F32),
            pltpu.VMEM((STEPS * TZ, 2 * ROWS), BF),
            pltpu.VMEM((NB * OWN, CAP), F32),
            pltpu.VMEM((STEPS * NB, CAP), F32),
            pltpu.VMEM((OWN * 8, CAP), F32),
            pltpu.VMEM((OWN * 8, CAP), F32),
            pltpu.VMEM((STEPS * OWN, CAP), F32),
            pltpu.VMEM((2, 208, TZ), F32),
            pltpu.VMEM((2, 208, TZ), F32),
            pltpu.VMEM((2, 208, TZ), F32),
            pltpu.VMEM((2, 208, TZ), F32),
            pltpu.VMEM((4, 24, TZ), F32),
            pltpu.VMEM((4, 24, TZ), F32),
            pltpu.VMEM((2, 5, GROUP, TZ), F32),
            pltpu.VMEM((2, 5, GROUP, TZ), F32),
            pltpu.VMEM((4, TY, TZ), F32),
            pltpu.VMEM((4, TY, TZ), F32),
            pltpu.VMEM((4, TY, TZ), F32),
            pltpu.VMEM((4, TY, TZ), F32),
            pltpu.VMEM((4, TY, TZ), F32),
            pltpu.VMEM((9, GROUP, TZ), F32),
            pltpu.SemaphoreType.DMA((9,)),
            pltpu.SemaphoreType.DMA((4,)),
            pltpu.SemaphoreType.DMA,
            pltpu.SemaphoreType.DMA((5,)),
            pltpu.SemaphoreType.DMA((8,)),
            pltpu.SemaphoreType.DMA((8,)),
            pltpu.SemaphoreType.DMA((2,)),
            pltpu.SemaphoreType.DMA((2,)),
            pltpu.SemaphoreType.DMA((8,)),
            pltpu.SemaphoreType.DMA((8,)),
            pltpu.SemaphoreType.DMA((OWN,)),
            pltpu.SemaphoreType.DMA((OWN,)),
            pltpu.SemaphoreType.REGULAR,
            pltpu.SemaphoreType.REGULAR,
        ],
        compiler_params=pltpu.CompilerParams(
            collective_id=0, has_side_effects=True, vmem_limit_bytes=63 * 1024 * 1024
        ),
    )(
        fields.reshape(4, ROWS, TZ),
        tone_freq.reshape(1, TONES),
        mode_freq.reshape(1, MODES),
        mode_amp.reshape(1, MODES),
        mode_map.reshape(1, MODES),
        src_pos,
        src_id.reshape(1, SRC),
        src_gain.reshape(1, SRC),
        sample_cell.reshape(OWN, CAP),
        sample_count.reshape(1, OWN),
        history.reshape(HIST * OWN, CAP),
    )
    fields_out, coefficients = pl.pallas_call(
        finish,
        out_shape=(
            jax.ShapeDtypeStruct((4, ROWS, TZ), F32),
            jax.ShapeDtypeStruct((NB * OWN, CAP), F32),
        ),
        in_specs=[hbm] * 4,
        out_specs=(hbm,) * 2,
        scratch_shapes=[
            pltpu.VMEM((4, ROWS, TZ), F32),
            pltpu.VMEM((NB * OWN, CAP), F32),
            pltpu.VMEM((STEPS * OWN, CAP), F32),
            pltpu.VMEM((STEPS * NB, CAP), F32),
            pltpu.SemaphoreType.DMA((2 + 2 * PARTS,)),
            pltpu.SemaphoreType.DMA((8,)),
        ],
        compiler_params=pltpu.CompilerParams(vmem_limit_bytes=63 * 1024 * 1024),
    )(*made)
    return fields_out.reshape(fields.shape), coefficients.reshape(NB, 1, 1, 1, OWN, CAP)


def solution(mesh):
    in_specs = (
        P(None, "gx", "gy", "gz"),
        P(),
        P(),
        P(),
        P(),
        P(),
        P(),
        P(),
        P("gx", "gy", "gz", None, None),
        P("gx", "gy", None, "gz"),
        P(None, "gx", "gy", "gz", None, None),
    )
    out_specs = (P(None, "gx", "gy", "gz"), P(None, "gx", "gy", "gz", None, None))
    return jax.shard_map(body, mesh=mesh, in_specs=in_specs, out_specs=out_specs, check_vma=False)
```

```python
import jax
import jax.numpy as jnp
import numpy as np
from jax import lax
from jax.experimental import pallas as pl
from jax.experimental.pallas import tpu as pltpu
from jax.sharding import PartitionSpec as P

STEPS = 4
HIST = 124
SOURCES = 48
TONES = 48
MODES = 2000
SRC = 4096
TX, TY, TZ = 16, 16, 128
ROWS = TX * TY
OWN = 16
CAP = 128
SLOTS = OWN * CAP
NB = 2 * TONES
KC = 1024
F32 = jnp.float32
BF = jnp.bfloat16
MESH = pl.DeviceIdType.MESH
ONE = np.asarray(1, BF)
ZERO = np.asarray(0, BF)


def split(values):
    high = values.astype(BF)
    return high, (values - high.astype(F32)).astype(BF)


def dot_nn(a, b):
    return lax.dot_general(a, b, (((1,), (0,)), ((), ())), preferred_element_type=F32)


def dot_nt(a, b):
    return lax.dot_general(a, b, (((1,), (1,)), ((), ())), preferred_element_type=F32)


def half_wave(x, half):
    k = jnp.floor(x * 0.3183098861837907 + (0.5 - half))
    h = k + half
    r = x - h * 3.140625
    r = r - h * 0.0009670257568359375
    r = r - h * 6.2771141529083251953e-07
    q = r * r
    s = -2.505210838544172e-08
    for c in (2.7557319223985893e-06, -1.984126984126984e-04, 8.333333333333333e-03, -0.16666666666666666):
        s = s * q + c
    s = r + r * q * s
    sign = 1.0 - 2.0 * (k - 2.0 * jnp.floor(k * 0.5))
    return jnp.where(half > 0.25, -sign, sign) * s


def iota(shape, dim):
    return lax.broadcasted_iota(jnp.int32, shape, dim)


GROUP = 8
HALF = 8
BRIDGE = 3
WIDE = 24
EXT = 584
WIDTHS = (("p", 4), ("c", 3), ("d2", 2), ("d3", 1))
LATER = [(f, k) for f, width in WIDTHS[1:] for k in range(width)]
RING_WIDTHS = (("p", 3), ("c", 2), ("d2", 1), ("v", 3))
RING_PLANES = [(f, k) for f, width in RING_WIDTHS for k in range(width)]
DIAGS = ((-1, -1), (-1, 1), (1, -1), (1, 1))
SIDES = ((-1, 0), (1, 0), (0, -1), (0, 1)) + DIAGS
CORNER = [("p", i, j) for i in range(3) for j in range(3 - i)] + [("v", i, j) for i in range(2) for j in range(2 - i)]
LATER_CORNER = [("c", i, j) for i in range(2) for j in range(2 - i)] + [("d2", 0, 0)]
RING_CORNER = [(f, i, j) for f in ("p", "v") for i in range(2) for j in range(2 - i)] + [("c", 0, 0)]
ALONG_Z = ("p", "c", "d2", "d3")
Z_SLOT = {"p": 0, "c": 2, "d2": 3, "d3": 4}
MAIN_GROUPS = [g for g in range(13, 60) if g % 3]


def row_of(x, y):
    return 8 + WIDE * (x + 4) + y


def roll_lanes(v, by):
    return pltpu.roll(v, by % TZ, 1) if by % TZ else v


def kernel(
    fields_h, tone_h, mfreq_h, mamp_h, mmap_h, spos_h, sid_h, sgain_h, cell_h, count_h, hist_h,
    fout_h, cout_h, heard_h, bt_h,
    tone_r, mfreq_r, mamp_r, mmap_r, spos_r, sid_r, sgain_r, cell_r, count_r,
    fv, hv, pm, pq, cm, cq, d2m, d2q, d3m, d3q, d4, vzm, vzq, vxs, vys, vxq, vyq, plast, sm, sq,
    ms, wv, srow, scol, acc, cone, zsel, both, ov, bt, sb, rb, hb,
    xs, xr, ys, yr, ds, dr, zs, zr, qs, qr, es, er, spare, zown,
    isem, fsem, hsem, osem, ss, rs, zss, zrs, qss, qrs, ass, ars, met, all_in,
):
    ix = lax.axis_index("gx")
    iy = lax.axis_index("gy")
    iz = lax.axis_index("gz")
    low_x, high_x = ix == 0, ix == 3
    low_y, high_y = iy == 0, iy == 3
    low_z, high_z = iz == 0, iz == OWN - 1

    def has(sx, sy):
        ok = None
        for s, low, high in ((sx, low_x, high_x), (sy, low_y, high_y)):
            if s:
                here = jnp.logical_not(low if s < 0 else high)
                ok = here if ok is None else ok & here
        return ok

    def at_side(sx, sy):
        where = {}
        if sx:
            where["gx"] = ix + sx
        if sy:
            where["gy"] = iy + sy
        return where

    barrier = pltpu.get_barrier_semaphore()
    half = (iz // HALF) * HALF
    bridge = (iz == BRIDGE) | (iz == BRIDGE + HALF)
    border = (iz == HALF - 1) | (iz == HALF)
    across = {"gz": lax.rem(iz + HALF, OWN)}
    mates = [{"gz": half + lax.rem(iz - half + k, HALF)} for k in range(1, HALF)]

    @pl.when(border)
    def _():
        pl.semaphore_signal(barrier, inc=1, device_id={"gz": OWN - 1 - iz}, device_id_type=MESH)

    @pl.when(bridge)
    def _():
        pl.semaphore_signal(barrier, inc=1, device_id=across, device_id_type=MESH)

    for mate in mates:
        pl.semaphore_signal(barrier, inc=1, device_id=mate, device_id_type=MESH)
    expected = HALF - 1 + jnp.where(border, 1, 0) + jnp.where(bridge, 1, 0)
    for side in SIDES:
        expected = expected + jnp.where(has(*side), 1, 0)

        @pl.when(has(*side))
        def _(side=side):
            pl.semaphore_signal(barrier, inc=1, device_id=at_side(*side), device_id_type=MESH)

    small = [
        pltpu.make_async_copy(src, dst, isem.at[k])
        for k, (src, dst) in enumerate((
            (mfreq_h, mfreq_r), (mamp_h, mamp_r), (mmap_h, mmap_r), (sid_h, sid_r), (sgain_h, sgain_r),
            (spos_h, spos_r), (tone_h, tone_r), (cell_h, cell_r), (count_h, count_r)))
    ]
    for copy in small:
        copy.start()
    loads = [pltpu.make_async_copy(fields_h.at[k], fv.at[k], fsem.at[k]) for k in range(4)]
    for copy in loads:
        copy.start()
    hist_load = pltpu.make_async_copy(hist_h, hv.at[pl.ds(0, HIST * OWN)], hsem)
    hist_load.start()

    lane = iota((1, TZ), 1)
    sub = iota((TY, 1), 0)
    row8 = iota((8, 1), 0)
    ext = {"p": pm.at[0], "c": cm, "v": vzm, "d2": d2m, "d3": d3m}
    ring = {"p": pq.at[0], "c": cq, "d2": d2q, "d3": d3q, "v": vzq}
    for ref in (vxs, vys, vxq, vyq, spare, sb):
        ref[...] = jnp.zeros_like(ref)

    ms[...] = jnp.zeros_like(ms)
    for copy in small:
        copy.wait()
    ms[0:1, 0:MODES] = mfreq_r[...]
    ms[1:2, 0:MODES] = mamp_r[...]
    ms[2:3, 0:MODES] = mmap_r[...].astype(F32)
    moment = (HIST + row8 % STEPS).astype(F32)
    waves = ms[1:2, :] * half_wave(ms[0:1, :] * moment, jnp.zeros((8, 1), F32))
    high = waves.astype(BF).astype(F32)
    waves = jnp.where(row8 < STEPS, high, waves - high).astype(BF)
    pick = jnp.where(iota((SOURCES, 1), 0).astype(F32) == ms[2:3, :], 1.0, 0.0).astype(BF)
    drive = dot_nt(waves, pick)
    drive = drive + pltpu.roll(drive, 4, 0)
    high = drive.astype(BF).astype(F32)
    drive = jnp.where(row8 < STEPS, high, drive - high).astype(BF)
    pick = jnp.where(iota((SOURCES, 1), 0) == sid_r[...], 1.0, 0.0).astype(BF)
    weight = dot_nn(drive, pick)
    weight = (weight + pltpu.roll(weight, 4, 0)) * sgain_r[...]
    high = weight.astype(BF).astype(F32)
    wv[...] = jnp.where(row8 < STEPS, high, weight - high)
    lx = spos_r[0:1, :] - ix * TX
    ly = spos_r[1:2, :] - iy * TY
    lz = spos_r[2:3, :] - iz * TZ
    inside = (lx >= 0) & (lx < TX) & (ly >= 0) & (ly < TY) & (lz >= 0) & (lz < TZ)
    srow[...] = jnp.where(inside, lx * TY + ly, -1).astype(F32)
    scol[...] = lz.astype(F32)

    def scattered(span):
        a = jnp.where(iota((ROWS, 1), 0).astype(F32).astype(BF) == srow[:, span].astype(BF), ONE, ZERO)
        m = iota((TZ, 1), 0).astype(F32).astype(BF) == scol[:, span].astype(BF)
        b = jnp.concatenate([jnp.where(m, wv[q:q + 1, span].astype(BF), ZERO) for q in range(2 * STEPS)], axis=0)
        return dot_nt(b, a)

    acc[...] = scattered(pl.ds(0, KC))

    for copy in loads:
        copy.wait()
    for x in range(TX):
        at = slice(x * TY, (x + 1) * TY)
        to = slice(row_of(x, 0), row_of(x, 0) + TY)
        pm[0, to, :] = fv[0, at, :]
        vzm[to, :] = 0.5 * fv[3, at, :]
    vxs[1, 4:20, :] = 0.5 * fv[1, ROWS - TY:ROWS, :]
    vys[1, 4:20, :] = 0.5 * fv[2, pl.ds(TY - 1, TX, stride=TY), :]

    def plane_at(along_x, q):
        return pl.ds(row_of(q, 0), TY) if along_x else pl.ds(row_of(0, q), TX, stride=WIDE)

    def inner(s):
        return (lambda k: k) if s == 0 else (lambda k: TX - 1 - k)

    def outer(s):
        return (lambda k: TX + k) if s == 0 else (lambda k: -1 - k)

    def up(step):
        return 0 if step < 0 else 1

    for face in range(4):
        along_x, s = face < 2, face % 2
        cell = inner(s)
        to = (xs if along_x else ys).at[s]
        for k in range(4):
            to[k * 16:(k + 1) * 16, :] = ext["p"][plane_at(along_x, cell(k)), :]
        ends = jnp.zeros((TY, TZ), F32)
        for k in range(3):
            ends = jnp.where(lane == k, pltpu.roll(vzm[plane_at(along_x, cell(k)), :], k + 1, 1), ends)
        to[64:80, :] = ends
        beside, through = (vys, vxs) if along_x else (vxs, vys)
        for k in range(3):
            to[80 + k:81 + k, :] = beside[1, 4 + cell(k):5 + cell(k), :]
        if s == 1:
            to[96:112, :] = through[1, 4:20, :]
    for s, (sx, sy) in enumerate(DIAGS):
        cx, cy = inner(up(sx)), inner(up(sy))
        for i, (f, a, b) in enumerate(CORNER):
            r = row_of(cx(a), cy(b))
            ds[s, i:i + 1, :] = ext[f][r:r + 1, :]
        for k in range(3):
            ds[s, 9 + k:10 + k, :] = vxs[1, 4 + cy(k):5 + cy(k), :]
            ds[s, 12 + k:13 + k, :] = vys[1, 4 + cx(k):5 + cx(k), :]

    def slot(u):
        return ((lane + 4) % TZ) // 8 == u

    lower = lane % 8 < 4

    def pack_z(f):
        made = []
        for odd in (0, 1):
            packed = jnp.zeros((GROUP, TZ), F32)
            for u in range(16):
                g = MAIN_GROUPS[2 * u + odd]
                value = ext[f][g * 8:g * 8 + 8, :]
                if f == "c":
                    value = jnp.where(lane == TZ - 4, roll_lanes(vzm[g * 8:g * 8 + 8, :], -3), value)
                packed = jnp.where(slot(u), roll_lanes(value, 8 * u), packed)
            made.append(packed)
        one, two = made
        i = Z_SLOT[f]
        zs[0, i] = jnp.where(lower, one, roll_lanes(two, 4))
        zs[1, i] = jnp.where(lower, roll_lanes(one, 4), roll_lanes(two, 8))
        zown[2 * i] = one
        zown[2 * i + 1] = two

    pack_z("p")
    packed = jnp.zeros((GROUP, TZ), F32)
    for u in range(4):
        value = (vxs, vys)[u // 2][1, 4 + 8 * (u % 2):12 + 8 * (u % 2), :]
        packed = jnp.where(slot(u), roll_lanes(value, 8 * u), packed)
    zs[0, 1] = packed
    zs[1, 1] = packed
    zown[2] = packed

    def copies(sends, arrivals, buffers):
        return [
            pltpu.make_async_remote_copy(
                src_ref=src, dst_ref=dst, send_sem=sends.at[i], recv_sem=arrivals.at[i],
                device_id=at_side(*side), device_id_type=MESH)
            for i, (side, (src, dst)) in enumerate(zip(SIDES, buffers))
        ]

    def first_copies(t):
        faces = [(a.at[s, r], b.at[s, r]) for a, b in ((xs, xr), (ys, yr)) for s, r in (
            (0, pl.ds(112, 96) if t else pl.ds(0, 96)), (1, pl.ds(112, 96) if t else pl.ds(0, 112)))]
        r = pl.ds(16, 8) if t else pl.ds(0, 16)
        return copies(ss.at[t], rs.at[t], faces + [(ds.at[s, r], dr.at[s, r]) for s in range(4)])

    def z_copies(t):
        r = pl.ds(2, 3) if t else pl.ds(0, 2)
        return [
            pltpu.make_async_remote_copy(
                src_ref=zs.at[s, r], dst_ref=zr.at[s, r], send_sem=zss.at[t, s], recv_sem=zrs.at[t, s],
                device_id={"gz": iz + (2 * s - 1)}, device_id_type=MESH)
            for s in (0, 1)
        ]

    firsts = [first_copies(t) for t in (0, 1)]
    to_z = [z_copies(t) for t in (0, 1)]
    from_z = (jnp.logical_not(high_z), jnp.logical_not(low_z))

    def send_first(t):
        for s in (0, 1):
            @pl.when(from_z[1 - s])
            def _(s=s):
                to_z[t][s].start()
        for side, copy in zip(SIDES, firsts[t]):
            @pl.when(has(*side))
            def _(copy=copy):
                copy.start()

    pl.semaphore_wait(barrier, expected)

    @pl.when(bridge)
    def _():
        pl.semaphore_signal(met, inc=1, device_id=across, device_id_type=MESH)

    send_first(0)

    @pl.loop(1, SRC // KC)
    def _(chunk):
        acc[...] += scattered(pl.ds(pl.multiple_of(chunk * KC, KC), KC))

    sheets = [(acc[n * TZ:(n + 1) * TZ, :] + acc[(STEPS + n) * TZ:(STEPS + n + 1) * TZ, :]).T for n in range(STEPS)]
    for x in range(TX):
        at = slice(x * TY, (x + 1) * TY)
        to = slice(row_of(x, 0), row_of(x, 0) + TY)
        added = [sheet[at, :] for sheet in sheets]
        p = fv[0, at, :]
        vx, vy, vz = (fv[k, at, :] for k in (1, 2, 3))
        gone = vx + (vy - jnp.where(sub == 0, 0.0, pltpu.roll(vy, 1, 0)))
        gone = gone + (vz - jnp.where(lane == 0, 0.0, pltpu.roll(vz, 1, 1)))
        if x:
            gone = gone - fv[1, (x - 1) * TY:x * TY, :]
        cm[to, :] = added[0] - 0.5 * (gone + p)
        d2m[to, :] = added[1] - added[0]
        d3m[to, :] = added[2] - added[1]
        d4[at, :] = added[3] - added[2]

    for face in range(4):
        along_x, s = face < 2, face % 2
        cell = inner(s)
        to = (xs if along_x else ys).at[s]
        for i, (f, k) in enumerate(LATER):
            to[112 + i * 16:128 + i * 16, :] = ext[f][plane_at(along_x, cell(k)), :]
    for s, (sx, sy) in enumerate(DIAGS):
        cx, cy = inner(up(sx)), inner(up(sy))
        for i, (f, a, b) in enumerate(LATER_CORNER):
            r = row_of(cx(a), cy(b))
            ds[s, 16 + i:17 + i, :] = ext[f][r:r + 1, :]
    for f in ALONG_Z[1:]:
        pack_z(f)
    send_first(1)

    for d in range(OWN):
        cells = cell_r[d:d + 1, :]
        span = slice(d * CAP, (d + 1) * CAP)
        one = jnp.where(iota((ROWS, 1), 0) == cells // TZ, 1.0, 0.0).astype(BF)
        cone[0:ROWS, span] = one
        cone[ROWS:2 * ROWS, span] = one
        zsel[:, span] = jnp.where(iota((TZ, 1), 0) == cells % TZ, 1.0, 0.0).astype(F32)

    eye = iota((TONES, TONES), 0) == iota((TONES, TONES), 1)
    freq = jnp.sum(jnp.where(eye, tone_r[...], 0.0), axis=1, keepdims=True)
    freq = jnp.concatenate([freq, freq], axis=0)
    angle = freq * lane.astype(F32)
    basis = half_wave(angle, jnp.where(iota((NB, 1), 0) < TONES, 0.5, 0.0).astype(F32)) * 0.125
    for n in range(STEPS):
        bt[n * NB:(n + 1) * NB, :] = jnp.broadcast_to(basis[:, HIST + n:HIST + n + 1], (NB, CAP))
    held = iota((OWN, OWN), 0) == iota((OWN, OWN), 1)
    counts = jnp.sum(jnp.where(held, count_r[...].astype(F32), 0.0), axis=1, keepdims=True)
    live = jnp.where(lane.astype(F32) < counts, 1.0, 0.0).astype(F32)
    bt_out = pltpu.make_async_copy(bt, bt_h, osem.at[3])
    bt_out.start()

    @pl.when(bridge)
    def _():
        pl.semaphore_wait(met, 1)
        for mate in mates:
            pl.semaphore_signal(all_in, inc=1, device_id=mate, device_id_type=MESH)

    for i in range(4):
        sx, sy = SIDES[i]

        @pl.when(has(-sx, -sy))
        def _(i=i):
            along_x, s = i < 2, i % 2
            out = outer(s)
            firsts[0][i].wait_recv()
            got = (xr if along_x else yr).at[s]
            for k in range(4):
                ext["p"][plane_at(along_x, out(k)), :] = got[k * 16:(k + 1) * 16, :]
            beside, through = (vys, vxs) if along_x else (vxs, vys)
            ends = got[64:80, :]
            for k in range(3):
                vzm[plane_at(along_x, out(k)), :] = pltpu.roll(ends, TZ - 1 - k, 1)
                beside[1, 4 + out(k):5 + out(k), :] = got[80 + k:81 + k, :]
            if s == 1:
                through[0, 4:20, :] = got[96:112, :]

    for i in range(4, 8):
        sx, sy = SIDES[i]

        @pl.when(has(-sx, -sy))
        def _(i=i, sx=sx, sy=sy):
            ox, oy = outer(up(sx)), outer(up(sy))
            firsts[0][i].wait_recv()
            for j, (f, a, b) in enumerate(CORNER):
                r = row_of(ox(a), oy(b))
                ext[f][r:r + 1, :] = dr[i - 4, j:j + 1, :]
            for k in range(3):
                if sx > 0:
                    vxs[0, 4 + oy(k):5 + oy(k), :] = dr[i - 4, 9 + k:10 + k, :]
                if sy > 0:
                    vys[0, 4 + ox(k):5 + ox(k), :] = dr[i - 4, 12 + k:13 + k, :]

    for i in range(4):
        sx, sy = SIDES[i]

        @pl.when(has(-sx, -sy))
        def _(i=i):
            along_x, s = i < 2, i % 2
            out = outer(s)
            firsts[1][i].wait_recv()
            got = (xr if along_x else yr).at[s]
            for j, (f, k) in enumerate(LATER):
                ext[f][plane_at(along_x, out(k)), :] = got[112 + j * 16:128 + j * 16, :]

    for i in range(4, 8):
        sx, sy = SIDES[i]

        @pl.when(has(-sx, -sy))
        def _(i=i, sx=sx, sy=sy):
            ox, oy = outer(up(sx)), outer(up(sy))
            firsts[1][i].wait_recv()
            for j, (f, a, b) in enumerate(LATER_CORNER):
                r = row_of(ox(a), oy(b))
                ext[f][r:r + 1, :] = dr[i - 4, 16 + j:17 + j, :]

    def borders(change, vx, vy):
        for k, x in ((0, 0), (1, TX)):
            r = row_of(x, -4)
            change[r:r + WIDE, :] = change[r:r + WIDE, :] + vx[k]
        for k, y in ((0, 0), (1, TY)):
            r = pl.ds(row_of(-4, y), WIDE, stride=WIDE)
            change[r, :] = change[r, :] + vy[k]

    def mirrors(refs, widths):
        for flag, low, along_x in (
            (low_x, True, True), (high_x, False, True), (low_y, True, False), (high_y, False, False)
        ):
            @pl.when(flag)
            def _(low=low, along_x=along_x):
                def rows(q):
                    return pl.ds(row_of(q, -4), WIDE) if along_x else pl.ds(row_of(-4, q), WIDE, stride=WIDE)

                for f, width in widths:
                    for k in range(width):
                        if low:
                            refs[f][rows(-1 - k), :] = refs[f][rows(k), :]
                        elif k == 0:
                            refs[f][rows(TX), :] = jnp.zeros((WIDE, TZ), F32)
                        else:
                            refs[f][rows(TX + k), :] = -refs[f][rows(TX - k), :]

    borders(cm, vxs, vys)
    mirrors(ext, WIDTHS + (("v", 3),))

    for s in (0, 1):
        @pl.when(from_z[s])
        def _(s=s):
            to_z[0][s].wait_recv()
            to_z[1][s].wait_recv()

    place = (lane + 4) % 8

    def joined(own, from_low, from_high, skip):
        below = jnp.zeros((GROUP, TZ), F32)
        above = jnp.zeros((GROUP, TZ), F32)
        for k in range(4):
            if not (skip and k == 3):
                below = jnp.where(place == 3 - k, roll_lanes(own, -(2 * k + 1)), below)
            if k:
                above = jnp.where(place == 4 + k, -roll_lanes(own, 2 * k), above)
        return jnp.where(
            place < 4, jnp.where(low_z, below, from_low), jnp.where(high_z, above, from_high))

    for f in ALONG_Z:
        i = Z_SLOT[f]
        lows, highs = zr[1, i], zr[0, i]
        for odd in (0, 1):
            merged = joined(
                zown[2 * i + odd], roll_lanes(lows, -4 - 4 * odd), roll_lanes(highs, -4 * odd), f == "c")
            for u in range(16):
                g = MAIN_GROUPS[2 * u + odd]
                value = roll_lanes(merged, -8 * u)
                ring[f][g * 8:g * 8 + 8, :] = value
                if f == "c":
                    vzq[g * 8:g * 8 + 8, :] = roll_lanes(value, 3)
    merged = joined(zown[2], zr[1, 1], zr[0, 1], False)
    for u in range(4):
        (vxq, vyq)[u // 2][1, 4 + 8 * (u % 2):12 + 8 * (u % 2), :] = roll_lanes(merged, -8 * u)

    for face in range(4):
        along_x, s = face < 2, face % 2
        cell = inner(s)
        beside, through = (vyq, vxq) if along_x else (vxq, vyq)
        for k in range(3):
            spare[face, k:k + 1, :] = beside[1, 4 + cell(k):5 + cell(k), :]
        planes = [ring[f][plane_at(along_x, cell(k)), :] for f, k in RING_PLANES] + [spare[face]]
        if s == 1:
            planes.append(through[1, 4:20, :])
        packed = jnp.zeros((TY, TZ), F32)
        for u, value in enumerate(planes):
            packed = jnp.where(slot(u), roll_lanes(value, 8 * u), packed)
        qs[face] = packed
    for s, (sx, sy) in enumerate(DIAGS):
        cx, cy = inner(up(sx)), inner(up(sy))
        for i, (f, a, b) in enumerate(RING_CORNER):
            r = row_of(cx(a), cy(b))
            es[s, i:i + 1, :] = ring[f][r:r + 1, :]
        for k in range(2):
            es[s, 8 + k:9 + k, :] = vxq[1, 4 + cy(k):5 + cy(k), :]
            es[s, 10 + k:11 + k, :] = vyq[1, 4 + cx(k):5 + cx(k), :]
    seconds = copies(qss, qrs, [(qs.at[s], qr.at[s]) for s in range(4)] + [(es.at[s], er.at[s]) for s in range(4)])
    for side, copy in zip(SIDES, seconds):
        @pl.when(has(*side))
        def _(copy=copy):
            copy.start()

    for i in range(4):
        sx, sy = SIDES[i]

        @pl.when(has(-sx, -sy))
        def _(i=i):
            along_x, s = i < 2, i % 2
            out = outer(s)
            seconds[i].wait_recv()
            got = qr[i]
            for u, (f, k) in enumerate(RING_PLANES):
                ring[f][plane_at(along_x, out(k)), :] = roll_lanes(got, -8 * u)
            beside, through = (vyq, vxq) if along_x else (vxq, vyq)
            last = len(RING_PLANES)
            side_rows = roll_lanes(got, -8 * last)
            for k in range(3):
                beside[1, 4 + out(k):5 + out(k), :] = side_rows[k:k + 1, :]
            if s == 1:
                through[0, 4:20, :] = roll_lanes(got, -8 * (last + 1))

    for i in range(4, 8):
        sx, sy = SIDES[i]

        @pl.when(has(-sx, -sy))
        def _(i=i, sx=sx, sy=sy):
            ox, oy = outer(up(sx)), outer(up(sy))
            seconds[i].wait_recv()
            for j, (f, a, b) in enumerate(RING_CORNER):
                r = row_of(ox(a), oy(b))
                ring[f][r:r + 1, :] = er[i - 4, j:j + 1, :]
            for k in range(2):
                if sx > 0:
                    vxq[0, 4 + oy(k):5 + oy(k), :] = er[i - 4, 8 + k:9 + k, :]
                if sy > 0:
                    vyq[0, 4 + ox(k):5 + ox(k), :] = er[i - 4, 10 + k:11 + k, :]

    borders(cq, vxq, vyq)
    mirrors(ring, RING_WIDTHS)

    for g in range(4, 69):
        at = slice(g * 8, g * 8 + 8)
        cm[at, :] = cm[at, :] + roll_lanes(jnp.where(lane == TZ - 1, vzq[at, :], 0.0), 1)
        if 7 <= g < 66:
            flow = roll_lanes(jnp.where(lane == TZ - 1, vzm[at, :], 0.0), 1)
            cq[at, :] = cq[at, :] + jnp.where(high_z, 0.0, flow)

    for n in range(STEPS):
        d_main = (cm, d2m, d3m, d4)[n]
        d_ring = (cq, d2q, d3q, None)[n]
        main_span = (range(4, 69), range(7, 66), range(10, 63), [g for g in range(13, 60) if g % 3])[n]
        ring_span = (range(7, 66), range(10, 63), range(13, 60), ())[n]
        for g in main_span:
            at = slice(g * 8, g * 8 + 8)
            here, ghost = pm[n, at, :], pq[n, at, :]

            def stepped(ref, d, here, other):
                sums = (ref[n, g * 8 - WIDE:g * 8 - WIDE + 8, :] + ref[n, g * 8 + WIDE:g * 8 + WIDE + 8, :]) + (
                    ref[n, g * 8 - 1:g * 8 + 7, :] + ref[n, g * 8 + 1:g * 8 + 9, :])
                back = pltpu.roll(jnp.where(lane == TZ - 1, other, here), 1, 1)
                fore = pltpu.roll(jnp.where(lane == 0, other, here), TZ - 1, 1)
                new = d + 0.25 * (sums + (back + fore))
                return new if n == 0 else new + (0.5 * here - ref[n - 1, at, :])

            if n < STEPS - 1:
                pm[n + 1, at, :] = stepped(pm, d_main[at, :], here, ghost)
                if g in ring_span:
                    pq[n + 1, at, :] = stepped(pq, d_ring[at, :], ghost, here)
            else:
                x, half = divmod(g - 13, 3)
                own = slice(x * TY + half * 8, x * TY + half * 8 + 8)
                plast[own, :] = stepped(pm, d4[own, :], here, ghost)
        new = plast[...] if n == STEPS - 1 else jnp.concatenate(
            [pm[n + 1, row_of(x, 0):row_of(x, 0) + TY, :] for x in range(TX)], axis=0)
        both[n * TZ:(n + 1) * TZ, :] = jnp.concatenate(split(new.T), axis=1)

    for d in range(0, OWN, 2):
        span = slice(d * CAP, (d + 2) * CAP)
        seen = dot_nn(both[...], cone[:, span])
        for n in range(STEPS):
            got = jnp.sum(seen[n * TZ:(n + 1) * TZ, :] * zsel[:, span], axis=0, keepdims=True)
            sb[d * 8 + n:d * 8 + n + 1, :] = got[:, :CAP]
            sb[(d + 1) * 8 + n:(d + 1) * 8 + n + 1, :] = got[:, CAP:]

    def block_copy(k):
        target = lax.rem(iz + k, OWN)
        return pltpu.make_async_remote_copy(
            src_ref=sb.at[pl.ds(pl.multiple_of(target * 8, 8), 8)],
            dst_ref=rb.at[pl.ds(pl.multiple_of(iz * 8, 8), 8)],
            send_sem=ass.at[k], recv_sem=ars.at[k], device_id={"gz": target}, device_id_type=MESH)

    @pl.when(jnp.logical_not(bridge))
    def _():
        pl.semaphore_wait(all_in, 1)

    sends = [block_copy(k) for k in range(1, OWN)]
    for k in (8, 7, 9, 6, 10, 5, 11, 4, 12, 3, 13, 2, 14, 1, 15):
        sends[k - 1].start()
    mine = pl.ds(pl.multiple_of(iz * 8, 8), 8)
    rb[mine, :] = sb[mine, :]

    outs = [pltpu.make_async_copy(plast, fout_h.at[0], osem.at[0])]
    outs[0].start()
    for side, *three in zip(SIDES, *firsts, seconds):
        @pl.when(has(*side))
        def _(three=three):
            for copy in three:
                copy.wait_send()
    for s in (0, 1):
        @pl.when(from_z[1 - s])
        def _(s=s):
            to_z[0][s].wait_send()
            to_z[1][s].wait_send()
    for g in range(13, 64):
        at = slice(g * 8, g * 8 + 8)
        sm[at, :] = (pm[0, at, :] + pm[1, at, :]) + (pm[2, at, :] + pm[3, at, :])
        sq[at, :] = (pq[0, at, :] + pq[1, at, :]) + (pq[2, at, :] + pq[3, at, :])
    for x in range(TX):
        at = slice(x * TY, (x + 1) * TY)
        r = row_of(x, 0)
        own = sm[r:r + TY, :]
        fv[1, at, :] = fv[1, at, :] - 0.5 * (sm[r + WIDE:r + WIDE + TY, :] - own)
        fv[2, at, :] = fv[2, at, :] - 0.5 * (sm[r + 1:r + 1 + TY, :] - own)
        fore = pltpu.roll(jnp.where(lane == 0, sq[r:r + TY, :], own), TZ - 1, 1)
        fv[3, at, :] = fv[3, at, :] - 0.5 * (fore - own)
    outs.append(pltpu.make_async_copy(fv.at[pl.ds(1, 3)], fout_h.at[pl.ds(1, 3)], osem.at[1]))
    outs[1].start()

    hist_load.wait()
    hv[HIST * OWN:, :] = jnp.zeros((STEPS * OWN, CAP), F32)
    bh, bl = split(basis)
    lhs = jnp.concatenate([bh, bl, bh], axis=1)
    for e in range(0, OWN, 2):
        hh, hl = split(jnp.concatenate(
            [hv[pl.ds(e, HIST + STEPS, stride=OWN), :], hv[pl.ds(e + 1, HIST + STEPS, stride=OWN), :]], axis=1))
        part = dot_nn(lhs, jnp.concatenate([hh, hh, hl], axis=0))
        ov[pl.ds(e, NB, stride=OWN), :] = part[:, :CAP] * live[e:e + 1]
        ov[pl.ds(e + 1, NB, stride=OWN), :] = part[:, CAP:] * live[e + 1:e + 2]
    ov_out = pltpu.make_async_copy(ov, cout_h, osem.at[2])
    ov_out.start()

    for copy in sends:
        copy.wait_recv()
    for n in range(STEPS):
        hb[n * OWN:(n + 1) * OWN, :] = rb[pl.ds(n, OWN, stride=8), :] * live
    outs.append(pltpu.make_async_copy(hb, heard_h, osem.at[4]))
    outs[-1].start()
    for copy in sends:
        copy.wait_send()
    for copy in outs + [bt_out, ov_out]:
        copy.wait()


PARTS = 4
PER = NB // PARTS


def finish(fields_h, part_h, heard_h, bt_h, fout_h, cout_h, fv, ov, hb, bt, sems, fsems):
    pieces = [pl.ds(k * PER * OWN, PER * OWN) for k in range(PARTS)]
    first = [pltpu.make_async_copy(heard_h, hb, sems.at[0]), pltpu.make_async_copy(bt_h, bt, sems.at[1])]
    loads = [pltpu.make_async_copy(part_h.at[r], ov.at[r], sems.at[2 + k]) for k, r in enumerate(pieces)]
    stores = [pltpu.make_async_copy(ov.at[r], cout_h.at[r], sems.at[2 + PARTS + k]) for k, r in enumerate(pieces)]
    gets = [pltpu.make_async_copy(fields_h.at[k], fv.at[k], fsems.at[k]) for k in range(4)]
    puts = [pltpu.make_async_copy(fv.at[k], fout_h.at[k], fsems.at[4 + k]) for k in range(4)]
    for copy in first + loads + gets:
        copy.start()
    for copy in first:
        copy.wait()
    heard = [hb[n * OWN:(n + 1) * OWN, :] for n in range(STEPS)]
    for k in range(PARTS):
        loads[k].wait()
        for j in range(k * PER, (k + 1) * PER):
            at = slice(j * OWN, (j + 1) * OWN)
            term = ov[at, :]
            for n in range(STEPS):
                term = term + bt[n * NB + j:n * NB + j + 1, :] * heard[n]
            ov[at, :] = term
        stores[k].start()
        gets[k].wait()
        puts[k].start()
    for copy in stores + puts:
        copy.wait()


def body(
    fields, tone_freq, mode_freq, mode_amp, mode_map, src_pos, src_id, src_gain, sample_cell, sample_count, history
):
    hbm = pl.BlockSpec(memory_space=pl.ANY)
    made = pl.pallas_call(
        kernel,
        out_shape=(
            jax.ShapeDtypeStruct((4, ROWS, TZ), F32),
            jax.ShapeDtypeStruct((NB * OWN, CAP), F32),
            jax.ShapeDtypeStruct((STEPS * OWN, CAP), F32),
            jax.ShapeDtypeStruct((STEPS * NB, CAP), F32),
        ),
        in_specs=[hbm] * 11,
        out_specs=(hbm,) * 4,
        scratch_shapes=[
            pltpu.VMEM((1, TONES), F32),
            pltpu.VMEM((1, MODES), F32),
            pltpu.VMEM((1, MODES), F32),
            pltpu.VMEM((1, MODES), jnp.int32),
            pltpu.VMEM((3, SRC), jnp.int32),
            pltpu.VMEM((1, SRC), jnp.int32),
            pltpu.VMEM((1, SRC), F32),
            pltpu.VMEM((OWN, CAP), jnp.int32),
            pltpu.VMEM((1, OWN), jnp.int32),
            pltpu.VMEM((4, ROWS, TZ), F32),
            pltpu.VMEM(((HIST + STEPS) * OWN, CAP), F32),
            pltpu.VMEM((STEPS, EXT, TZ), F32),
            pltpu.VMEM((STEPS, EXT, TZ), F32),
            pltpu.VMEM((EXT, TZ), F32),
            pltpu.VMEM((EXT, TZ), F32),
            pltpu.VMEM((EXT, TZ), F32),
            pltpu.VMEM((EXT, TZ), F32),
            pltpu.VMEM((EXT, TZ), F32),
            pltpu.VMEM((EXT, TZ), F32),
            pltpu.VMEM((ROWS, TZ), F32),
            pltpu.VMEM((EXT, TZ), F32),
            pltpu.VMEM((EXT, TZ), F32),
            pltpu.VMEM((2, WIDE, TZ), F32),
            pltpu.VMEM((2, WIDE, TZ), F32),
            pltpu.VMEM((2, WIDE, TZ), F32),
            pltpu.VMEM((2, WIDE, TZ), F32),
            pltpu.VMEM((ROWS, TZ), F32),
            pltpu.VMEM((EXT, TZ), F32),
            pltpu.VMEM((EXT, TZ), F32),
            pltpu.VMEM((8, 2048), F32),
            pltpu.VMEM((8, SRC), F32),
            pltpu.VMEM((1, SRC), F32),
            pltpu.VMEM((1, SRC), F32),
            pltpu.VMEM((2 * STEPS * TZ, ROWS), F32),
            pltpu.VMEM((2 * ROWS, SLOTS), BF),
            pltpu.VMEM((TZ, SLOTS), F32),
            pltpu.VMEM((STEPS * TZ, 2 * ROWS), BF),
            pltpu.VMEM((NB * OWN, CAP), F32),
            pltpu.VMEM((STEPS * NB, CAP), F32),
            pltpu.VMEM((OWN * 8, CAP), F32),
            pltpu.VMEM((OWN * 8, CAP), F32),
            pltpu.VMEM((STEPS * OWN, CAP), F32),
            pltpu.VMEM((2, 208, TZ), F32),
            pltpu.VMEM((2, 208, TZ), F32),
            pltpu.VMEM((2, 208, TZ), F32),
            pltpu.VMEM((2, 208, TZ), F32),
            pltpu.VMEM((4, 24, TZ), F32),
            pltpu.VMEM((4, 24, TZ), F32),
            pltpu.VMEM((2, 5, GROUP, TZ), F32),
            pltpu.VMEM((2, 5, GROUP, TZ), F32),
            pltpu.VMEM((4, TY, TZ), F32),
            pltpu.VMEM((4, TY, TZ), F32),
            pltpu.VMEM((4, TY, TZ), F32),
            pltpu.VMEM((4, TY, TZ), F32),
            pltpu.VMEM((4, TY, TZ), F32),
            pltpu.VMEM((10, GROUP, TZ), F32),
            pltpu.SemaphoreType.DMA((9,)),
            pltpu.SemaphoreType.DMA((4,)),
            pltpu.SemaphoreType.DMA,
            pltpu.SemaphoreType.DMA((5,)),
            pltpu.SemaphoreType.DMA((2, 8)),
            pltpu.SemaphoreType.DMA((2, 8)),
            pltpu.SemaphoreType.DMA((2, 2)),
            pltpu.SemaphoreType.DMA((2, 2)),
            pltpu.SemaphoreType.DMA((8,)),
            pltpu.SemaphoreType.DMA((8,)),
            pltpu.SemaphoreType.DMA((OWN,)),
            pltpu.SemaphoreType.DMA((OWN,)),
            pltpu.SemaphoreType.REGULAR,
            pltpu.SemaphoreType.REGULAR,
        ],
        compiler_params=pltpu.CompilerParams(
            collective_id=0, has_side_effects=True, vmem_limit_bytes=63 * 1024 * 1024
        ),
    )(
        fields.reshape(4, ROWS, TZ),
        tone_freq.reshape(1, TONES),
        mode_freq.reshape(1, MODES),
        mode_amp.reshape(1, MODES),
        mode_map.reshape(1, MODES),
        src_pos,
        src_id.reshape(1, SRC),
        src_gain.reshape(1, SRC),
        sample_cell.reshape(OWN, CAP),
        sample_count.reshape(1, OWN),
        history.reshape(HIST * OWN, CAP),
    )
    fields_out, coefficients = pl.pallas_call(
        finish,
        out_shape=(
            jax.ShapeDtypeStruct((4, ROWS, TZ), F32),
            jax.ShapeDtypeStruct((NB * OWN, CAP), F32),
        ),
        in_specs=[hbm] * 4,
        out_specs=(hbm,) * 2,
        scratch_shapes=[
            pltpu.VMEM((4, ROWS, TZ), F32),
            pltpu.VMEM((NB * OWN, CAP), F32),
            pltpu.VMEM((STEPS * OWN, CAP), F32),
            pltpu.VMEM((STEPS * NB, CAP), F32),
            pltpu.SemaphoreType.DMA((2 + 2 * PARTS,)),
            pltpu.SemaphoreType.DMA((8,)),
        ],
        compiler_params=pltpu.CompilerParams(vmem_limit_bytes=63 * 1024 * 1024),
    )(*made)
    return fields_out.reshape(fields.shape), coefficients.reshape(NB, 1, 1, 1, OWN, CAP)


def solution(mesh):
    in_specs = (
        P(None, "gx", "gy", "gz"),
        P(),
        P(),
        P(),
        P(),
        P(),
        P(),
        P(),
        P("gx", "gy", "gz", None, None),
        P("gx", "gy", None, "gz"),
        P(None, "gx", "gy", "gz", None, None),
    )
    out_specs = (P(None, "gx", "gy", "gz"), P(None, "gx", "gy", "gz", None, None))
    return jax.shard_map(body, mesh=mesh, in_specs=in_specs, out_specs=out_specs, check_vma=False)
```

```python
import jax
import jax.numpy as jnp
import numpy as np
from jax import lax
from jax.experimental import pallas as pl
from jax.experimental.pallas import tpu as pltpu
from jax.sharding import PartitionSpec as P

STEPS = 4
HIST = 124
SOURCES = 48
TONES = 48
MODES = 2000
SRC = 4096
TX, TY, TZ = 16, 16, 128
ROWS = TX * TY
OWN = 16
CAP = 128
SLOTS = OWN * CAP
NB = 2 * TONES
KC = 1024
F32 = jnp.float32
BF = jnp.bfloat16
MESH = pl.DeviceIdType.MESH
ONE = np.asarray(1, BF)
ZERO = np.asarray(0, BF)


def split(values):
    high = values.astype(BF)
    return high, (values - high.astype(F32)).astype(BF)


def dot_nn(a, b):
    return lax.dot_general(a, b, (((1,), (0,)), ((), ())), preferred_element_type=F32)


def dot_nt(a, b):
    return lax.dot_general(a, b, (((1,), (1,)), ((), ())), preferred_element_type=F32)


def half_wave(x, half):
    k = jnp.floor(x * 0.3183098861837907 + (0.5 - half))
    h = k + half
    r = x - h * 3.140625
    r = r - h * 0.0009670257568359375
    r = r - h * 6.2771141529083251953e-07
    q = r * r
    s = -2.505210838544172e-08
    for c in (2.7557319223985893e-06, -1.984126984126984e-04, 8.333333333333333e-03, -0.16666666666666666):
        s = s * q + c
    s = r + r * q * s
    sign = 1.0 - 2.0 * (k - 2.0 * jnp.floor(k * 0.5))
    return jnp.where(half > 0.25, -sign, sign) * s


def iota(shape, dim):
    return lax.broadcasted_iota(jnp.int32, shape, dim)


GROUP = 8
HALF = 8
BRIDGE = 3
WIDE = 24
EXT = 584
WIDTHS = (("p", 4), ("c", 3), ("d2", 2), ("d3", 1))
LATER = [(f, k) for f, width in WIDTHS[1:] for k in range(width)]
RING_WIDTHS = (("p", 3), ("c", 2), ("d2", 1), ("v", 3))
RING_PLANES = [(f, k) for f, width in RING_WIDTHS for k in range(width)]
DIAGS = ((-1, -1), (-1, 1), (1, -1), (1, 1))
SIDES = ((-1, 0), (1, 0), (0, -1), (0, 1)) + DIAGS
CORNER = [("p", i, j) for i in range(3) for j in range(3 - i)] + [("v", i, j) for i in range(2) for j in range(2 - i)]
LATER_CORNER = [("c", i, j) for i in range(2) for j in range(2 - i)] + [("d2", 0, 0)]
RING_CORNER = [(f, i, j) for f in ("p", "v") for i in range(2) for j in range(2 - i)] + [("c", 0, 0)]
ALONG_Z = ("p", "c", "d2", "d3")
Z_SLOT = {"p": 0, "c": 2, "d2": 3, "d3": 4}
MAIN_GROUPS = [g for g in range(13, 60) if g % 3]


def row_of(x, y):
    return 8 + WIDE * (x + 4) + y


def roll_lanes(v, by):
    return pltpu.roll(v, by % TZ, 1) if by % TZ else v


def kernel(
    fields_h, tone_h, mfreq_h, mamp_h, mmap_h, spos_h, sid_h, sgain_h, cell_h, count_h, hist_h,
    fout_h, cout_h, heard_h, bt_h,
    tone_r, mfreq_r, mamp_r, mmap_r, spos_r, sid_r, sgain_r, cell_r, count_r,
    fv, hv, pm, pq, cm, cq, d2m, d2q, d3m, d3q, d4, vzm, vzq, vxs, vys, vxq, vyq, plast, sm, sq,
    ms, wv, srow, scol, acc, cone, zsel, both, ov, bt, sb, rb, hb,
    xs, xr, ys, yr, ds, dr, zs, zr, qs, qr, es, er, spare, zown,
    isem, fsem, hsem, osem, ss, rs, zss, zrs, qss, qrs, ass, ars, met, all_in,
):
    ix = lax.axis_index("gx")
    iy = lax.axis_index("gy")
    iz = lax.axis_index("gz")
    low_x, high_x = ix == 0, ix == 3
    low_y, high_y = iy == 0, iy == 3
    low_z, high_z = iz == 0, iz == OWN - 1

    small = [
        pltpu.make_async_copy(src, dst, isem.at[k])
        for k, (src, dst) in enumerate((
            (mfreq_h, mfreq_r), (mamp_h, mamp_r), (mmap_h, mmap_r), (sid_h, sid_r), (sgain_h, sgain_r),
            (spos_h, spos_r), (tone_h, tone_r), (cell_h, cell_r), (count_h, count_r)))
    ]
    for copy in small:
        copy.start()
    loads = [pltpu.make_async_copy(fields_h.at[k], fv.at[k], fsem.at[k]) for k in range(4)]
    for copy in loads:
        copy.start()
    def has(sx, sy):
        ok = None
        for s, low, high in ((sx, low_x, high_x), (sy, low_y, high_y)):
            if s:
                here = jnp.logical_not(low if s < 0 else high)
                ok = here if ok is None else ok & here
        return ok

    def at_side(sx, sy):
        where = {}
        if sx:
            where["gx"] = ix + sx
        if sy:
            where["gy"] = iy + sy
        return where

    barrier = pltpu.get_barrier_semaphore()
    half = (iz // HALF) * HALF
    bridge = (iz == BRIDGE) | (iz == BRIDGE + HALF)
    border = (iz == HALF - 1) | (iz == HALF)
    across = {"gz": lax.rem(iz + HALF, OWN)}
    mates = [{"gz": half + lax.rem(iz - half + k, HALF)} for k in range(1, HALF)]

    @pl.when(border)
    def _():
        pl.semaphore_signal(barrier, inc=1, device_id={"gz": OWN - 1 - iz}, device_id_type=MESH)

    @pl.when(bridge)
    def _():
        pl.semaphore_signal(barrier, inc=1, device_id=across, device_id_type=MESH)

    for mate in mates:
        pl.semaphore_signal(barrier, inc=1, device_id=mate, device_id_type=MESH)
    expected = HALF - 1 + jnp.where(border, 1, 0) + jnp.where(bridge, 1, 0)
    for side in SIDES:
        expected = expected + jnp.where(has(*side), 1, 0)

        @pl.when(has(*side))
        def _(side=side):
            pl.semaphore_signal(barrier, inc=1, device_id=at_side(*side), device_id_type=MESH)

    hist_load = pltpu.make_async_copy(hist_h, hv.at[pl.ds(0, HIST * OWN)], hsem)
    hist_load.start()

    lane = iota((1, TZ), 1)
    sub = iota((TY, 1), 0)
    row8 = iota((8, 1), 0)
    ext = {"p": pm.at[0], "c": cm, "v": vzm, "d2": d2m, "d3": d3m}
    ring = {"p": pq.at[0], "c": cq, "d2": d2q, "d3": d3q, "v": vzq}
    for ref in (vxs, vys, vxq, vyq, spare):
        ref[...] = jnp.zeros_like(ref)

    ms[...] = jnp.zeros_like(ms)
    for copy in small:
        copy.wait()
    ms[0:1, 0:MODES] = mfreq_r[...]
    ms[1:2, 0:MODES] = mamp_r[...]
    ms[2:3, 0:MODES] = mmap_r[...].astype(F32)
    moment = (HIST + row8 % STEPS).astype(F32)
    waves = ms[1:2, :] * half_wave(ms[0:1, :] * moment, jnp.zeros((8, 1), F32))
    high = waves.astype(BF).astype(F32)
    waves = jnp.where(row8 < STEPS, high, waves - high).astype(BF)
    pick = jnp.where(iota((SOURCES, 1), 0).astype(F32) == ms[2:3, :], 1.0, 0.0).astype(BF)
    drive = dot_nt(waves, pick)
    drive = drive + pltpu.roll(drive, 4, 0)
    high = drive.astype(BF).astype(F32)
    drive = jnp.where(row8 < STEPS, high, drive - high).astype(BF)
    pick = jnp.where(iota((SOURCES, 1), 0) == sid_r[...], 1.0, 0.0).astype(BF)
    weight = dot_nn(drive, pick)
    weight = (weight + pltpu.roll(weight, 4, 0)) * sgain_r[...]
    high = weight.astype(BF).astype(F32)
    wv[...] = jnp.where(row8 < STEPS, high, weight - high)
    lx = spos_r[0:1, :] - ix * TX
    ly = spos_r[1:2, :] - iy * TY
    lz = spos_r[2:3, :] - iz * TZ
    inside = (lx >= 0) & (lx < TX) & (ly >= 0) & (ly < TY) & (lz >= 0) & (lz < TZ)
    srow[...] = jnp.where(inside, lx * TY + ly, -1).astype(F32)
    scol[...] = lz.astype(F32)

    def scattered(span):
        a = jnp.where(iota((ROWS, 1), 0).astype(F32).astype(BF) == srow[:, span].astype(BF), ONE, ZERO)
        m = iota((TZ, 1), 0).astype(F32).astype(BF) == scol[:, span].astype(BF)
        b = jnp.concatenate([jnp.where(m, wv[q:q + 1, span].astype(BF), ZERO) for q in range(2 * STEPS)], axis=0)
        return dot_nt(b, a)

    acc[...] = scattered(pl.ds(0, KC))

    for copy in loads:
        copy.wait()
    for x in range(TX):
        at = slice(x * TY, (x + 1) * TY)
        to = slice(row_of(x, 0), row_of(x, 0) + TY)
        pm[0, to, :] = fv[0, at, :]
        vzm[to, :] = 0.5 * fv[3, at, :]
    vxs[1, 4:20, :] = 0.5 * fv[1, ROWS - TY:ROWS, :]
    vys[1, 4:20, :] = 0.5 * fv[2, pl.ds(TY - 1, TX, stride=TY), :]

    def plane_at(along_x, q):
        return pl.ds(row_of(q, 0), TY) if along_x else pl.ds(row_of(0, q), TX, stride=WIDE)

    def inner(s):
        return (lambda k: k) if s == 0 else (lambda k: TX - 1 - k)

    def outer(s):
        return (lambda k: TX + k) if s == 0 else (lambda k: -1 - k)

    def up(step):
        return 0 if step < 0 else 1

    for face in range(4):
        along_x, s = face < 2, face % 2
        cell = inner(s)
        to = (xs if along_x else ys).at[s]
        for k in range(4):
            to[k * 16:(k + 1) * 16, :] = ext["p"][plane_at(along_x, cell(k)), :]
        ends = jnp.zeros((TY, TZ), F32)
        for k in range(3):
            ends = jnp.where(lane == k, pltpu.roll(vzm[plane_at(along_x, cell(k)), :], k + 1, 1), ends)
        to[64:80, :] = ends
        beside, through = (vys, vxs) if along_x else (vxs, vys)
        for k in range(3):
            to[80 + k:81 + k, :] = beside[1, 4 + cell(k):5 + cell(k), :]
        if s == 1:
            to[96:112, :] = through[1, 4:20, :]
    for s, (sx, sy) in enumerate(DIAGS):
        cx, cy = inner(up(sx)), inner(up(sy))
        for i, (f, a, b) in enumerate(CORNER):
            r = row_of(cx(a), cy(b))
            ds[s, i:i + 1, :] = ext[f][r:r + 1, :]
        for k in range(3):
            ds[s, 9 + k:10 + k, :] = vxs[1, 4 + cy(k):5 + cy(k), :]
            ds[s, 12 + k:13 + k, :] = vys[1, 4 + cx(k):5 + cx(k), :]

    def slot(u):
        return ((lane + 4) % TZ) // 8 == u

    lower = lane % 8 < 4

    def pack_z(f):
        made = []
        for odd in (0, 1):
            packed = jnp.zeros((GROUP, TZ), F32)
            for u in range(16):
                g = MAIN_GROUPS[2 * u + odd]
                value = ext[f][g * 8:g * 8 + 8, :]
                if f == "c":
                    value = jnp.where(lane == TZ - 4, roll_lanes(vzm[g * 8:g * 8 + 8, :], -3), value)
                packed = jnp.where(slot(u), roll_lanes(value, 8 * u), packed)
            made.append(packed)
        one, two = made
        i = Z_SLOT[f]
        zs[0, i] = jnp.where(lower, one, roll_lanes(two, 4))
        zs[1, i] = jnp.where(lower, roll_lanes(one, 4), roll_lanes(two, 8))
        zown[2 * i] = one
        zown[2 * i + 1] = two

    pack_z("p")
    packed = jnp.zeros((GROUP, TZ), F32)
    for u in range(4):
        value = (vxs, vys)[u // 2][1, 4 + 8 * (u % 2):12 + 8 * (u % 2), :]
        packed = jnp.where(slot(u), roll_lanes(value, 8 * u), packed)
    zs[0, 1] = packed
    zs[1, 1] = packed
    zown[2] = packed

    def copies(sends, arrivals, buffers):
        return [
            pltpu.make_async_remote_copy(
                src_ref=src, dst_ref=dst, send_sem=sends.at[i], recv_sem=arrivals.at[i],
                device_id=at_side(*side), device_id_type=MESH)
            for i, (side, (src, dst)) in enumerate(zip(SIDES, buffers))
        ]

    def first_copies(t):
        faces = [(a.at[s, r], b.at[s, r]) for a, b in ((xs, xr), (ys, yr)) for s, r in (
            (0, pl.ds(112, 96) if t else pl.ds(0, 96)), (1, pl.ds(112, 96) if t else pl.ds(0, 112)))]
        r = pl.ds(16, 8) if t else pl.ds(0, 16)
        return copies(ss.at[t], rs.at[t], faces + [(ds.at[s, r], dr.at[s, r]) for s in range(4)])

    def z_copies(t):
        r = pl.ds(2, 3) if t else pl.ds(0, 2)
        return [
            pltpu.make_async_remote_copy(
                src_ref=zs.at[s, r], dst_ref=zr.at[s, r], send_sem=zss.at[t, s], recv_sem=zrs.at[t, s],
                device_id={"gz": iz + (2 * s - 1)}, device_id_type=MESH)
            for s in (0, 1)
        ]

    firsts = [first_copies(t) for t in (0, 1)]
    to_z = [z_copies(t) for t in (0, 1)]
    from_z = (jnp.logical_not(high_z), jnp.logical_not(low_z))

    def send_first(t):
        for s in (0, 1):
            @pl.when(from_z[1 - s])
            def _(s=s):
                to_z[t][s].start()
        for side, copy in zip(SIDES, firsts[t]):
            @pl.when(has(*side))
            def _(copy=copy):
                copy.start()

    slow = border | bridge

    @pl.when(jnp.logical_not(slow))
    def _():
        pl.semaphore_wait(barrier, expected)
        send_first(0)

    @pl.loop(1, SRC // KC)
    def _(chunk):
        acc[...] += scattered(pl.ds(pl.multiple_of(chunk * KC, KC), KC))

    sheets = [(acc[n * TZ:(n + 1) * TZ, :] + acc[(STEPS + n) * TZ:(STEPS + n + 1) * TZ, :]).T for n in range(STEPS)]
    for x in range(TX):
        at = slice(x * TY, (x + 1) * TY)
        to = slice(row_of(x, 0), row_of(x, 0) + TY)
        added = [sheet[at, :] for sheet in sheets]
        p = fv[0, at, :]
        vx, vy, vz = (fv[k, at, :] for k in (1, 2, 3))
        gone = vx + (vy - jnp.where(sub == 0, 0.0, pltpu.roll(vy, 1, 0)))
        gone = gone + (vz - jnp.where(lane == 0, 0.0, pltpu.roll(vz, 1, 1)))
        if x:
            gone = gone - fv[1, (x - 1) * TY:x * TY, :]
        cm[to, :] = added[0] - 0.5 * (gone + p)
        d2m[to, :] = added[1] - added[0]
        d3m[to, :] = added[2] - added[1]
        d4[at, :] = added[3] - added[2]

    for face in range(4):
        along_x, s = face < 2, face % 2
        cell = inner(s)
        to = (xs if along_x else ys).at[s]
        for i, (f, k) in enumerate(LATER):
            to[112 + i * 16:128 + i * 16, :] = ext[f][plane_at(along_x, cell(k)), :]
    for s, (sx, sy) in enumerate(DIAGS):
        cx, cy = inner(up(sx)), inner(up(sy))
        for i, (f, a, b) in enumerate(LATER_CORNER):
            r = row_of(cx(a), cy(b))
            ds[s, 16 + i:17 + i, :] = ext[f][r:r + 1, :]
    for f in ALONG_Z[1:]:
        pack_z(f)

    @pl.when(slow)
    def _():
        pl.semaphore_wait(barrier, expected)

        @pl.when(bridge)
        def _():
            pl.semaphore_signal(met, inc=1, device_id=across, device_id_type=MESH)

        send_first(0)

    send_first(1)

    for d in range(OWN):
        cells = cell_r[d:d + 1, :]
        span = slice(d * CAP, (d + 1) * CAP)
        one = jnp.where(iota((ROWS, 1), 0) == cells // TZ, 1.0, 0.0).astype(BF)
        cone[0:ROWS, span] = one
        cone[ROWS:2 * ROWS, span] = one
        zsel[:, span] = jnp.where(iota((TZ, 1), 0) == cells % TZ, 1.0, 0.0).astype(F32)

    eye = iota((TONES, TONES), 0) == iota((TONES, TONES), 1)
    freq = jnp.sum(jnp.where(eye, tone_r[...], 0.0), axis=1, keepdims=True)
    freq = jnp.concatenate([freq, freq], axis=0)
    angle = freq * lane.astype(F32)
    basis = half_wave(angle, jnp.where(iota((NB, 1), 0) < TONES, 0.5, 0.0).astype(F32)) * 0.125
    for n in range(STEPS):
        bt[n * NB:(n + 1) * NB, :] = jnp.broadcast_to(basis[:, HIST + n:HIST + n + 1], (NB, CAP))
    held = iota((OWN, OWN), 0) == iota((OWN, OWN), 1)
    counts = jnp.sum(jnp.where(held, count_r[...].astype(F32), 0.0), axis=1, keepdims=True)
    live = jnp.where(lane.astype(F32) < counts, 1.0, 0.0).astype(F32)
    bt_out = pltpu.make_async_copy(bt, bt_h, osem.at[3])
    bt_out.start()

    @pl.when(bridge)
    def _():
        pl.semaphore_wait(met, 1)
        for mate in mates:
            pl.semaphore_signal(all_in, inc=1, device_id=mate, device_id_type=MESH)

    for i in range(4):
        sx, sy = SIDES[i]

        @pl.when(has(-sx, -sy))
        def _(i=i):
            along_x, s = i < 2, i % 2
            out = outer(s)
            firsts[0][i].wait_recv()
            got = (xr if along_x else yr).at[s]
            for k in range(4):
                ext["p"][plane_at(along_x, out(k)), :] = got[k * 16:(k + 1) * 16, :]
            beside, through = (vys, vxs) if along_x else (vxs, vys)
            ends = got[64:80, :]
            for k in range(3):
                vzm[plane_at(along_x, out(k)), :] = pltpu.roll(ends, TZ - 1 - k, 1)
                beside[1, 4 + out(k):5 + out(k), :] = got[80 + k:81 + k, :]
            if s == 1:
                through[0, 4:20, :] = got[96:112, :]

    for i in range(4, 8):
        sx, sy = SIDES[i]

        @pl.when(has(-sx, -sy))
        def _(i=i, sx=sx, sy=sy):
            ox, oy = outer(up(sx)), outer(up(sy))
            firsts[0][i].wait_recv()
            for j, (f, a, b) in enumerate(CORNER):
                r = row_of(ox(a), oy(b))
                ext[f][r:r + 1, :] = dr[i - 4, j:j + 1, :]
            for k in range(3):
                if sx > 0:
                    vxs[0, 4 + oy(k):5 + oy(k), :] = dr[i - 4, 9 + k:10 + k, :]
                if sy > 0:
                    vys[0, 4 + ox(k):5 + ox(k), :] = dr[i - 4, 12 + k:13 + k, :]

    for i in range(4):
        sx, sy = SIDES[i]

        @pl.when(has(-sx, -sy))
        def _(i=i):
            along_x, s = i < 2, i % 2
            out = outer(s)
            firsts[1][i].wait_recv()
            got = (xr if along_x else yr).at[s]
            for j, (f, k) in enumerate(LATER):
                ext[f][plane_at(along_x, out(k)), :] = got[112 + j * 16:128 + j * 16, :]

    for i in range(4, 8):
        sx, sy = SIDES[i]

        @pl.when(has(-sx, -sy))
        def _(i=i, sx=sx, sy=sy):
            ox, oy = outer(up(sx)), outer(up(sy))
            firsts[1][i].wait_recv()
            for j, (f, a, b) in enumerate(LATER_CORNER):
                r = row_of(ox(a), oy(b))
                ext[f][r:r + 1, :] = dr[i - 4, 16 + j:17 + j, :]

    def borders(change, vx, vy):
        for k, x in ((0, 0), (1, TX)):
            r = row_of(x, -4)
            change[r:r + WIDE, :] = change[r:r + WIDE, :] + vx[k]
        for k, y in ((0, 0), (1, TY)):
            r = pl.ds(row_of(-4, y), WIDE, stride=WIDE)
            change[r, :] = change[r, :] + vy[k]

    def mirrors(refs, widths):
        for flag, low, along_x in (
            (low_x, True, True), (high_x, False, True), (low_y, True, False), (high_y, False, False)
        ):
            @pl.when(flag)
            def _(low=low, along_x=along_x):
                def rows(q):
                    return pl.ds(row_of(q, -4), WIDE) if along_x else pl.ds(row_of(-4, q), WIDE, stride=WIDE)

                for f, width in widths:
                    for k in range(width):
                        if low:
                            refs[f][rows(-1 - k), :] = refs[f][rows(k), :]
                        elif k == 0:
                            refs[f][rows(TX), :] = jnp.zeros((WIDE, TZ), F32)
                        else:
                            refs[f][rows(TX + k), :] = -refs[f][rows(TX - k), :]

    borders(cm, vxs, vys)
    mirrors(ext, WIDTHS + (("v", 3),))

    for s in (0, 1):
        @pl.when(from_z[s])
        def _(s=s):
            to_z[0][s].wait_recv()
            to_z[1][s].wait_recv()

    place = (lane + 4) % 8

    def joined(own, from_low, from_high, skip):
        below = jnp.zeros((GROUP, TZ), F32)
        above = jnp.zeros((GROUP, TZ), F32)
        for k in range(4):
            if not (skip and k == 3):
                below = jnp.where(place == 3 - k, roll_lanes(own, -(2 * k + 1)), below)
            if k:
                above = jnp.where(place == 4 + k, -roll_lanes(own, 2 * k), above)
        return jnp.where(
            place < 4, jnp.where(low_z, below, from_low), jnp.where(high_z, above, from_high))

    for f in ALONG_Z:
        i = Z_SLOT[f]
        lows, highs = zr[1, i], zr[0, i]
        for odd in (0, 1):
            merged = joined(
                zown[2 * i + odd], roll_lanes(lows, -4 - 4 * odd), roll_lanes(highs, -4 * odd), f == "c")
            for u in range(16):
                g = MAIN_GROUPS[2 * u + odd]
                value = roll_lanes(merged, -8 * u)
                ring[f][g * 8:g * 8 + 8, :] = value
                if f == "c":
                    vzq[g * 8:g * 8 + 8, :] = roll_lanes(value, 3)
    merged = joined(zown[2], zr[1, 1], zr[0, 1], False)
    for u in range(4):
        (vxq, vyq)[u // 2][1, 4 + 8 * (u % 2):12 + 8 * (u % 2), :] = roll_lanes(merged, -8 * u)

    for face in range(4):
        along_x, s = face < 2, face % 2
        cell = inner(s)
        beside, through = (vyq, vxq) if along_x else (vxq, vyq)
        for k in range(3):
            spare[face, k:k + 1, :] = beside[1, 4 + cell(k):5 + cell(k), :]
        planes = [ring[f][plane_at(along_x, cell(k)), :] for f, k in RING_PLANES] + [spare[face]]
        if s == 1:
            planes.append(through[1, 4:20, :])
        packed = jnp.zeros((TY, TZ), F32)
        for u, value in enumerate(planes):
            packed = jnp.where(slot(u), roll_lanes(value, 8 * u), packed)
        qs[face] = packed
    for s, (sx, sy) in enumerate(DIAGS):
        cx, cy = inner(up(sx)), inner(up(sy))
        for i, (f, a, b) in enumerate(RING_CORNER):
            r = row_of(cx(a), cy(b))
            es[s, i:i + 1, :] = ring[f][r:r + 1, :]
        for k in range(2):
            es[s, 8 + k:9 + k, :] = vxq[1, 4 + cy(k):5 + cy(k), :]
            es[s, 10 + k:11 + k, :] = vyq[1, 4 + cx(k):5 + cx(k), :]
    seconds = copies(qss, qrs, [(qs.at[s], qr.at[s]) for s in range(4)] + [(es.at[s], er.at[s]) for s in range(4)])
    for side, copy in zip(SIDES, seconds):
        @pl.when(has(*side))
        def _(copy=copy):
            copy.start()

    for i in range(4):
        sx, sy = SIDES[i]

        @pl.when(has(-sx, -sy))
        def _(i=i):
            along_x, s = i < 2, i % 2
            out = outer(s)
            seconds[i].wait_recv()
            got = qr[i]
            for u, (f, k) in enumerate(RING_PLANES):
                ring[f][plane_at(along_x, out(k)), :] = roll_lanes(got, -8 * u)
            beside, through = (vyq, vxq) if along_x else (vxq, vyq)
            last = len(RING_PLANES)
            side_rows = roll_lanes(got, -8 * last)
            for k in range(3):
                beside[1, 4 + out(k):5 + out(k), :] = side_rows[k:k + 1, :]
            if s == 1:
                through[0, 4:20, :] = roll_lanes(got, -8 * (last + 1))

    for i in range(4, 8):
        sx, sy = SIDES[i]

        @pl.when(has(-sx, -sy))
        def _(i=i, sx=sx, sy=sy):
            ox, oy = outer(up(sx)), outer(up(sy))
            seconds[i].wait_recv()
            for j, (f, a, b) in enumerate(RING_CORNER):
                r = row_of(ox(a), oy(b))
                ring[f][r:r + 1, :] = er[i - 4, j:j + 1, :]
            for k in range(2):
                if sx > 0:
                    vxq[0, 4 + oy(k):5 + oy(k), :] = er[i - 4, 8 + k:9 + k, :]
                if sy > 0:
                    vyq[0, 4 + ox(k):5 + ox(k), :] = er[i - 4, 10 + k:11 + k, :]

    borders(cq, vxq, vyq)
    mirrors(ring, RING_WIDTHS)

    for g in range(4, 69):
        at = slice(g * 8, g * 8 + 8)
        cm[at, :] = cm[at, :] + roll_lanes(jnp.where(lane == TZ - 1, vzq[at, :], 0.0), 1)
        if 7 <= g < 66:
            flow = roll_lanes(jnp.where(lane == TZ - 1, vzm[at, :], 0.0), 1)
            cq[at, :] = cq[at, :] + jnp.where(high_z, 0.0, flow)

    for n in range(STEPS):
        d_main = (cm, d2m, d3m, d4)[n]
        d_ring = (cq, d2q, d3q, None)[n]
        main_span = (range(4, 69), range(7, 66), range(10, 63), [g for g in range(13, 60) if g % 3])[n]
        ring_span = (range(7, 66), range(10, 63), range(13, 60), ())[n]
        for g in main_span:
            at = slice(g * 8, g * 8 + 8)
            here, ghost = pm[n, at, :], pq[n, at, :]

            def stepped(ref, d, here, other):
                sums = (ref[n, g * 8 - WIDE:g * 8 - WIDE + 8, :] + ref[n, g * 8 + WIDE:g * 8 + WIDE + 8, :]) + (
                    ref[n, g * 8 - 1:g * 8 + 7, :] + ref[n, g * 8 + 1:g * 8 + 9, :])
                back = pltpu.roll(jnp.where(lane == TZ - 1, other, here), 1, 1)
                fore = pltpu.roll(jnp.where(lane == 0, other, here), TZ - 1, 1)
                new = d + 0.25 * (sums + (back + fore))
                return new if n == 0 else new + (0.5 * here - ref[n - 1, at, :])

            if n < STEPS - 1:
                pm[n + 1, at, :] = stepped(pm, d_main[at, :], here, ghost)
                if g in ring_span:
                    pq[n + 1, at, :] = stepped(pq, d_ring[at, :], ghost, here)
            else:
                x, half = divmod(g - 13, 3)
                own = slice(x * TY + half * 8, x * TY + half * 8 + 8)
                plast[own, :] = stepped(pm, d4[own, :], here, ghost)
        new = plast[...] if n == STEPS - 1 else jnp.concatenate(
            [pm[n + 1, row_of(x, 0):row_of(x, 0) + TY, :] for x in range(TX)], axis=0)
        both[n * TZ:(n + 1) * TZ, :] = jnp.concatenate(split(new.T), axis=1)

        if n >= 2:
            first = 0 if n == 2 else 3
            for d in range(0, OWN, 2):
                span = slice(d * CAP, (d + 2) * CAP)
                seen = dot_nn(both[first * TZ:(n + 1) * TZ, :], cone[:, span])
                for m in range(first, n + 1):
                    part = seen[(m - first) * TZ:(m - first + 1) * TZ, :]
                    got = jnp.sum(part * zsel[:, span], axis=0, keepdims=True)
                    sb[d, m:m + 1, :] = got[:, :CAP]
                    sb[d + 1, m:m + 1, :] = got[:, CAP:]

    def block_copy(k):
        target = lax.rem(iz + k, OWN)
        return pltpu.make_async_remote_copy(
            src_ref=sb.at[target],
            dst_ref=rb.at[iz],
            send_sem=ass, recv_sem=ars, device_id={"gz": target}, device_id_type=MESH)

    @pl.when(jnp.logical_not(bridge))
    def _():
        pl.semaphore_wait(all_in, 1)

    sends = [block_copy(k) for k in range(1, OWN)]
    for k in (8, 7, 9, 6, 10, 5, 11, 4, 12, 3, 13, 2, 14, 1, 15):
        sends[k - 1].start()
    rb[iz] = sb[iz]

    outs = [pltpu.make_async_copy(plast, fout_h.at[0], osem.at[0])]
    outs[0].start()
    for side, *three in zip(SIDES, *firsts, seconds):
        @pl.when(has(*side))
        def _(three=three):
            for copy in three:
                copy.wait_send()
    for s in (0, 1):
        @pl.when(from_z[1 - s])
        def _(s=s):
            to_z[0][s].wait_send()
            to_z[1][s].wait_send()
    for g in range(13, 64):
        at = slice(g * 8, g * 8 + 8)
        sm[at, :] = (pm[0, at, :] + pm[1, at, :]) + (pm[2, at, :] + pm[3, at, :])
        sq[at, :] = (pq[0, at, :] + pq[1, at, :]) + (pq[2, at, :] + pq[3, at, :])
    for x in range(TX):
        at = slice(x * TY, (x + 1) * TY)
        r = row_of(x, 0)
        own = sm[r:r + TY, :]
        fv[1, at, :] = fv[1, at, :] - 0.5 * (sm[r + WIDE:r + WIDE + TY, :] - own)
        fv[2, at, :] = fv[2, at, :] - 0.5 * (sm[r + 1:r + 1 + TY, :] - own)
        fore = pltpu.roll(jnp.where(lane == 0, sq[r:r + TY, :], own), TZ - 1, 1)
        fv[3, at, :] = fv[3, at, :] - 0.5 * (fore - own)
    outs.append(pltpu.make_async_copy(fv.at[pl.ds(1, 3)], fout_h.at[pl.ds(1, 3)], osem.at[1]))
    outs[1].start()

    hist_load.wait()
    hv[HIST * OWN:, :] = jnp.zeros((STEPS * OWN, CAP), F32)
    bh, bl = split(basis)
    lhs = jnp.concatenate([bh, bl, bh], axis=1)
    for e in range(0, OWN, 2):
        hh, hl = split(jnp.concatenate(
            [hv[pl.ds(e, HIST + STEPS, stride=OWN), :], hv[pl.ds(e + 1, HIST + STEPS, stride=OWN), :]], axis=1))
        part = dot_nn(lhs, jnp.concatenate([hh, hh, hl], axis=0))
        ov[pl.ds(e, NB, stride=OWN), :] = part[:, :CAP] * live[e:e + 1]
        ov[pl.ds(e + 1, NB, stride=OWN), :] = part[:, CAP:] * live[e + 1:e + 2]
    ov_out = pltpu.make_async_copy(ov, cout_h, osem.at[2])
    ov_out.start()

    every = pltpu.make_async_remote_copy(
        src_ref=sb.at[pl.ds(0, OWN - 1)], dst_ref=rb.at[pl.ds(0, OWN - 1)], send_sem=ass, recv_sem=ars,
        device_id={"gz": lax.rem(iz + 1, OWN)}, device_id_type=MESH)
    every.wait_recv()
    for n in range(STEPS):
        for e in range(OWN):
            hb[n * OWN + e:n * OWN + e + 1, :] = rb[e, n:n + 1, :] * live[e:e + 1, :]
    outs.append(pltpu.make_async_copy(hb, heard_h, osem.at[4]))
    outs[-1].start()
    every.wait_send()
    for copy in outs + [bt_out, ov_out]:
        copy.wait()


PARTS = 4
PER = NB // PARTS


def finish(fields_h, part_h, heard_h, bt_h, fout_h, cout_h, fv, ov, hb, bt, sems, fsems):
    pieces = [pl.ds(k * PER * OWN, PER * OWN) for k in range(PARTS)]
    first = [pltpu.make_async_copy(heard_h, hb, sems.at[0]), pltpu.make_async_copy(bt_h, bt, sems.at[1])]
    loads = [pltpu.make_async_copy(part_h.at[r], ov.at[r], sems.at[2 + k]) for k, r in enumerate(pieces)]
    stores = [pltpu.make_async_copy(ov.at[r], cout_h.at[r], sems.at[2 + PARTS + k]) for k, r in enumerate(pieces)]
    gets = [pltpu.make_async_copy(fields_h.at[k], fv.at[k], fsems.at[k]) for k in range(4)]
    puts = [pltpu.make_async_copy(fv.at[k], fout_h.at[k], fsems.at[4 + k]) for k in range(4)]
    for copy in first + loads + gets:
        copy.start()
    for copy in first:
        copy.wait()
    heard = [hb[n * OWN:(n + 1) * OWN, :] for n in range(STEPS)]
    for k in range(PARTS):
        loads[k].wait()
        for j in range(k * PER, (k + 1) * PER):
            at = slice(j * OWN, (j + 1) * OWN)
            term = ov[at, :]
            for n in range(STEPS):
                term = term + bt[n * NB + j:n * NB + j + 1, :] * heard[n]
            ov[at, :] = term
        stores[k].start()
        gets[k].wait()
        puts[k].start()
    for copy in stores + puts:
        copy.wait()


def body(
    fields, tone_freq, mode_freq, mode_amp, mode_map, src_pos, src_id, src_gain, sample_cell, sample_count, history
):
    hbm = pl.BlockSpec(memory_space=pl.ANY)
    made = pl.pallas_call(
        kernel,
        out_shape=(
            jax.ShapeDtypeStruct((4, ROWS, TZ), F32),
            jax.ShapeDtypeStruct((NB * OWN, CAP), F32),
            jax.ShapeDtypeStruct((STEPS * OWN, CAP), F32),
            jax.ShapeDtypeStruct((STEPS * NB, CAP), F32),
        ),
        in_specs=[hbm] * 11,
        out_specs=(hbm,) * 4,
        scratch_shapes=[
            pltpu.VMEM((1, TONES), F32),
            pltpu.VMEM((1, MODES), F32),
            pltpu.VMEM((1, MODES), F32),
            pltpu.VMEM((1, MODES), jnp.int32),
            pltpu.VMEM((3, SRC), jnp.int32),
            pltpu.VMEM((1, SRC), jnp.int32),
            pltpu.VMEM((1, SRC), F32),
            pltpu.VMEM((OWN, CAP), jnp.int32),
            pltpu.VMEM((1, OWN), jnp.int32),
            pltpu.VMEM((4, ROWS, TZ), F32),
            pltpu.VMEM(((HIST + STEPS) * OWN, CAP), F32),
            pltpu.VMEM((STEPS, EXT, TZ), F32),
            pltpu.VMEM((STEPS, EXT, TZ), F32),
            pltpu.VMEM((EXT, TZ), F32),
            pltpu.VMEM((EXT, TZ), F32),
            pltpu.VMEM((EXT, TZ), F32),
            pltpu.VMEM((EXT, TZ), F32),
            pltpu.VMEM((EXT, TZ), F32),
            pltpu.VMEM((EXT, TZ), F32),
            pltpu.VMEM((ROWS, TZ), F32),
            pltpu.VMEM((EXT, TZ), F32),
            pltpu.VMEM((EXT, TZ), F32),
            pltpu.VMEM((2, WIDE, TZ), F32),
            pltpu.VMEM((2, WIDE, TZ), F32),
            pltpu.VMEM((2, WIDE, TZ), F32),
            pltpu.VMEM((2, WIDE, TZ), F32),
            pltpu.VMEM((ROWS, TZ), F32),
            pltpu.VMEM((EXT, TZ), F32),
            pltpu.VMEM((EXT, TZ), F32),
            pltpu.VMEM((8, 2048), F32),
            pltpu.VMEM((8, SRC), F32),
            pltpu.VMEM((1, SRC), F32),
            pltpu.VMEM((1, SRC), F32),
            pltpu.VMEM((2 * STEPS * TZ, ROWS), F32),
            pltpu.VMEM((2 * ROWS, SLOTS), BF),
            pltpu.VMEM((TZ, SLOTS), F32),
            pltpu.VMEM((STEPS * TZ, 2 * ROWS), BF),
            pltpu.VMEM((NB * OWN, CAP), F32),
            pltpu.VMEM((STEPS * NB, CAP), F32),
            pltpu.VMEM((OWN, STEPS, CAP), F32),
            pltpu.VMEM((OWN, STEPS, CAP), F32),
            pltpu.VMEM((STEPS * OWN, CAP), F32),
            pltpu.VMEM((2, 208, TZ), F32),
            pltpu.VMEM((2, 208, TZ), F32),
            pltpu.VMEM((2, 208, TZ), F32),
            pltpu.VMEM((2, 208, TZ), F32),
            pltpu.VMEM((4, 24, TZ), F32),
            pltpu.VMEM((4, 24, TZ), F32),
            pltpu.VMEM((2, 5, GROUP, TZ), F32),
            pltpu.VMEM((2, 5, GROUP, TZ), F32),
            pltpu.VMEM((4, TY, TZ), F32),
            pltpu.VMEM((4, TY, TZ), F32),
            pltpu.VMEM((4, TY, TZ), F32),
            pltpu.VMEM((4, TY, TZ), F32),
            pltpu.VMEM((4, TY, TZ), F32),
            pltpu.VMEM((10, GROUP, TZ), F32),
            pltpu.SemaphoreType.DMA((9,)),
            pltpu.SemaphoreType.DMA((4,)),
            pltpu.SemaphoreType.DMA,
            pltpu.SemaphoreType.DMA((5,)),
            pltpu.SemaphoreType.DMA((2, 8)),
            pltpu.SemaphoreType.DMA((2, 8)),
            pltpu.SemaphoreType.DMA((2, 2)),
            pltpu.SemaphoreType.DMA((2, 2)),
            pltpu.SemaphoreType.DMA((8,)),
            pltpu.SemaphoreType.DMA((8,)),
            pltpu.SemaphoreType.DMA,
            pltpu.SemaphoreType.DMA,
            pltpu.SemaphoreType.REGULAR,
            pltpu.SemaphoreType.REGULAR,
        ],
        compiler_params=pltpu.CompilerParams(
            collective_id=0, has_side_effects=True, vmem_limit_bytes=63 * 1024 * 1024
        ),
    )(
        fields.reshape(4, ROWS, TZ),
        tone_freq.reshape(1, TONES),
        mode_freq.reshape(1, MODES),
        mode_amp.reshape(1, MODES),
        mode_map.reshape(1, MODES),
        src_pos,
        src_id.reshape(1, SRC),
        src_gain.reshape(1, SRC),
        sample_cell.reshape(OWN, CAP),
        sample_count.reshape(1, OWN),
        history.reshape(HIST * OWN, CAP),
    )
    fields_out, coefficients = pl.pallas_call(
        finish,
        out_shape=(
            jax.ShapeDtypeStruct((4, ROWS, TZ), F32),
            jax.ShapeDtypeStruct((NB * OWN, CAP), F32),
        ),
        in_specs=[hbm] * 4,
        out_specs=(hbm,) * 2,
        scratch_shapes=[
            pltpu.VMEM((4, ROWS, TZ), F32),
            pltpu.VMEM((NB * OWN, CAP), F32),
            pltpu.VMEM((STEPS * OWN, CAP), F32),
            pltpu.VMEM((STEPS * NB, CAP), F32),
            pltpu.SemaphoreType.DMA((2 + 2 * PARTS,)),
            pltpu.SemaphoreType.DMA((8,)),
        ],
        compiler_params=pltpu.CompilerParams(vmem_limit_bytes=63 * 1024 * 1024),
    )(*made)
    return fields_out.reshape(fields.shape), coefficients.reshape(NB, 1, 1, 1, OWN, CAP)


def solution(mesh):
    in_specs = (
        P(None, "gx", "gy", "gz"),
        P(),
        P(),
        P(),
        P(),
        P(),
        P(),
        P(),
        P("gx", "gy", "gz", None, None),
        P("gx", "gy", None, "gz"),
        P(None, "gx", "gy", "gz", None, None),
    )
    out_specs = (P(None, "gx", "gy", "gz"), P(None, "gx", "gy", "gz", None, None))
    return jax.shard_map(body, mesh=mesh, in_specs=in_specs, out_specs=out_specs, check_vma=False)
```

```python
import jax
import jax.numpy as jnp
import numpy as np
from jax import lax
from jax.experimental import pallas as pl
from jax.experimental.pallas import tpu as pltpu
from jax.sharding import PartitionSpec as P

STEPS = 4
HIST = 124
SOURCES = 48
TONES = 48
MODES = 2000
SRC = 4096
TX, TY, TZ = 16, 16, 128
ROWS = TX * TY
OWN = 16
CAP = 128
SLOTS = OWN * CAP
NB = 2 * TONES
KC = 1024
F32 = jnp.float32
BF = jnp.bfloat16
MESH = pl.DeviceIdType.MESH
ONE = np.asarray(1, BF)
ZERO = np.asarray(0, BF)


def split(values):
    high = values.astype(BF)
    return high, (values - high.astype(F32)).astype(BF)


def dot_nn(a, b):
    return lax.dot_general(a, b, (((1,), (0,)), ((), ())), preferred_element_type=F32)


def dot_nt(a, b):
    return lax.dot_general(a, b, (((1,), (1,)), ((), ())), preferred_element_type=F32)


def half_wave(x, half):
    k = jnp.floor(x * 0.3183098861837907 + (0.5 - half))
    h = k + half
    r = x - h * 3.140625
    r = r - h * 0.0009670257568359375
    r = r - h * 6.2771141529083251953e-07
    q = r * r
    s = -2.505210838544172e-08
    for c in (2.7557319223985893e-06, -1.984126984126984e-04, 8.333333333333333e-03, -0.16666666666666666):
        s = s * q + c
    s = r + r * q * s
    sign = 1.0 - 2.0 * (k - 2.0 * jnp.floor(k * 0.5))
    return jnp.where(half > 0.25, -sign, sign) * s


def iota(shape, dim):
    return lax.broadcasted_iota(jnp.int32, shape, dim)


GROUP = 8
HALF = 8
BRIDGE = 3
WIDE = 24
EXT = 584
WIDTHS = (("p", 4), ("c", 3), ("d2", 2), ("d3", 1))
LATER = [(f, k) for f, width in WIDTHS[1:] for k in range(width)]
RING_WIDTHS = (("p", 3), ("c", 2), ("d2", 1), ("v", 3))
RING_PLANES = [(f, k) for f, width in RING_WIDTHS for k in range(width)]
DIAGS = ((-1, -1), (-1, 1), (1, -1), (1, 1))
SIDES = ((-1, 0), (1, 0), (0, -1), (0, 1)) + DIAGS
CORNER = [("p", i, j) for i in range(3) for j in range(3 - i)] + [("v", i, j) for i in range(2) for j in range(2 - i)]
LATER_CORNER = [("c", i, j) for i in range(2) for j in range(2 - i)] + [("d2", 0, 0)]
RING_CORNER = [(f, i, j) for f in ("p", "v") for i in range(2) for j in range(2 - i)] + [("c", 0, 0)]
ALONG_Z = ("p", "c", "d2", "d3")
Z_SLOT = {"p": 0, "c": 2, "d2": 3, "d3": 4}
MAIN_GROUPS = [g for g in range(13, 60) if g % 3]


def row_of(x, y):
    return 8 + WIDE * (x + 4) + y


def roll_lanes(v, by):
    return pltpu.roll(v, by % TZ, 1) if by % TZ else v


def kernel(
    fields_h, tone_h, mfreq_h, mamp_h, mmap_h, spos_h, sid_h, sgain_h, cell_h, count_h, hist_h,
    fout_h, cout_h, heard_h, bt_h,
    tone_r, mfreq_r, mamp_r, mmap_r, spos_r, sid_r, sgain_r, cell_r, count_r,
    fv, hv, pm, pq, cm, cq, d2m, d2q, d3m, d3q, d4, vzm, vzq, vxs, vys, vxq, vyq, plast, sm, sq,
    ms, wv, srow, scol, acc, cone, zsel, both, ov, bt, sb, rb, hb,
    xs, xr, ys, yr, ds, dr, zs, zr, qs, qr, es, er, spare, zown,
    isem, fsem, hsem, osem, ss, rs, zss, zrs, qss, qrs, ass, ars, met, all_in,
):
    ix = lax.axis_index("gx")
    iy = lax.axis_index("gy")
    iz = lax.axis_index("gz")
    low_x, high_x = ix == 0, ix == 3
    low_y, high_y = iy == 0, iy == 3
    low_z, high_z = iz == 0, iz == OWN - 1

    small = [
        pltpu.make_async_copy(src, dst, isem.at[k])
        for k, (src, dst) in enumerate((
            (mfreq_h, mfreq_r), (mamp_h, mamp_r), (mmap_h, mmap_r), (sid_h, sid_r), (sgain_h, sgain_r),
            (spos_h, spos_r), (tone_h, tone_r), (cell_h, cell_r), (count_h, count_r)))
    ]
    for copy in small:
        copy.start()
    loads = [pltpu.make_async_copy(fields_h.at[k], fv.at[k], fsem.at[k]) for k in range(4)]
    for copy in loads:
        copy.start()
    def has(sx, sy):
        ok = None
        for s, low, high in ((sx, low_x, high_x), (sy, low_y, high_y)):
            if s:
                here = jnp.logical_not(low if s < 0 else high)
                ok = here if ok is None else ok & here
        return ok

    def at_side(sx, sy):
        where = {}
        if sx:
            where["gx"] = ix + sx
        if sy:
            where["gy"] = iy + sy
        return where

    barrier = pltpu.get_barrier_semaphore()
    half = (iz // HALF) * HALF
    bridge = (iz == BRIDGE) | (iz == BRIDGE + HALF)
    border = (iz == HALF - 1) | (iz == HALF)
    across = {"gz": lax.rem(iz + HALF, OWN)}
    mates = [{"gz": half + lax.rem(iz - half + k, HALF)} for k in range(1, HALF)]

    @pl.when(border)
    def _():
        pl.semaphore_signal(barrier, inc=1, device_id={"gz": OWN - 1 - iz}, device_id_type=MESH)

    @pl.when(bridge)
    def _():
        pl.semaphore_signal(barrier, inc=1, device_id=across, device_id_type=MESH)

    for mate in mates:
        pl.semaphore_signal(barrier, inc=1, device_id=mate, device_id_type=MESH)
    expected = HALF - 1 + jnp.where(border, 1, 0) + jnp.where(bridge, 1, 0)
    for side in SIDES:
        expected = expected + jnp.where(has(*side), 1, 0)

        @pl.when(has(*side))
        def _(side=side):
            pl.semaphore_signal(barrier, inc=1, device_id=at_side(*side), device_id_type=MESH)

    hist_load = pltpu.make_async_copy(hist_h, hv.at[pl.ds(0, HIST * OWN)], hsem)
    hist_load.start()

    lane = iota((1, TZ), 1)
    sub = iota((TY, 1), 0)
    row8 = iota((8, 1), 0)
    ext = {"p": pm.at[0], "c": cm, "v": vzm, "d2": d2m, "d3": d3m}
    ring = {"p": pq.at[0], "c": cq, "d2": d2q, "d3": d3q, "v": vzq}
    for ref in (vxs, vys, vxq, vyq, spare):
        ref[...] = jnp.zeros_like(ref)

    ms[...] = jnp.zeros_like(ms)
    for copy in small:
        copy.wait()
    ms[0:1, 0:MODES] = mfreq_r[...]
    ms[1:2, 0:MODES] = mamp_r[...]
    ms[2:3, 0:MODES] = mmap_r[...].astype(F32)
    moment = (HIST + row8 % STEPS).astype(F32)
    waves = ms[1:2, :] * half_wave(ms[0:1, :] * moment, jnp.zeros((8, 1), F32))
    high = waves.astype(BF).astype(F32)
    waves = jnp.where(row8 < STEPS, high, waves - high).astype(BF)
    pick = jnp.where(iota((SOURCES, 1), 0).astype(F32) == ms[2:3, :], 1.0, 0.0).astype(BF)
    drive = dot_nt(waves, pick)
    drive = drive + pltpu.roll(drive, 4, 0)
    high = drive.astype(BF).astype(F32)
    drive = jnp.where(row8 < STEPS, high, drive - high).astype(BF)
    pick = jnp.where(iota((SOURCES, 1), 0) == sid_r[...], 1.0, 0.0).astype(BF)
    weight = dot_nn(drive, pick)
    weight = (weight + pltpu.roll(weight, 4, 0)) * sgain_r[...]
    high = weight.astype(BF).astype(F32)
    wv[...] = jnp.where(row8 < STEPS, high, weight - high)
    lx = spos_r[0:1, :] - ix * TX
    ly = spos_r[1:2, :] - iy * TY
    lz = spos_r[2:3, :] - iz * TZ
    inside = (lx >= 0) & (lx < TX) & (ly >= 0) & (ly < TY) & (lz >= 0) & (lz < TZ)
    srow[...] = jnp.where(inside, lx * TY + ly, -1).astype(F32)
    scol[...] = lz.astype(F32)

    def scattered(span):
        a = jnp.where(iota((ROWS, 1), 0).astype(F32).astype(BF) == srow[:, span].astype(BF), ONE, ZERO)
        m = iota((TZ, 1), 0).astype(F32).astype(BF) == scol[:, span].astype(BF)
        b = jnp.concatenate([jnp.where(m, wv[q:q + 1, span].astype(BF), ZERO) for q in range(2 * STEPS)], axis=0)
        return dot_nt(b, a)

    for copy in loads:
        copy.wait()
    for x in range(TX):
        at = slice(x * TY, (x + 1) * TY)
        to = slice(row_of(x, 0), row_of(x, 0) + TY)
        pm[0, to, :] = fv[0, at, :]
        vzm[to, :] = 0.5 * fv[3, at, :]
    vxs[1, 4:20, :] = 0.5 * fv[1, ROWS - TY:ROWS, :]
    vys[1, 4:20, :] = 0.5 * fv[2, pl.ds(TY - 1, TX, stride=TY), :]

    def plane_at(along_x, q):
        return pl.ds(row_of(q, 0), TY) if along_x else pl.ds(row_of(0, q), TX, stride=WIDE)

    def inner(s):
        return (lambda k: k) if s == 0 else (lambda k: TX - 1 - k)

    def outer(s):
        return (lambda k: TX + k) if s == 0 else (lambda k: -1 - k)

    def up(step):
        return 0 if step < 0 else 1

    for face in range(4):
        along_x, s = face < 2, face % 2
        cell = inner(s)
        to = (xs if along_x else ys).at[s]
        for k in range(4):
            to[k * 16:(k + 1) * 16, :] = ext["p"][plane_at(along_x, cell(k)), :]
        ends = jnp.zeros((TY, TZ), F32)
        for k in range(3):
            ends = jnp.where(lane == k, pltpu.roll(vzm[plane_at(along_x, cell(k)), :], k + 1, 1), ends)
        to[64:80, :] = ends
        beside, through = (vys, vxs) if along_x else (vxs, vys)
        for k in range(3):
            to[80 + k:81 + k, :] = beside[1, 4 + cell(k):5 + cell(k), :]
        if s == 1:
            to[96:112, :] = through[1, 4:20, :]
    for s, (sx, sy) in enumerate(DIAGS):
        cx, cy = inner(up(sx)), inner(up(sy))
        for i, (f, a, b) in enumerate(CORNER):
            r = row_of(cx(a), cy(b))
            ds[s, i:i + 1, :] = ext[f][r:r + 1, :]
        for k in range(3):
            ds[s, 9 + k:10 + k, :] = vxs[1, 4 + cy(k):5 + cy(k), :]
            ds[s, 12 + k:13 + k, :] = vys[1, 4 + cx(k):5 + cx(k), :]

    def slot(u):
        return ((lane + 4) % TZ) // 8 == u

    lower = lane % 8 < 4

    def pack_z(f):
        made = []
        for odd in (0, 1):
            packed = jnp.zeros((GROUP, TZ), F32)
            for u in range(16):
                g = MAIN_GROUPS[2 * u + odd]
                value = ext[f][g * 8:g * 8 + 8, :]
                if f == "c":
                    value = jnp.where(lane == TZ - 4, roll_lanes(vzm[g * 8:g * 8 + 8, :], -3), value)
                packed = jnp.where(slot(u), roll_lanes(value, 8 * u), packed)
            made.append(packed)
        one, two = made
        i = Z_SLOT[f]
        zs[0, i] = jnp.where(lower, one, roll_lanes(two, 4))
        zs[1, i] = jnp.where(lower, roll_lanes(one, 4), roll_lanes(two, 8))
        zown[2 * i] = one
        zown[2 * i + 1] = two

    pack_z("p")
    packed = jnp.zeros((GROUP, TZ), F32)
    for u in range(4):
        value = (vxs, vys)[u // 2][1, 4 + 8 * (u % 2):12 + 8 * (u % 2), :]
        packed = jnp.where(slot(u), roll_lanes(value, 8 * u), packed)
    zs[0, 1] = packed
    zs[1, 1] = packed
    zown[2] = packed

    def copies(sends, arrivals, buffers):
        return [
            pltpu.make_async_remote_copy(
                src_ref=src, dst_ref=dst, send_sem=sends.at[i], recv_sem=arrivals.at[i],
                device_id=at_side(*side), device_id_type=MESH)
            for i, (side, (src, dst)) in enumerate(zip(SIDES, buffers))
        ]

    def first_copies(t):
        faces = [(a.at[s, r], b.at[s, r]) for a, b in ((xs, xr), (ys, yr)) for s, r in (
            (0, pl.ds(112, 96) if t else pl.ds(0, 96)), (1, pl.ds(112, 96) if t else pl.ds(0, 112)))]
        r = pl.ds(16, 8) if t else pl.ds(0, 16)
        return copies(ss.at[t], rs.at[t], faces + [(ds.at[s, r], dr.at[s, r]) for s in range(4)])

    def z_copies(t):
        r = pl.ds(2, 3) if t else pl.ds(0, 2)
        return [
            pltpu.make_async_remote_copy(
                src_ref=zs.at[s, r], dst_ref=zr.at[s, r], send_sem=zss.at[t, s], recv_sem=zrs.at[t, s],
                device_id={"gz": iz + (2 * s - 1)}, device_id_type=MESH)
            for s in (0, 1)
        ]

    firsts = [first_copies(t) for t in (0, 1)]
    to_z = [z_copies(t) for t in (0, 1)]
    from_z = (jnp.logical_not(high_z), jnp.logical_not(low_z))

    def send_first(t):
        for s in (0, 1):
            @pl.when(from_z[1 - s])
            def _(s=s):
                to_z[t][s].start()
        for side, copy in zip(SIDES, firsts[t]):
            @pl.when(has(*side))
            def _(copy=copy):
                copy.start()

    slow = border | bridge

    @pl.when(jnp.logical_not(slow))
    def _():
        pl.semaphore_wait(barrier, expected)
        send_first(0)

    acc[...] = scattered(pl.ds(0, KC))

    @pl.loop(1, SRC // KC)
    def _(chunk):
        acc[...] += scattered(pl.ds(pl.multiple_of(chunk * KC, KC), KC))

    sheets = [(acc[n * TZ:(n + 1) * TZ, :] + acc[(STEPS + n) * TZ:(STEPS + n + 1) * TZ, :]).T for n in range(STEPS)]
    for x in range(TX):
        at = slice(x * TY, (x + 1) * TY)
        to = slice(row_of(x, 0), row_of(x, 0) + TY)
        added = [sheet[at, :] for sheet in sheets]
        p = fv[0, at, :]
        vx, vy, vz = (fv[k, at, :] for k in (1, 2, 3))
        gone = vx + (vy - jnp.where(sub == 0, 0.0, pltpu.roll(vy, 1, 0)))
        gone = gone + (vz - jnp.where(lane == 0, 0.0, pltpu.roll(vz, 1, 1)))
        if x:
            gone = gone - fv[1, (x - 1) * TY:x * TY, :]
        cm[to, :] = added[0] - 0.5 * (gone + p)
        d2m[to, :] = added[1] - added[0]
        d3m[to, :] = added[2] - added[1]
        d4[at, :] = added[3] - added[2]

    for face in range(4):
        along_x, s = face < 2, face % 2
        cell = inner(s)
        to = (xs if along_x else ys).at[s]
        for i, (f, k) in enumerate(LATER):
            to[112 + i * 16:128 + i * 16, :] = ext[f][plane_at(along_x, cell(k)), :]
    for s, (sx, sy) in enumerate(DIAGS):
        cx, cy = inner(up(sx)), inner(up(sy))
        for i, (f, a, b) in enumerate(LATER_CORNER):
            r = row_of(cx(a), cy(b))
            ds[s, 16 + i:17 + i, :] = ext[f][r:r + 1, :]
    for f in ALONG_Z[1:]:
        pack_z(f)

    @pl.when(slow)
    def _():
        pl.semaphore_wait(barrier, expected)

        @pl.when(bridge)
        def _():
            pl.semaphore_signal(met, inc=1, device_id=across, device_id_type=MESH)

        send_first(0)

    send_first(1)

    for d in range(OWN):
        cells = cell_r[d:d + 1, :]
        span = slice(d * CAP, (d + 1) * CAP)
        one = jnp.where(iota((ROWS, 1), 0) == cells // TZ, 1.0, 0.0).astype(BF)
        cone[0:ROWS, span] = one
        cone[ROWS:2 * ROWS, span] = one
        zsel[:, span] = jnp.where(iota((TZ, 1), 0) == cells % TZ, 1.0, 0.0).astype(F32)

    eye = iota((TONES, TONES), 0) == iota((TONES, TONES), 1)
    freq = jnp.sum(jnp.where(eye, tone_r[...], 0.0), axis=1, keepdims=True)
    freq = jnp.concatenate([freq, freq], axis=0)
    angle = freq * lane.astype(F32)
    basis = half_wave(angle, jnp.where(iota((NB, 1), 0) < TONES, 0.5, 0.0).astype(F32)) * 0.125
    for n in range(STEPS):
        bt[n * NB:(n + 1) * NB, :] = jnp.broadcast_to(basis[:, HIST + n:HIST + n + 1], (NB, CAP))
    held = iota((OWN, OWN), 0) == iota((OWN, OWN), 1)
    counts = jnp.sum(jnp.where(held, count_r[...].astype(F32), 0.0), axis=1, keepdims=True)
    live = jnp.where(lane.astype(F32) < counts, 1.0, 0.0).astype(F32)
    bt_out = pltpu.make_async_copy(bt, bt_h, osem.at[3])
    bt_out.start()

    @pl.when(bridge)
    def _():
        pl.semaphore_wait(met, 1)
        for mate in mates:
            pl.semaphore_signal(all_in, inc=1, device_id=mate, device_id_type=MESH)

    for i in range(4):
        sx, sy = SIDES[i]

        @pl.when(has(-sx, -sy))
        def _(i=i):
            along_x, s = i < 2, i % 2
            out = outer(s)
            firsts[0][i].wait_recv()
            got = (xr if along_x else yr).at[s]
            for k in range(4):
                ext["p"][plane_at(along_x, out(k)), :] = got[k * 16:(k + 1) * 16, :]
            beside, through = (vys, vxs) if along_x else (vxs, vys)
            ends = got[64:80, :]
            for k in range(3):
                vzm[plane_at(along_x, out(k)), :] = pltpu.roll(ends, TZ - 1 - k, 1)
                beside[1, 4 + out(k):5 + out(k), :] = got[80 + k:81 + k, :]
            if s == 1:
                through[0, 4:20, :] = got[96:112, :]

    for i in range(4, 8):
        sx, sy = SIDES[i]

        @pl.when(has(-sx, -sy))
        def _(i=i, sx=sx, sy=sy):
            ox, oy = outer(up(sx)), outer(up(sy))
            firsts[0][i].wait_recv()
            for j, (f, a, b) in enumerate(CORNER):
                r = row_of(ox(a), oy(b))
                ext[f][r:r + 1, :] = dr[i - 4, j:j + 1, :]
            for k in range(3):
                if sx > 0:
                    vxs[0, 4 + oy(k):5 + oy(k), :] = dr[i - 4, 9 + k:10 + k, :]
                if sy > 0:
                    vys[0, 4 + ox(k):5 + ox(k), :] = dr[i - 4, 12 + k:13 + k, :]

    for i in range(4):
        sx, sy = SIDES[i]

        @pl.when(has(-sx, -sy))
        def _(i=i):
            along_x, s = i < 2, i % 2
            out = outer(s)
            firsts[1][i].wait_recv()
            got = (xr if along_x else yr).at[s]
            for j, (f, k) in enumerate(LATER):
                ext[f][plane_at(along_x, out(k)), :] = got[112 + j * 16:128 + j * 16, :]

    for i in range(4, 8):
        sx, sy = SIDES[i]

        @pl.when(has(-sx, -sy))
        def _(i=i, sx=sx, sy=sy):
            ox, oy = outer(up(sx)), outer(up(sy))
            firsts[1][i].wait_recv()
            for j, (f, a, b) in enumerate(LATER_CORNER):
                r = row_of(ox(a), oy(b))
                ext[f][r:r + 1, :] = dr[i - 4, 16 + j:17 + j, :]

    def borders(change, vx, vy):
        for k, x in ((0, 0), (1, TX)):
            r = row_of(x, -4)
            change[r:r + WIDE, :] = change[r:r + WIDE, :] + vx[k]
        for k, y in ((0, 0), (1, TY)):
            r = pl.ds(row_of(-4, y), WIDE, stride=WIDE)
            change[r, :] = change[r, :] + vy[k]

    def mirrors(refs, widths):
        for flag, low, along_x in (
            (low_x, True, True), (high_x, False, True), (low_y, True, False), (high_y, False, False)
        ):
            @pl.when(flag)
            def _(low=low, along_x=along_x):
                def rows(q):
                    return pl.ds(row_of(q, -4), WIDE) if along_x else pl.ds(row_of(-4, q), WIDE, stride=WIDE)

                for f, width in widths:
                    for k in range(width):
                        if low:
                            refs[f][rows(-1 - k), :] = refs[f][rows(k), :]
                        elif k == 0:
                            refs[f][rows(TX), :] = jnp.zeros((WIDE, TZ), F32)
                        else:
                            refs[f][rows(TX + k), :] = -refs[f][rows(TX - k), :]

    borders(cm, vxs, vys)
    mirrors(ext, WIDTHS + (("v", 3),))

    for s in (0, 1):
        @pl.when(from_z[s])
        def _(s=s):
            to_z[0][s].wait_recv()
            to_z[1][s].wait_recv()

    place = (lane + 4) % 8

    def joined(own, from_low, from_high, skip):
        below = jnp.zeros((GROUP, TZ), F32)
        above = jnp.zeros((GROUP, TZ), F32)
        for k in range(4):
            if not (skip and k == 3):
                below = jnp.where(place == 3 - k, roll_lanes(own, -(2 * k + 1)), below)
            if k:
                above = jnp.where(place == 4 + k, -roll_lanes(own, 2 * k), above)
        return jnp.where(
            place < 4, jnp.where(low_z, below, from_low), jnp.where(high_z, above, from_high))

    for f in ALONG_Z:
        i = Z_SLOT[f]
        lows, highs = zr[1, i], zr[0, i]
        for odd in (0, 1):
            merged = joined(
                zown[2 * i + odd], roll_lanes(lows, -4 - 4 * odd), roll_lanes(highs, -4 * odd), f == "c")
            for u in range(16):
                g = MAIN_GROUPS[2 * u + odd]
                value = roll_lanes(merged, -8 * u)
                ring[f][g * 8:g * 8 + 8, :] = value
                if f == "c":
                    vzq[g * 8:g * 8 + 8, :] = roll_lanes(value, 3)
    merged = joined(zown[2], zr[1, 1], zr[0, 1], False)
    for u in range(4):
        (vxq, vyq)[u // 2][1, 4 + 8 * (u % 2):12 + 8 * (u % 2), :] = roll_lanes(merged, -8 * u)

    for face in range(4):
        along_x, s = face < 2, face % 2
        cell = inner(s)
        beside, through = (vyq, vxq) if along_x else (vxq, vyq)
        for k in range(3):
            spare[face, k:k + 1, :] = beside[1, 4 + cell(k):5 + cell(k), :]
        planes = [ring[f][plane_at(along_x, cell(k)), :] for f, k in RING_PLANES] + [spare[face]]
        if s == 1:
            planes.append(through[1, 4:20, :])
        packed = jnp.zeros((TY, TZ), F32)
        for u, value in enumerate(planes):
            packed = jnp.where(slot(u), roll_lanes(value, 8 * u), packed)
        qs[face] = packed
    for s, (sx, sy) in enumerate(DIAGS):
        cx, cy = inner(up(sx)), inner(up(sy))
        for i, (f, a, b) in enumerate(RING_CORNER):
            r = row_of(cx(a), cy(b))
            es[s, i:i + 1, :] = ring[f][r:r + 1, :]
        for k in range(2):
            es[s, 8 + k:9 + k, :] = vxq[1, 4 + cy(k):5 + cy(k), :]
            es[s, 10 + k:11 + k, :] = vyq[1, 4 + cx(k):5 + cx(k), :]
    seconds = copies(qss, qrs, [(qs.at[s], qr.at[s]) for s in range(4)] + [(es.at[s], er.at[s]) for s in range(4)])
    for side, copy in zip(SIDES, seconds):
        @pl.when(has(*side))
        def _(copy=copy):
            copy.start()

    for i in range(4):
        sx, sy = SIDES[i]

        @pl.when(has(-sx, -sy))
        def _(i=i):
            along_x, s = i < 2, i % 2
            out = outer(s)
            seconds[i].wait_recv()
            got = qr[i]
            for u, (f, k) in enumerate(RING_PLANES):
                ring[f][plane_at(along_x, out(k)), :] = roll_lanes(got, -8 * u)
            beside, through = (vyq, vxq) if along_x else (vxq, vyq)
            last = len(RING_PLANES)
            side_rows = roll_lanes(got, -8 * last)
            for k in range(3):
                beside[1, 4 + out(k):5 + out(k), :] = side_rows[k:k + 1, :]
            if s == 1:
                through[0, 4:20, :] = roll_lanes(got, -8 * (last + 1))

    for i in range(4, 8):
        sx, sy = SIDES[i]

        @pl.when(has(-sx, -sy))
        def _(i=i, sx=sx, sy=sy):
            ox, oy = outer(up(sx)), outer(up(sy))
            seconds[i].wait_recv()
            for j, (f, a, b) in enumerate(RING_CORNER):
                r = row_of(ox(a), oy(b))
                ring[f][r:r + 1, :] = er[i - 4, j:j + 1, :]
            for k in range(2):
                if sx > 0:
                    vxq[0, 4 + oy(k):5 + oy(k), :] = er[i - 4, 8 + k:9 + k, :]
                if sy > 0:
                    vyq[0, 4 + ox(k):5 + ox(k), :] = er[i - 4, 10 + k:11 + k, :]

    borders(cq, vxq, vyq)
    mirrors(ring, RING_WIDTHS)

    for g in range(4, 69):
        at = slice(g * 8, g * 8 + 8)
        cm[at, :] = cm[at, :] + roll_lanes(jnp.where(lane == TZ - 1, vzq[at, :], 0.0), 1)
        if 7 <= g < 66:
            flow = roll_lanes(jnp.where(lane == TZ - 1, vzm[at, :], 0.0), 1)
            cq[at, :] = cq[at, :] + jnp.where(high_z, 0.0, flow)

    for n in range(STEPS):
        d_main = (cm, d2m, d3m, d4)[n]
        d_ring = (cq, d2q, d3q, None)[n]
        main_span = (range(4, 69), range(7, 66), range(10, 63), [g for g in range(13, 60) if g % 3])[n]
        ring_span = (range(7, 66), range(10, 63), range(13, 60), ())[n]
        for g in main_span:
            at = slice(g * 8, g * 8 + 8)
            here, ghost = pm[n, at, :], pq[n, at, :]

            def stepped(ref, d, here, other):
                sums = (ref[n, g * 8 - WIDE:g * 8 - WIDE + 8, :] + ref[n, g * 8 + WIDE:g * 8 + WIDE + 8, :]) + (
                    ref[n, g * 8 - 1:g * 8 + 7, :] + ref[n, g * 8 + 1:g * 8 + 9, :])
                back = pltpu.roll(jnp.where(lane == TZ - 1, other, here), 1, 1)
                fore = pltpu.roll(jnp.where(lane == 0, other, here), TZ - 1, 1)
                new = d + 0.25 * (sums + (back + fore))
                return new if n == 0 else new + (0.5 * here - ref[n - 1, at, :])

            if n < STEPS - 1:
                pm[n + 1, at, :] = stepped(pm, d_main[at, :], here, ghost)
                if g in ring_span:
                    pq[n + 1, at, :] = stepped(pq, d_ring[at, :], ghost, here)
            else:
                x, half = divmod(g - 13, 3)
                own = slice(x * TY + half * 8, x * TY + half * 8 + 8)
                plast[own, :] = stepped(pm, d4[own, :], here, ghost)
        new = plast[...] if n == STEPS - 1 else jnp.concatenate(
            [pm[n + 1, row_of(x, 0):row_of(x, 0) + TY, :] for x in range(TX)], axis=0)
        both[n * TZ:(n + 1) * TZ, :] = jnp.concatenate(split(new.T), axis=1)

        if n >= 2:
            first = 0 if n == 2 else 3
            for d in range(0, OWN, 2):
                span = slice(d * CAP, (d + 2) * CAP)
                seen = dot_nn(both[first * TZ:(n + 1) * TZ, :], cone[:, span])
                for m in range(first, n + 1):
                    part = seen[(m - first) * TZ:(m - first + 1) * TZ, :]
                    got = jnp.sum(part * zsel[:, span], axis=0, keepdims=True)
                    sb[d, m:m + 1, :] = got[:, :CAP]
                    sb[d + 1, m:m + 1, :] = got[:, CAP:]

    def block_copy(k):
        target = lax.rem(iz + k, OWN)
        return pltpu.make_async_remote_copy(
            src_ref=sb.at[target],
            dst_ref=rb.at[iz],
            send_sem=ass, recv_sem=ars, device_id={"gz": target}, device_id_type=MESH)

    @pl.when(jnp.logical_not(bridge))
    def _():
        pl.semaphore_wait(all_in, 1)

    sends = [block_copy(k) for k in range(1, OWN)]
    for k in (8, 7, 9, 6, 10, 5, 11, 4, 12, 3, 13, 2, 14, 1, 15):
        sends[k - 1].start()
    rb[iz] = sb[iz]

    outs = [pltpu.make_async_copy(plast, fout_h.at[0], osem.at[0])]
    outs[0].start()
    for side, *three in zip(SIDES, *firsts, seconds):
        @pl.when(has(*side))
        def _(three=three):
            for copy in three:
                copy.wait_send()
    for s in (0, 1):
        @pl.when(from_z[1 - s])
        def _(s=s):
            to_z[0][s].wait_send()
            to_z[1][s].wait_send()
    for g in range(13, 64):
        at = slice(g * 8, g * 8 + 8)
        sm[at, :] = (pm[0, at, :] + pm[1, at, :]) + (pm[2, at, :] + pm[3, at, :])
        sq[at, :] = (pq[0, at, :] + pq[1, at, :]) + (pq[2, at, :] + pq[3, at, :])
    for x in range(TX):
        at = slice(x * TY, (x + 1) * TY)
        r = row_of(x, 0)
        own = sm[r:r + TY, :]
        fv[1, at, :] = fv[1, at, :] - 0.5 * (sm[r + WIDE:r + WIDE + TY, :] - own)
        fv[2, at, :] = fv[2, at, :] - 0.5 * (sm[r + 1:r + 1 + TY, :] - own)
        fore = pltpu.roll(jnp.where(lane == 0, sq[r:r + TY, :], own), TZ - 1, 1)
        fv[3, at, :] = fv[3, at, :] - 0.5 * (fore - own)
    outs.append(pltpu.make_async_copy(fv.at[pl.ds(1, 3)], fout_h.at[pl.ds(1, 3)], osem.at[1]))
    outs[1].start()

    hist_load.wait()
    hv[HIST * OWN:, :] = jnp.zeros((STEPS * OWN, CAP), F32)
    bh, bl = split(basis)
    lhs = jnp.concatenate([bh, bl, bh], axis=1)
    for e in range(0, OWN, 2):
        hh, hl = split(jnp.concatenate(
            [hv[pl.ds(e, HIST + STEPS, stride=OWN), :], hv[pl.ds(e + 1, HIST + STEPS, stride=OWN), :]], axis=1))
        part = dot_nn(lhs, jnp.concatenate([hh, hh, hl], axis=0))
        ov[pl.ds(e, NB, stride=OWN), :] = part[:, :CAP] * live[e:e + 1]
        ov[pl.ds(e + 1, NB, stride=OWN), :] = part[:, CAP:] * live[e + 1:e + 2]
    ov_out = pltpu.make_async_copy(ov, cout_h, osem.at[2])
    ov_out.start()

    every = pltpu.make_async_remote_copy(
        src_ref=sb.at[pl.ds(0, OWN - 1)], dst_ref=rb.at[pl.ds(0, OWN - 1)], send_sem=ass, recv_sem=ars,
        device_id={"gz": lax.rem(iz + 1, OWN)}, device_id_type=MESH)
    every.wait_recv()
    for n in range(STEPS):
        for e in range(OWN):
            hb[n * OWN + e:n * OWN + e + 1, :] = rb[e, n:n + 1, :] * live[e:e + 1, :]
    outs.append(pltpu.make_async_copy(hb, heard_h, osem.at[4]))
    outs[-1].start()
    every.wait_send()
    for copy in outs + [bt_out, ov_out]:
        copy.wait()


PARTS = 4
PER = NB // PARTS


def finish(fields_h, part_h, heard_h, bt_h, fout_h, cout_h, fv, ov, hb, bt, sems, fsems):
    pieces = [pl.ds(k * PER * OWN, PER * OWN) for k in range(PARTS)]
    first = [pltpu.make_async_copy(heard_h, hb, sems.at[0]), pltpu.make_async_copy(bt_h, bt, sems.at[1])]
    loads = [pltpu.make_async_copy(part_h.at[r], ov.at[r], sems.at[2 + k]) for k, r in enumerate(pieces)]
    stores = [pltpu.make_async_copy(ov.at[r], cout_h.at[r], sems.at[2 + PARTS + k]) for k, r in enumerate(pieces)]
    gets = [pltpu.make_async_copy(fields_h.at[k], fv.at[k], fsems.at[k]) for k in range(4)]
    puts = [pltpu.make_async_copy(fv.at[k], fout_h.at[k], fsems.at[4 + k]) for k in range(4)]
    for copy in first + loads + gets:
        copy.start()
    for copy in first:
        copy.wait()
    heard = [hb[n * OWN:(n + 1) * OWN, :] for n in range(STEPS)]
    for k in range(PARTS):
        loads[k].wait()
        for j in range(k * PER, (k + 1) * PER):
            at = slice(j * OWN, (j + 1) * OWN)
            term = ov[at, :]
            for n in range(STEPS):
                term = term + bt[n * NB + j:n * NB + j + 1, :] * heard[n]
            ov[at, :] = term
        stores[k].start()
        gets[k].wait()
        puts[k].start()
    for copy in stores + puts:
        copy.wait()


def body(
    fields, tone_freq, mode_freq, mode_amp, mode_map, src_pos, src_id, src_gain, sample_cell, sample_count, history
):
    hbm = pl.BlockSpec(memory_space=pl.ANY)
    made = pl.pallas_call(
        kernel,
        out_shape=(
            jax.ShapeDtypeStruct((4, ROWS, TZ), F32),
            jax.ShapeDtypeStruct((NB * OWN, CAP), F32),
            jax.ShapeDtypeStruct((STEPS * OWN, CAP), F32),
            jax.ShapeDtypeStruct((STEPS * NB, CAP), F32),
        ),
        in_specs=[hbm] * 11,
        out_specs=(hbm,) * 4,
        scratch_shapes=[
            pltpu.VMEM((1, TONES), F32),
            pltpu.VMEM((1, MODES), F32),
            pltpu.VMEM((1, MODES), F32),
            pltpu.VMEM((1, MODES), jnp.int32),
            pltpu.VMEM((3, SRC), jnp.int32),
            pltpu.VMEM((1, SRC), jnp.int32),
            pltpu.VMEM((1, SRC), F32),
            pltpu.VMEM((OWN, CAP), jnp.int32),
            pltpu.VMEM((1, OWN), jnp.int32),
            pltpu.VMEM((4, ROWS, TZ), F32),
            pltpu.VMEM(((HIST + STEPS) * OWN, CAP), F32),
            pltpu.VMEM((STEPS, EXT, TZ), F32),
            pltpu.VMEM((STEPS, EXT, TZ), F32),
            pltpu.VMEM((EXT, TZ), F32),
            pltpu.VMEM((EXT, TZ), F32),
            pltpu.VMEM((EXT, TZ), F32),
            pltpu.VMEM((EXT, TZ), F32),
            pltpu.VMEM((EXT, TZ), F32),
            pltpu.VMEM((EXT, TZ), F32),
            pltpu.VMEM((ROWS, TZ), F32),
            pltpu.VMEM((EXT, TZ), F32),
            pltpu.VMEM((EXT, TZ), F32),
            pltpu.VMEM((2, WIDE, TZ), F32),
            pltpu.VMEM((2, WIDE, TZ), F32),
            pltpu.VMEM((2, WIDE, TZ), F32),
            pltpu.VMEM((2, WIDE, TZ), F32),
            pltpu.VMEM((ROWS, TZ), F32),
            pltpu.VMEM((EXT, TZ), F32),
            pltpu.VMEM((EXT, TZ), F32),
            pltpu.VMEM((8, 2048), F32),
            pltpu.VMEM((8, SRC), F32),
            pltpu.VMEM((1, SRC), F32),
            pltpu.VMEM((1, SRC), F32),
            pltpu.VMEM((2 * STEPS * TZ, ROWS), F32),
            pltpu.VMEM((2 * ROWS, SLOTS), BF),
            pltpu.VMEM((TZ, SLOTS), F32),
            pltpu.VMEM((STEPS * TZ, 2 * ROWS), BF),
            pltpu.VMEM((NB * OWN, CAP), F32),
            pltpu.VMEM((STEPS * NB, CAP), F32),
            pltpu.VMEM((OWN, STEPS, CAP), F32),
            pltpu.VMEM((OWN, STEPS, CAP), F32),
            pltpu.VMEM((STEPS * OWN, CAP), F32),
            pltpu.VMEM((2, 208, TZ), F32),
            pltpu.VMEM((2, 208, TZ), F32),
            pltpu.VMEM((2, 208, TZ), F32),
            pltpu.VMEM((2, 208, TZ), F32),
            pltpu.VMEM((4, 24, TZ), F32),
            pltpu.VMEM((4, 24, TZ), F32),
            pltpu.VMEM((2, 5, GROUP, TZ), F32),
            pltpu.VMEM((2, 5, GROUP, TZ), F32),
            pltpu.VMEM((4, TY, TZ), F32),
            pltpu.VMEM((4, TY, TZ), F32),
            pltpu.VMEM((4, TY, TZ), F32),
            pltpu.VMEM((4, TY, TZ), F32),
            pltpu.VMEM((4, TY, TZ), F32),
            pltpu.VMEM((10, GROUP, TZ), F32),
            pltpu.SemaphoreType.DMA((9,)),
            pltpu.SemaphoreType.DMA((4,)),
            pltpu.SemaphoreType.DMA,
            pltpu.SemaphoreType.DMA((5,)),
            pltpu.SemaphoreType.DMA((2, 8)),
            pltpu.SemaphoreType.DMA((2, 8)),
            pltpu.SemaphoreType.DMA((2, 2)),
            pltpu.SemaphoreType.DMA((2, 2)),
            pltpu.SemaphoreType.DMA((8,)),
            pltpu.SemaphoreType.DMA((8,)),
            pltpu.SemaphoreType.DMA,
            pltpu.SemaphoreType.DMA,
            pltpu.SemaphoreType.REGULAR,
            pltpu.SemaphoreType.REGULAR,
        ],
        compiler_params=pltpu.CompilerParams(
            collective_id=0, has_side_effects=True, vmem_limit_bytes=63 * 1024 * 1024
        ),
    )(
        fields.reshape(4, ROWS, TZ),
        tone_freq.reshape(1, TONES),
        mode_freq.reshape(1, MODES),
        mode_amp.reshape(1, MODES),
        mode_map.reshape(1, MODES),
        src_pos,
        src_id.reshape(1, SRC),
        src_gain.reshape(1, SRC),
        sample_cell.reshape(OWN, CAP),
        sample_count.reshape(1, OWN),
        history.reshape(HIST * OWN, CAP),
    )
    fields_out, coefficients = pl.pallas_call(
        finish,
        out_shape=(
            jax.ShapeDtypeStruct((4, ROWS, TZ), F32),
            jax.ShapeDtypeStruct((NB * OWN, CAP), F32),
        ),
        in_specs=[hbm] * 4,
        out_specs=(hbm,) * 2,
        scratch_shapes=[
            pltpu.VMEM((4, ROWS, TZ), F32),
            pltpu.VMEM((NB * OWN, CAP), F32),
            pltpu.VMEM((STEPS * OWN, CAP), F32),
            pltpu.VMEM((STEPS * NB, CAP), F32),
            pltpu.SemaphoreType.DMA((2 + 2 * PARTS,)),
            pltpu.SemaphoreType.DMA((8,)),
        ],
        compiler_params=pltpu.CompilerParams(vmem_limit_bytes=63 * 1024 * 1024),
    )(*made)
    return fields_out.reshape(fields.shape), coefficients.reshape(NB, 1, 1, 1, OWN, CAP)


def solution(mesh):
    in_specs = (
        P(None, "gx", "gy", "gz"),
        P(),
        P(),
        P(),
        P(),
        P(),
        P(),
        P(),
        P("gx", "gy", "gz", None, None),
        P("gx", "gy", None, "gz"),
        P(None, "gx", "gy", "gz", None, None),
    )
    out_specs = (P(None, "gx", "gy", "gz"), P(None, "gx", "gy", "gz", None, None))
    return jax.shard_map(body, mesh=mesh, in_specs=in_specs, out_specs=out_specs, check_vma=False)
```
